32 devices in a mesh: lat: 8 (over z, core), lon: 4 (over y, x).
Axes of the slice: x: 2, y: 2, z: 4, core: 2. Of those that a mesh axis runs over, the one named last changes fastest.
Arguments:
- fields: bfloat16 [32, 360, 256], P('lat', 'lon'), may hold values from -6 to 6
- w_mix: bfloat16 [256, 1024], replicated, may hold values from -0.375 to 0.375
- filters: bfloat16 [4, 32, 3, 17], P(None, 'lat'), may hold values from -0.5 to 0.5
- reach: int32 [32], P('lat'), may hold values from 1 to 8, as said below
- w_up: bfloat16 [256, 512], replicated, may hold values from -0.375 to 0.375
- w_down: bfloat16 [512, 256], replicated, may hold values from -0.25 to 0.25
- cotangent: bfloat16 [32, 360, 256], P('lat', 'lon'), may hold values from -6 to 6
Outputs:
- result: bfloat16 [32, 360, 256], P('lat', 'lon')
- field_grad: bfloat16 [32, 360, 256], P('lat', 'lon')
The draws below stay inside these ranges and needn't reach their ends.
Inputs may be any that keep to these rules, and one draw needn't show every extreme that they name: reach equals 8 at the two rows at each end of the grid.
All inputs are finite; a program needn't handle non-finite values.
Results may differ from the reference program's by a relative error of at most 0.0061.
Values may be sent and summed in bfloat16 or wider, within the bound.
No kernel may reach another device: no remote copies, remote signals or barrier semaphores. Data moves between devices by JAX's collectives and lax.ppermute only.
A program may use at most 64 MiB of HBM per device.

```python
import jax
import jax.numpy as jnp
from jax import lax

CH = 256
HID = 512
KB = 4
LREACH = 8
NLAT = 32
NLON = 360


def draw_reach(key, part):
    rows_index = jnp.arange(NLAT, dtype=jnp.int32)
    base = jax.random.randint(key, (NLAT,), 1, LREACH + 1, dtype=jnp.int32)
    polar = (rows_index < 2) | (rows_index >= NLAT - 2)
    return jnp.where(polar, LREACH, base).astype(jnp.int32)


def block_levels(own_key, shape, cuts, least, high):
    loudness = 1.0
    for dim, blocks in cuts:
        steps = jax.random.uniform(jax.random.fold_in(jax.random.fold_in(own_key, 6), dim), (blocks,), jnp.float32, least / len(cuts), high / len(cuts))
        loudness = loudness * jnp.repeat(jnp.exp(steps), shape[dim] // blocks).reshape((-1,) + (1,) * (len(shape) - 1 - dim))
    return loudness


def bell_draw(own_key, shape, width, bound, shards=(), held_as=jnp.bfloat16):
    gain = block_levels(own_key, shape, shards, -0.22, 0.18) if shards else 1.0
    entries = jax.random.normal(own_key, shape, jnp.float32) * width * gain
    return jnp.minimum(jnp.maximum(entries, -bound), bound).astype(held_as)


def setup_inputs(seed: int = 0) -> dict:
    seeds = jax.random.split(jax.random.key(seed), 8)
    fields = bell_draw(seeds[0], (NLAT, NLON, CH), 1.0, 6.0, ((0, 8), (1, 4)))
    w_mix = bell_draw(seeds[1], (CH, KB * CH), CH ** -0.5, 0.375)
    filters = bell_draw(seeds[2], (KB, NLAT, 3, 2 * LREACH + 1), 0.1, 0.5, ((1, 8),))
    reach = draw_reach(jax.random.fold_in(seeds[7], 71), 0)
    w_up = bell_draw(seeds[4], (CH, HID), CH ** -0.5, 0.375)
    w_down = bell_draw(seeds[5], (HID, CH), HID ** -0.5, 0.25)
    cotangent = bell_draw(seeds[6], (NLAT, NLON, CH), 1.0, 6.0, ((0, 8), (1, 4)))
    return {"fields": fields, "w_mix": w_mix, "filters": filters, "reach": reach, "w_up": w_up, "w_down": w_down, "cotangent": cotangent}


def gelu_value(pre):
    return 0.5 * pre * (1.0 + jax.scipy.special.erf(pre * 0.7071067811865476))


def gelu_slope(pre):
    return 0.5 * (1.0 + jax.scipy.special.erf(pre * 0.7071067811865476)) + pre * jnp.exp(-0.5 * pre * pre) * 0.3989422804014327


def masked_filters(filters, reach):
    offsets = jnp.arange(2 * LREACH + 1, dtype=jnp.int32) - LREACH
    keep = (jnp.abs(offsets)[None, :] <= reach[:, None]).astype(filters.dtype)
    return filters * keep[None, :, None, :]


def contract_last(left, right):
    return lax.dot_general(left, right, (((1,), (1,)), ((), ())), preferred_element_type=jnp.float32)


def reference(fields, w_mix, filters, reach, w_up, w_down, cotangent):
    span_taps = 2 * LREACH + 1
    masked = masked_filters(filters, reach)
    mixed = jnp.dot(fields.reshape(-1, CH), w_mix, preferred_element_type=jnp.float32).astype(jnp.bfloat16)
    mixed = mixed.reshape(NLAT, NLON, KB, CH)
    padded = jnp.pad(mixed, ((1, 1), (0, 0), (0, 0), (0, 0)))

    def forward_row(index):
        block = lax.dynamic_slice_in_dim(padded, index, 3, 0).astype(jnp.float32)
        weights = lax.dynamic_slice_in_dim(masked, index, 1, 1)[:, 0].astype(jnp.float32)
        total = jnp.zeros((NLON, CH), jnp.float32)
        for tap in range(span_taps):
            moved = jnp.roll(block, LREACH - tap, axis=1)
            total = total + jnp.einsum("ka,ajkc->jc", weights[:, :, tap], moved, precision=lax.Precision.HIGHEST)
        return total

    spatial = lax.map(forward_row, jnp.arange(NLAT, dtype=jnp.int32))
    hidden = (fields.astype(jnp.float32) + spatial).astype(jnp.bfloat16)
    flat_hidden = hidden.reshape(-1, CH)
    pre = jnp.dot(flat_hidden, w_up, preferred_element_type=jnp.float32)
    active = gelu_value(pre).astype(jnp.bfloat16)
    result = (flat_hidden.astype(jnp.float32) + jnp.dot(active, w_down, preferred_element_type=jnp.float32)).astype(jnp.bfloat16)
    upstream = cotangent.reshape(-1, CH)
    grad_active = (contract_last(upstream, w_down) * gelu_slope(pre)).astype(jnp.bfloat16)
    grad_hidden = (upstream.astype(jnp.float32) + contract_last(grad_active, w_up)).astype(jnp.bfloat16)
    grad_pad = jnp.pad(grad_hidden.reshape(NLAT, NLON, CH), ((1, 1), (0, 0), (0, 0)))
    masked_pad = jnp.pad(masked, ((0, 0), (1, 1), (0, 0), (0, 0)))

    def backward_row(index):
        block = lax.dynamic_slice_in_dim(grad_pad, index, 3, 0).astype(jnp.float32)
        near = lax.dynamic_slice_in_dim(masked_pad, index, 3, 1).astype(jnp.float32)
        weights = jnp.stack([near[:, step, 2 - step] for step in range(3)], axis=1)
        total = jnp.zeros((NLON, KB, CH), jnp.float32)
        for tap in range(span_taps):
            moved = jnp.roll(block, tap - LREACH, axis=1)
            total = total + jnp.einsum("kt,tjc->jkc", weights[:, :, tap], moved, precision=lax.Precision.HIGHEST)
        return total.astype(jnp.bfloat16).reshape(NLON, KB * CH)

    grad_mixed = lax.map(backward_row, jnp.arange(NLAT, dtype=jnp.int32))
    field_grad = grad_hidden.astype(jnp.float32) + contract_last(grad_mixed.reshape(-1, KB * CH), w_mix)
    field_grad = field_grad.astype(jnp.bfloat16).reshape(NLAT, NLON, CH)
    return result.reshape(NLAT, NLON, CH), field_grad
```

```python
import jax
import jax.numpy as jnp
from jax import lax
from jax.experimental import pallas as pl
from jax.experimental.pallas import tpu as pltpu
from jax.sharding import PartitionSpec as P

KB = 4
LREACH = 8
TAPS = 2 * LREACH + 1
BLOCK = 64
PITCH = BLOCK + 2 * LREACH
LANES = 256
F32 = jnp.float32
BF16 = jnp.bfloat16
VMEM_BYTES = 48 * 1024 * 1024


def ceil_to(size, unit):
    return -(-size // unit) * unit


def vmem():
    return pl.BlockSpec(memory_space=pltpu.VMEM)


def smem():
    return pl.BlockSpec(memory_space=pltpu.SMEM)


def call(kernel, outs, in_specs, scratch, cost, *args):
    return pl.pallas_call(
        kernel,
        out_shape=outs,
        in_specs=in_specs,
        out_specs=jax.tree.map(lambda _: vmem(), outs),
        scratch_shapes=scratch,
        compiler_params=pltpu.CompilerParams(vmem_limit_bytes=VMEM_BYTES),
        cost_estimate=pl.CostEstimate(flops=cost[0], bytes_accessed=cost[1], transcendentals=0),
    )(*args)


def swap(cells, axis, shift, closed):
    count = lax.axis_size(axis)
    pairs = []
    for first in range(shift, count, 2):
        second = (first + 1) % count
        if second > first or closed:
            pairs += [(first, second), (second, first)]
    return lax.ppermute(cells, axis, pairs)


def pack_lat(parity, fields, cotangent, filters, reach, send_a, send_b, taps, raw):
    rows, width, chans = fields.shape
    step = ceil_to(width, 16)
    odd = parity[0]
    raw[...] = jnp.zeros(raw.shape, F32)
    for r in range(rows):
        for k in range(KB):
            raw[r, 8 * k : 8 * k + 3, 0:TAPS] = filters[k, r].astype(F32)
    offset = jnp.abs(lax.broadcasted_iota(jnp.int32, (8 * KB, 128), 1) - LREACH)
    for r in range(rows):
        kept = jnp.where(offset <= reach[r], raw[r], 0.0)
        raw[r] = kept
        taps[8 * KB * r : 8 * KB * (r + 1), :] = kept.astype(BF16)
    for send, low in ((send_a, 1 - odd), (send_b, odd)):
        send[0:width, :] = fields[low * (rows - 2)]
        send[step : step + width, :] = fields[low * (rows - 2) + 1]
        send[2 * step : 2 * step + width, :] = cotangent[low * (rows - 1)]
        own = raw[low * (rows - 1)].astype(BF16)
        send[3 * step : 3 * step + 16, 0:128] = own[0:16]
        send[3 * step : 3 * step + 16, 128:256] = own[16:32]


def pack_lon(parity, odd_lat, fields, cotangent, got_a, got_b, send_c, send_d):
    rows, width, chans = fields.shape
    step = ceil_to(width, 16)
    odd = parity[0] == 1
    top_is_a = odd_lat[0] == 1

    def lat_rows(first, last, at, keep, top):
        a, b = got_a[at + first : at + last, :], got_b[at + first : at + last, :]
        return jnp.where(top_is_a == top, a, b)

    def edges(first, last, at_top, at_bottom, own):
        parts = [lat_rows(first, last, at, None, True).astype(F32) for at in at_top]
        parts += [own[r, first:last, :].astype(F32) for r in range(rows)]
        parts += [lat_rows(first, last, at, None, False).astype(F32) for at in at_bottom]
        return jnp.concatenate(parts, axis=0).astype(BF16)

    def both(low, high):
        near = edges(0, 2 * LREACH, (0, step), (0, step), fields)
        far = edges(width - 2 * LREACH, width, (0, step), (0, step), fields)
        return near, far

    near, far = both(0, 0)
    near_cot = edges(0, LREACH, (2 * step,), (2 * step,), cotangent)
    far_cot = edges(width - LREACH, width, (2 * step,), (2 * step,), cotangent)
    size = near.shape[0]
    send_c[0:size, :] = jnp.where(odd, near, far)
    send_d[0:size, :] = jnp.where(odd, far, near)
    send_c[size:, :] = jnp.where(odd, near_cot, far_cot)
    send_d[size:, :] = jnp.where(odd, far_cot, near_cot)


def build_bands(odd_lat, taps, got_a, got_b, forward, backward):
    rows = backward.shape[0]
    top_is_a = odd_lat[0] == 1
    at = got_a.shape[0] - 16
    a, b = got_a[at:, :], got_b[at:, :]
    top = jnp.where(top_is_a, a, b)
    bottom = jnp.where(top_is_a, b, a)
    every = jnp.concatenate([top[:, 0:128], top[:, 128:256], taps[...], bottom[:, 0:128], bottom[:, 128:256]], axis=0)
    col = lax.broadcasted_iota(jnp.int32, (128, 2 * LANES), 1)
    tap = lax.broadcasted_iota(jnp.int32, (128, 2 * LANES), 0)
    turned = col >= LANES
    inner = jnp.where(turned, col - LANES, col)
    part = jnp.where(inner >= PITCH, 1, 0) + jnp.where(inner >= 2 * PITCH, 1, 0)
    place = inner - PITCH * part
    wanted = jnp.where(turned, 2 * LREACH - place, place)
    table = jnp.where((tap == wanted) & (tap < TAPS), 1.0, 0.0).astype(BF16)
    spread = jnp.dot(every, table, preferred_element_type=F32)
    groups = (rows + 2) * KB
    lat_tap = lax.broadcasted_iota(jnp.int32, (groups, 8, 2 * LANES), 1)
    col = lax.broadcasted_iota(jnp.int32, (groups, 8, 2 * LANES), 2)
    turned = col >= LANES
    inner = jnp.where(turned, col - LANES, col)
    part = jnp.where(inner >= PITCH, 1, 0) + jnp.where(inner >= 2 * PITCH, 1, 0)
    chosen = jnp.where(turned, 2 - part, part) == lat_tap
    lines = jnp.sum(jnp.where(chosen, spread.reshape(groups, 8, 2 * LANES), 0.0), axis=1)

    def slant(line):
        wide = jnp.broadcast_to(line, (BLOCK, LANES))
        return pltpu.roll(wide, 0, 1, stride=1, stride_axis=0).astype(BF16)

    for i in range(rows + 2):
        for k in range(KB):
            forward[i, BLOCK * k : BLOCK * (k + 1), :] = slant(lines[KB * i + k : KB * i + k + 1, 0:LANES])
    lane = lax.broadcasted_iota(jnp.int32, (1, LANES), 1)
    for i in range(rows):
        for k in range(KB):
            near = [lines[KB * (i + t) + k : KB * (i + t) + k + 1, LANES:] for t in range(3)]
            line = jnp.where(lane < PITCH, near[0], jnp.where(lane < 2 * PITCH, near[1], near[2]))
            backward[i, BLOCK * k : BLOCK * (k + 1), :] = slant(line)


def gelu_parts(pre):
    size = jnp.abs(pre)
    bell = jnp.exp(-0.5 * pre * pre)
    t = 1.0 / (1.0 + 0.23164188836 * size)
    poly = t * (0.127414796 + t * (-0.142248368 + t * (0.7107068705 + t * (-0.7265760135 + t * 0.5307027145))))
    tail = poly * bell
    cdf = jnp.where(pre >= 0.0, 1.0 - tail, tail)
    return pre * cdf, cdf + pre * bell * 0.3989422804014327


def contract_last(left, right):
    return lax.dot_general(left, right, (((1,), (1,)), ((), ())), preferred_element_type=F32)


def block_kernel(
    odd_lat, odd_lon, fields, cotangent, got_a, got_b, got_c, got_d, forward, backward, w_mix, w_up, w_down,
    result, field_grad, source, basis, hidden, upstream, grads, grad_mixed,
):
    rows, width, chans = fields.shape
    step = ceil_to(width, 16)
    top_is_a = odd_lat[0] == 1
    left_is_c = odd_lon[0] == 1
    ext = rows + 2
    rest = ceil_to(width + 2 * LREACH - BLOCK, 16)
    span = BLOCK + rest
    split = BLOCK - LREACH

    def lat_rows(at, top):
        return jnp.where(top_is_a == top, got_a[at : at + width, :], got_b[at : at + width, :])

    def side(first, size, left):
        return jnp.where(left_is_c == left, got_c[first : first + size, :], got_d[first : first + size, :])

    def zeros(size):
        return jnp.zeros((size, chans), F32)

    for i in range(rows + 4):
        if i < 2:
            line = lat_rows(step * i, True)
        elif i < rows + 2:
            line = fields[i - 2]
        else:
            line = lat_rows(step * (i - rows - 2), False)
        left = side(2 * LREACH * i, 2 * LREACH, True)
        right = side(2 * LREACH * i, 2 * LREACH, False)
        at = PITCH * i
        source[0, at : at + 2 * LREACH, :] = left
        source[0, at + 2 * LREACH : at + PITCH, :] = line[0:BLOCK]
        tail = line[BLOCK - 2 * LREACH :].astype(F32)
        fill = PITCH - tail.shape[0] - 2 * LREACH
        source[1, at : at + PITCH, :] = jnp.concatenate([tail, right.astype(F32), zeros(fill)], axis=0).astype(BF16)
    source[:, PITCH * (rows + 4) :, :] = jnp.zeros((2, LANES - 3 * PITCH, chans), BF16)

    edge = 2 * LREACH * (rows + 4)
    for i in range(ext):
        if i == 0:
            line = lat_rows(2 * step, True)
        elif i < ext - 1:
            line = cotangent[i - 1]
        else:
            line = lat_rows(2 * step, False)
        line = line.astype(F32)
        pair = edge + 2 * LREACH * (i // 2)
        inside = LREACH * (i % 2)
        left = side(pair, 2 * LREACH, True).astype(F32)[inside : inside + LREACH]
        right = side(pair, 2 * LREACH, False).astype(F32)[inside : inside + LREACH]
        fill = span - width - 2 * LREACH
        whole = jnp.concatenate([left, line, right, zeros(fill)], axis=0)
        upstream[span * i : span * (i + 1), :] = whole.astype(BF16)

    for i in range(ext):
        for part, size in ((0, BLOCK), (1, rest)):
            band = forward[i]
            if size < BLOCK:
                band = jnp.concatenate([band[BLOCK * k : BLOCK * k + size] for k in range(KB)], axis=0)
            moved = jnp.dot(band, source[part, PITCH * i : PITCH * i + LANES, :], preferred_element_type=F32).astype(BF16)
            at = span * i + BLOCK * part
            for k in range(KB):
                basis[at : at + size, chans * k : chans * (k + 1)] = moved[size * k : size * (k + 1)]
    stacked = jnp.concatenate([w_mix[:, chans * k : chans * (k + 1)] for k in range(KB)], axis=0)
    spatial = jnp.dot(basis[...], stacked, preferred_element_type=F32)
    for i in range(ext):
        at = PITCH * (i + 1)
        first = source[0, at : at + PITCH, :].astype(F32)[LREACH : LREACH + BLOCK]
        second = source[1, at : at + PITCH, :].astype(F32)[LREACH : LREACH + rest]
        here = span * i
        hidden[here : here + BLOCK, :] = (first + spatial[here : here + BLOCK]).astype(BF16)
        hidden[here + BLOCK : here + span, :] = (second + spatial[here + BLOCK : here + span]).astype(BF16)

    for i in range(ext):
        here = span * i
        mine = hidden[here : here + span, :]
        up = upstream[here : here + span, :]
        pre = jnp.dot(mine, w_up[...], preferred_element_type=F32)
        active, slope = gelu_parts(pre)
        if 0 < i < ext - 1:
            out = mine.astype(F32) + jnp.dot(active.astype(BF16), w_down[...], preferred_element_type=F32)
            result[i - 1] = out[LREACH : LREACH + width].astype(BF16)
        grad_active = (contract_last(up, w_down[...]) * slope).astype(BF16)
        grad = (up.astype(F32) + contract_last(grad_active, w_up[...])).astype(BF16)
        at = PITCH * i
        grads[0, at : at + PITCH, :] = grad[0:PITCH]
        grads[1, at : at + rest, :] = grad[BLOCK:span]
        grads[1, at + rest : at + PITCH, :] = jnp.zeros((PITCH - rest, chans), BF16)
    grads[:, PITCH * ext :, :] = jnp.zeros((2, LANES - 3 * PITCH, chans), BF16)

    last = ceil_to(width - BLOCK, 16)
    out_span = BLOCK + last
    for i in range(rows):
        for part, size in ((0, BLOCK), (1, last)):
            band = backward[i]
            if size < BLOCK:
                band = jnp.concatenate([band[BLOCK * k : BLOCK * k + size] for k in range(KB)], axis=0)
            moved = jnp.dot(band, grads[part, PITCH * i : PITCH * i + LANES, :], preferred_element_type=F32).astype(BF16)
            at = out_span * i + BLOCK * part
            for k in range(KB):
                grad_mixed[at : at + size, chans * k : chans * (k + 1)] = moved[size * k : size * (k + 1)]
    back = contract_last(grad_mixed[...], w_mix[...])
    for i in range(rows):
        at = PITCH * (i + 1)
        first = grads[0, at : at + PITCH, :].astype(F32)[LREACH : LREACH + BLOCK]
        second = grads[1, at : at + PITCH, :].astype(F32)[LREACH : LREACH + last]
        whole = jnp.concatenate([first, second], axis=0) + back[out_span * i : out_span * (i + 1)]
        field_grad[i] = whole[0:width].astype(BF16)


def on_device(fields, w_mix, filters, reach, w_up, w_down, cotangent):
    rows, width, chans = fields.shape
    step = ceil_to(width, 16)
    odd_lat = (lax.axis_index("lat") % 2).astype(jnp.int32).reshape(1)
    odd_lon = (lax.axis_index("lon") % 2).astype(jnp.int32).reshape(1)
    lat_size = 3 * step + 16
    lon_size = 2 * LREACH * (rows + 4) + LREACH * (rows + 2)
    sent = jax.ShapeDtypeStruct((lat_size, chans), BF16)
    send_a, send_b, taps = call(
        pack_lat,
        (sent, sent, jax.ShapeDtypeStruct((8 * KB * rows, 128), BF16)),
        [smem(), vmem(), vmem(), vmem(), smem()],
        [pltpu.VMEM((rows, 8 * KB, 128), F32)],
        (1000, 1000000),
        odd_lat, fields, cotangent, filters, reach,
    )
    got_a = swap(send_a, "lat", 0, False)
    got_b = swap(send_b, "lat", 1, False)
    sent = jax.ShapeDtypeStruct((lon_size, chans), BF16)
    send_c, send_d = call(
        pack_lon,
        (sent, sent),
        [smem(), smem()] + [vmem()] * 4,
        [],
        (1000, 1000000),
        odd_lon, odd_lat, fields, cotangent, got_a, got_b,
    )
    got_c = swap(send_c, "lon", 0, True)
    got_d = swap(send_d, "lon", 1, True)
    forward, backward = call(
        build_bands,
        (
            jax.ShapeDtypeStruct((rows + 2, KB * BLOCK, LANES), BF16),
            jax.ShapeDtypeStruct((rows, KB * BLOCK, LANES), BF16),
        ),
        [smem()] + [vmem()] * 3,
        [],
        (1000000, 3000000),
        odd_lat, taps, got_a, got_b,
    )
    ext = rows + 2
    span = BLOCK + ceil_to(width + 2 * LREACH - BLOCK, 16)
    out_span = BLOCK + ceil_to(width - BLOCK, 16)
    pad = LANES - 3 * PITCH
    out = jax.ShapeDtypeStruct(fields.shape, BF16)
    return call(
        block_kernel,
        (out, out),
        [smem(), smem()] + [vmem()] * 11,
        [
            pltpu.VMEM((2, PITCH * (rows + 4) + pad, chans), BF16),
            pltpu.VMEM((span * ext, KB * chans), BF16),
            pltpu.VMEM((span * ext, chans), BF16),
            pltpu.VMEM((span * ext, chans), BF16),
            pltpu.VMEM((2, PITCH * ext + pad, chans), BF16),
            pltpu.VMEM((out_span * rows, KB * chans), BF16),
        ],
        (2000000000, 5000000),
        odd_lat, odd_lon, fields, cotangent, got_a, got_b, got_c, got_d, forward, backward, w_mix, w_up, w_down,
    )


def solution(mesh):
    return jax.shard_map(
        on_device,
        mesh=mesh,
        in_specs=(
            P("lat", "lon", None),
            P(),
            P(None, "lat", None, None),
            P("lat"),
            P(),
            P(),
            P("lat", "lon", None),
        ),
        out_specs=(P("lat", "lon", None), P("lat", "lon", None)),
        check_vma=False,
    )
```

```python
import jax
import jax.numpy as jnp
from jax import lax
from jax.experimental import pallas as pl
from jax.experimental.pallas import tpu as pltpu
from jax.sharding import PartitionSpec as P

KB = 4
LREACH = 8
TAPS = 2 * LREACH + 1
BLOCK = 64
PITCH = BLOCK + 2 * LREACH
EDGE = 2 * LREACH
EDGE_PITCH = 2 * EDGE
LANES = 256
EDGE_LANES = 128
F32 = jnp.float32
BF16 = jnp.bfloat16
VMEM_BYTES = 48 * 1024 * 1024


def ceil_to(size, unit):
    return -(-size // unit) * unit


def vmem():
    return pl.BlockSpec(memory_space=pltpu.VMEM)


def hbm():
    return pl.BlockSpec(memory_space=pltpu.HBM)


def is_odd(axis):
    return lax.rem(lax.axis_index(axis), 2)


def call(kernel, outs, in_specs, scratch, cost, *args, out_specs=None):
    return pl.pallas_call(
        kernel,
        out_shape=outs,
        in_specs=in_specs,
        out_specs=out_specs or jax.tree.map(lambda _: vmem(), outs),
        scratch_shapes=scratch,
        compiler_params=pltpu.CompilerParams(vmem_limit_bytes=VMEM_BYTES),
        cost_estimate=pl.CostEstimate(flops=cost[0], bytes_accessed=cost[1], transcendentals=0),
    )(*args)


def swap(cells, axis, shift, closed):
    count = lax.axis_size(axis)
    pairs = []
    for first in range(shift, count, 2):
        second = (first + 1) % count
        if second > first or closed:
            pairs += [(first, second), (second, first)]
    return lax.ppermute(cells, axis, pairs)


def fetch(fields, cotangent, filters, reach, fields_here, cotangent_here, taps, filters_here, reach_here, raw, sems):
    copies = [
        pltpu.make_async_copy(src, dst, sems.at[n])
        for n, (src, dst) in enumerate(
            ((filters, filters_here), (reach, reach_here), (fields, fields_here), (cotangent, cotangent_here))
        )
    ]
    for copy in copies:
        copy.start()
    rows = taps.shape[0]
    raw[...] = jnp.zeros(raw.shape, F32)
    offset = jnp.abs(lax.broadcasted_iota(jnp.int32, (8 * KB, 128), 1) - LREACH)
    copies[0].wait()
    copies[1].wait()
    for k in range(KB):
        for a in range(3):
            line = filters_here[k, a].astype(F32)
            for r in range(rows):
                raw[r, 8 * k + a : 8 * k + a + 1, 0:TAPS] = line[r : r + 1]
    for r in range(rows):
        taps[r] = jnp.where(offset <= reach_here[r], raw[r], 0.0).astype(BF16)
    copies[2].wait()
    copies[3].wait()


def pack_lat(fields, cotangent, taps, send_a, send_b):
    rows, width, chans = fields.shape
    step = ceil_to(width, 16)
    odd = is_odd("lat")
    for send, low in ((send_a, 1 - odd), (send_b, odd)):
        send[0:width, :] = fields[low * (rows - 2)]
        send[step : step + width, :] = fields[low * (rows - 2) + 1]
        send[2 * step : 2 * step + width, :] = cotangent[low * (rows - 1)]
        own = taps[low * (rows - 1)]
        send[3 * step : 3 * step + 16, 0:128] = own[0:16]
        send[3 * step : 3 * step + 16, 128:256] = own[16:32]


def pack_lon(fields, cotangent, got_a, got_b, send_c, send_d):
    rows, width, chans = fields.shape
    step = ceil_to(width, 16)
    odd = is_odd("lon") == 1
    top_is_a = is_odd("lat") == 1

    def lat_rows(at, first, last, top):
        return jnp.where(top_is_a == top, got_a[at + first : at + last, :], got_b[at + first : at + last, :])

    def edges(first, last, starts, own):
        parts = [lat_rows(at, first, last, True).astype(F32) for at in starts]
        parts += [own[r, first:last, :].astype(F32) for r in range(rows)]
        parts += [lat_rows(at, first, last, False).astype(F32) for at in starts]
        return jnp.concatenate(parts, axis=0).astype(BF16)

    near = edges(0, EDGE, (0, step), fields)
    far = edges(width - EDGE, width, (0, step), fields)
    near_cot = edges(0, LREACH, (2 * step,), cotangent)
    far_cot = edges(width - LREACH, width, (2 * step,), cotangent)
    size = near.shape[0]
    send_c[0:size, :] = jnp.where(odd, near, far)
    send_d[0:size, :] = jnp.where(odd, far, near)
    send_c[size:, :] = jnp.where(odd, near_cot, far_cot)
    send_d[size:, :] = jnp.where(odd, far_cot, near_cot)


def lay_taps(every, pitch, lanes):
    groups = every.shape[0] // 8

    def places(shape, dim):
        col = lax.broadcasted_iota(jnp.int32, shape, dim)
        turned = col >= lanes
        inner = jnp.where(turned, col - lanes, col)
        part = jnp.where(inner >= pitch, 1, 0) + jnp.where(inner >= 2 * pitch, 1, 0)
        return turned, inner - pitch * part, part

    turned, place, _ = places((128, 2 * lanes), 1)
    tap = lax.broadcasted_iota(jnp.int32, (128, 2 * lanes), 0)
    wanted = jnp.where(turned, 2 * LREACH - place, place)
    table = jnp.where((tap == wanted) & (tap < TAPS), 1.0, 0.0).astype(BF16)
    spread = jnp.dot(every, table, preferred_element_type=F32).reshape(groups, 8, 2 * lanes)
    turned, _, part = places((groups, 8, 2 * lanes), 2)
    lat_tap = lax.broadcasted_iota(jnp.int32, (groups, 8, 2 * lanes), 1)
    chosen = jnp.where(turned, 2 - part, part) == lat_tap
    return jnp.sum(jnp.where(chosen, spread, 0.0), axis=1)


def build_bands(every, forward, backward, size, pitch, lanes):
    lines = lay_taps(every, pitch, lanes)
    rows = every.shape[0] // (8 * KB) - 2
    lane = lax.broadcasted_iota(jnp.int32, (1, lanes), 1)

    def slant(line):
        return pltpu.roll(jnp.broadcast_to(line, (size, lanes)), 0, 1, stride=1, stride_axis=0).astype(BF16)

    for i in range(rows + 2):
        for k in range(KB):
            at = KB * i + k
            forward[i, size * k : size * (k + 1), :] = slant(lines[at : at + 1, 0:lanes])
    for i in range(rows):
        for k in range(KB):
            near = [lines[KB * (i + t) + k : KB * (i + t) + k + 1, lanes:] for t in range(3)]
            line = jnp.where(lane < pitch, near[0], jnp.where(lane < 2 * pitch, near[1], near[2]))
            backward[i, size * k : size * (k + 1), :] = slant(line)


def gelu_parts(pre):
    size = jnp.abs(pre)
    bell = jnp.exp(-0.5 * pre * pre)
    t = 1.0 / (1.0 + 0.23164188836 * size)
    poly = t * (0.127414796 + t * (-0.142248368 + t * (0.7107068705 + t * (-0.7265760135 + t * 0.5307027145))))
    tail = poly * bell
    cdf = jnp.where(pre >= 0.0, 1.0 - tail, tail)
    return pre * cdf, cdf + pre * bell * 0.3989422804014327


def contract_last(left, right):
    return lax.dot_general(left, right, (((1,), (1,)), ((), ())), preferred_element_type=F32)


def mlp(mine, up, w_up, w_down, wants_result):
    pre = jnp.dot(mine, w_up[...], preferred_element_type=F32)
    active, slope = gelu_parts(pre)
    out = None
    if wants_result:
        out = mine.astype(F32) + jnp.dot(active.astype(BF16), w_down[...], preferred_element_type=F32)
    grad_active = (contract_last(up.astype(BF16), w_down[...]) * slope).astype(BF16)
    return out, (up + contract_last(grad_active, w_up[...])).astype(BF16)


def middle_kernel(
    fields, cotangent, taps, got_a, got_b, w_mix, w_up, w_down,
    result, field_grad, grads, edge_forward, edge_backward, forward, backward, wide, narrow, basis, grad_mixed,
):
    rows, width, chans = fields.shape
    step = ceil_to(width, 16)
    top_is_a = is_odd("lat") == 1
    ext = rows + 2
    rest = EDGE
    span = BLOCK + rest

    def lat_rows(at, size, top):
        return jnp.where(top_is_a == top, got_a[at : at + size, :], got_b[at : at + size, :])

    def taps_of(top):
        both = lat_rows(3 * step, 16, top)
        return [both[:, 0:128], both[:, 128:256]]

    every = jnp.concatenate(taps_of(True) + [taps[r] for r in range(rows)] + taps_of(False), axis=0)
    build_bands(every, forward, backward, BLOCK, PITCH, LANES)
    build_bands(every, edge_forward, edge_backward, EDGE, EDGE_PITCH, EDGE_LANES)

    fill = PITCH + EDGE - width
    for i in range(rows + 4):
        if i < 2:
            line = lat_rows(step * i, width, True)
        elif i < rows + 2:
            line = fields[i - 2]
        else:
            line = lat_rows(step * (i - rows - 2), width, False)
        wide[PITCH * i : PITCH * (i + 1), :] = line[0:PITCH]
        tail = jnp.concatenate([line[BLOCK:].astype(F32), jnp.zeros((fill, chans), F32)], axis=0)
        narrow[EDGE_PITCH * i : EDGE_PITCH * (i + 1), :] = tail.astype(BF16)
    wide[PITCH * (rows + 4) :, :] = jnp.zeros((LANES - 3 * PITCH, chans), BF16)
    narrow[EDGE_PITCH * (rows + 4) :, :] = jnp.zeros((EDGE_LANES - 3 * EDGE_PITCH, chans), BF16)

    for i in range(ext):
        at = span * i
        moved = jnp.dot(forward[i], wide[PITCH * i : PITCH * i + LANES, :], preferred_element_type=F32).astype(BF16)
        other = jnp.dot(
            edge_forward[i], narrow[EDGE_PITCH * i : EDGE_PITCH * i + EDGE_LANES, :], preferred_element_type=F32
        ).astype(BF16)
        for k in range(KB):
            basis[at : at + BLOCK, chans * k : chans * (k + 1)] = moved[BLOCK * k : BLOCK * (k + 1)]
            basis[at + BLOCK : at + span, chans * k : chans * (k + 1)] = other[rest * k : rest * (k + 1)]
    stacked = jnp.concatenate([w_mix[:, chans * k : chans * (k + 1)] for k in range(KB)], axis=0)
    for i in range(ext):
        at = PITCH * (i + 1)
        first = wide[at : at + PITCH, :].astype(F32)[LREACH : LREACH + BLOCK]
        at = EDGE_PITCH * (i + 1)
        second = narrow[at : at + EDGE_PITCH, :].astype(F32)[LREACH : LREACH + rest]
        spatial = jnp.dot(basis[span * i : span * (i + 1), :], stacked, preferred_element_type=F32)
        mine = (jnp.concatenate([first, second], axis=0) + spatial).astype(BF16)
        if i == 0:
            up = lat_rows(2 * step, width, True)
        elif i < ext - 1:
            up = cotangent[i - 1]
        else:
            up = lat_rows(2 * step, width, False)
        up = up.astype(F32)[LREACH : LREACH + span]
        out, grad = mlp(mine, up, w_up, w_down, 0 < i < ext - 1)
        if out is not None:
            result[i - 1] = out.astype(BF16)
        grads[span * i : span * (i + 1), :] = grad
    grads[span * ext :, :] = jnp.zeros((LANES - 3 * PITCH, chans), BF16)

    for i in range(rows):
        moved = jnp.dot(backward[i], grads[PITCH * i : PITCH * i + LANES, :], preferred_element_type=F32).astype(BF16)
        for k in range(KB):
            grad_mixed[BLOCK * i : BLOCK * (i + 1), chans * k : chans * (k + 1)] = moved[BLOCK * k : BLOCK * (k + 1)]
    back = contract_last(grad_mixed[...], w_mix[...])
    for i in range(rows):
        at = PITCH * (i + 1)
        own = grads[at : at + PITCH, :].astype(F32)[LREACH : LREACH + BLOCK]
        field_grad[i] = (own + back[BLOCK * i : BLOCK * (i + 1)]).astype(BF16)


def edge_kernel(
    middle_result, middle_grad, middle_grads, edge_forward, edge_backward, send_c, send_d, got_c, got_d, w_mix, w_up, w_down,
    result, field_grad, source, basis, hidden, upstream, grads, grad_mixed,
):
    rows, width, chans = result.shape
    ext = rows + 2
    span = BLOCK + EDGE
    left_is_c = is_odd("lon") == 1
    cot_at = EDGE * (rows + 4)

    def pick(at, size, of_c, of_d, left):
        return jnp.where(left_is_c == left, of_c[at : at + size, :], of_d[at : at + size, :])

    for i in range(rows + 4):
        at = EDGE_PITCH * i
        source[at : at + EDGE, 0:chans] = pick(EDGE * i, EDGE, got_c, got_d, True)
        source[at + EDGE : at + 2 * EDGE, 0:chans] = pick(EDGE * i, EDGE, send_c, send_d, True)
        source[at : at + EDGE, chans:] = pick(EDGE * i, EDGE, send_c, send_d, False)
        source[at + EDGE : at + 2 * EDGE, chans:] = pick(EDGE * i, EDGE, got_c, got_d, False)
    source[EDGE_PITCH * (rows + 4) :, :] = jnp.zeros((EDGE_LANES - 3 * EDGE_PITCH, 2 * chans), BF16)

    for i in range(ext):
        at = cot_at + EDGE * (i // 2)
        inside = LREACH * (i % 2)
        for left in (True, False):
            got = pick(at, EDGE, got_c, got_d, left).astype(F32)[inside : inside + LREACH]
            sent = pick(at, EDGE, send_c, send_d, left).astype(F32)[inside : inside + LREACH]
            here = EDGE * (2 * i + (0 if left else 1))
            whole = jnp.concatenate([got, sent] if left else [sent, got], axis=0)
            upstream[here : here + EDGE, :] = whole.astype(BF16)

    def spread(band, cells, at, out):
        moved = jnp.dot(band, cells, preferred_element_type=F32).astype(BF16)
        for part in range(2):
            for k in range(KB):
                out[at + EDGE * part : at + EDGE * (part + 1), chans * k : chans * (k + 1)] = moved[
                    EDGE * k : EDGE * (k + 1), chans * part : chans * (part + 1)
                ]

    for i in range(ext):
        spread(edge_forward[i], source[EDGE_PITCH * i : EDGE_PITCH * i + EDGE_LANES, :], 2 * EDGE * i, basis)
    stacked = jnp.concatenate([w_mix[:, chans * k : chans * (k + 1)] for k in range(KB)], axis=0)
    spatial = jnp.dot(basis[...], stacked, preferred_element_type=F32)
    for i in range(ext):
        at = EDGE_PITCH * (i + 1)
        cells = source[at : at + EDGE_PITCH, :].astype(F32)[LREACH : LREACH + EDGE]
        for part in range(2):
            here = EDGE * (2 * i + part)
            hidden[here : here + EDGE, :] = (
                cells[:, chans * part : chans * (part + 1)] + spatial[here : here + EDGE]
            ).astype(BF16)
    out, grad = mlp(hidden[...], upstream[...].astype(F32), w_up, w_down, True)
    for i in range(rows):
        here = 2 * EDGE * (i + 1)
        left = out[here + LREACH : here + EDGE]
        right = out[here + EDGE : here + EDGE + LREACH]
        middle = middle_result[i].astype(F32)[0 : width - 2 * LREACH]
        result[i] = jnp.concatenate([left, middle, right], axis=0).astype(BF16)

    first = width - EDGE - 2 * LREACH
    for i in range(ext):
        at = EDGE_PITCH * i
        here = 2 * EDGE * i
        middle = middle_grads[span * i : span * (i + 1), :]
        grads[at : at + EDGE, 0:chans] = grad[here : here + EDGE]
        grads[at + EDGE : at + 2 * EDGE, 0:chans] = middle[0:EDGE]
        grads[at : at + EDGE, chans:] = middle.astype(F32)[first : first + EDGE].astype(BF16)
        grads[at + EDGE : at + 2 * EDGE, chans:] = grad[here + EDGE : here + 2 * EDGE]
    grads[EDGE_PITCH * ext :, :] = jnp.zeros((EDGE_LANES - 3 * EDGE_PITCH, 2 * chans), BF16)
    for i in range(rows):
        spread(edge_backward[i], grads[EDGE_PITCH * i : EDGE_PITCH * i + EDGE_LANES, :], 2 * EDGE * i, grad_mixed)
    back = contract_last(grad_mixed[...], w_mix[...])
    for i in range(rows):
        at = EDGE_PITCH * (i + 1)
        own = grads[at : at + EDGE_PITCH, :].astype(F32)[LREACH : LREACH + EDGE]
        here = 2 * EDGE * i
        left = own[:, 0:chans] + back[here : here + EDGE]
        right = own[:, chans:] + back[here + EDGE : here + 2 * EDGE]
        middle = middle_grad[i].astype(F32)[0 : width - 2 * EDGE]
        field_grad[i] = jnp.concatenate([left, middle, right], axis=0).astype(BF16)


def store(result, field_grad, result_out, field_grad_out, sems):
    copies = [
        pltpu.make_async_copy(result, result_out, sems.at[0]),
        pltpu.make_async_copy(field_grad, field_grad_out, sems.at[1]),
    ]
    for copy in copies:
        copy.start()
    for copy in copies:
        copy.wait()


def on_device(fields, w_mix, filters, reach, w_up, w_down, cotangent):
    rows, width, chans = fields.shape
    step = ceil_to(width, 16)
    ext = rows + 2
    span = BLOCK + EDGE
    pad = LANES - 3 * PITCH
    edge_pad = EDGE_LANES - 3 * EDGE_PITCH

    def shaped(*shape):
        return jax.ShapeDtypeStruct(shape, BF16)

    turned = shaped(width, rows, chans)
    fields_here, cotangent_here, taps = call(
        fetch,
        (turned, turned, shaped(rows, 8 * KB, 128)),
        [hbm()] * 4,
        [
            pltpu.VMEM((KB, 3, rows, TAPS), BF16),
            pltpu.SMEM((rows,), jnp.int32),
            pltpu.VMEM((rows, 8 * KB, 128), F32),
            pltpu.SemaphoreType.DMA((4,)),
        ],
        (1000, 1000000),
        *(
            pltpu.with_memory_space_constraint(x, pltpu.HBM)
            for x in (fields.transpose(1, 0, 2), cotangent.transpose(1, 0, 2), filters.transpose(0, 2, 1, 3), reach)
        ),
    )
    fields = fields_here.transpose(1, 0, 2)
    cotangent = cotangent_here.transpose(1, 0, 2)
    sent = shaped(3 * step + 16, chans)
    send_a, send_b = call(pack_lat, (sent, sent), [vmem()] * 3, [], (1000, 1000000), fields, cotangent, taps)
    got_b = swap(send_b, "lat", 1, False)
    got_a = swap(send_a, "lat", 0, False)
    sent = shaped(EDGE * (rows + 4) + LREACH * ext, chans)
    send_c, send_d = call(
        pack_lon, (sent, sent), [vmem()] * 4, [], (1000, 1000000), fields, cotangent, got_a, got_b
    )
    got_d = swap(send_d, "lon", 1, True)
    got_c = swap(send_c, "lon", 0, True)
    middle_result, middle_grad, middle_grads, edge_forward, edge_backward = call(
        middle_kernel,
        (
            shaped(rows, span, chans),
            shaped(rows, BLOCK, chans),
            shaped(span * ext + pad, chans),
            shaped(ext, KB * EDGE, EDGE_LANES),
            shaped(rows, KB * EDGE, EDGE_LANES),
        ),
        [vmem()] * 8,
        [
            pltpu.VMEM((ext, KB * BLOCK, LANES), BF16),
            pltpu.VMEM((rows, KB * BLOCK, LANES), BF16),
            pltpu.VMEM((PITCH * (rows + 4) + pad, chans), BF16),
            pltpu.VMEM((EDGE_PITCH * (rows + 4) + edge_pad, chans), BF16),
            pltpu.VMEM((span * ext, KB * chans), BF16),
            pltpu.VMEM((BLOCK * rows, KB * chans), BF16),
        ],
        (2000000000, 5000000),
        fields, cotangent, taps, got_a, got_b, w_mix, w_up, w_down,
    )
    out = shaped(rows, width, chans)
    result, field_grad = call(
        edge_kernel,
        (out, out),
        [vmem()] * 12,
        [
            pltpu.VMEM((EDGE_PITCH * (rows + 4) + edge_pad, 2 * chans), BF16),
            pltpu.VMEM((2 * EDGE * ext, KB * chans), BF16),
            pltpu.VMEM((2 * EDGE * ext, chans), BF16),
            pltpu.VMEM((2 * EDGE * ext, chans), BF16),
            pltpu.VMEM((EDGE_PITCH * ext + edge_pad, 2 * chans), BF16),
            pltpu.VMEM((2 * EDGE * rows, KB * chans), BF16),
        ],
        (500000000, 3000000),
        middle_result, middle_grad, middle_grads, edge_forward, edge_backward, send_c, send_d, got_c, got_d, w_mix, w_up, w_down,
    )
    result, field_grad = call(
        store,
        (turned, turned),
        [vmem()] * 2,
        [pltpu.SemaphoreType.DMA((2,))],
        (1000, 700000),
        result.transpose(1, 0, 2), field_grad.transpose(1, 0, 2),
        out_specs=(hbm(), hbm()),
    )
    return result.transpose(1, 0, 2), field_grad.transpose(1, 0, 2)


def solution(mesh):
    return jax.shard_map(
        on_device,
        mesh=mesh,
        in_specs=(
            P("lat", "lon", None),
            P(),
            P(None, "lat", None, None),
            P("lat"),
            P(),
            P(),
            P("lat", "lon", None),
        ),
        out_specs=(P("lat", "lon", None), P("lat", "lon", None)),
        check_vma=False,
    )
```

```python
import functools

import jax
import jax.numpy as jnp
from jax import lax
from jax.experimental import pallas as pl
from jax.experimental.pallas import tpu as pltpu
from jax.sharding import PartitionSpec as P

KB = 4
LREACH = 8
TAPS = 2 * LREACH + 1
BLOCK = 64
PITCH = BLOCK + 2 * LREACH
EDGE = 2 * LREACH
EDGE_PITCH = 2 * EDGE
LANES = 256
EDGE_LANES = 128
F32 = jnp.float32
BF16 = jnp.bfloat16
VMEM_BYTES = 48 * 1024 * 1024


def ceil_to(size, unit):
    return -(-size // unit) * unit


def vmem():
    return pl.BlockSpec(memory_space=pltpu.VMEM)


def hbm():
    return pl.BlockSpec(memory_space=pltpu.HBM)


def is_odd(axis):
    return lax.rem(lax.axis_index(axis), 2)


def call(kernel, outs, in_specs, scratch, cost, *args, out_specs=None):
    return pl.pallas_call(
        kernel,
        out_shape=outs,
        in_specs=in_specs,
        out_specs=out_specs or jax.tree.map(lambda _: vmem(), outs),
        scratch_shapes=scratch,
        compiler_params=pltpu.CompilerParams(vmem_limit_bytes=VMEM_BYTES),
        cost_estimate=pl.CostEstimate(flops=cost[0], bytes_accessed=cost[1], transcendentals=0),
    )(*args)


def swap(cells, axis, shift):
    count = lax.axis_size(axis)
    pairs = []
    for first in range(shift, count, 2):
        second = (first + 1) % count
        pairs += [(first, second), (second, first)]
    return lax.ppermute(cells, axis, pairs)


def swap_inner_lat(cells):
    count, around = lax.axis_size("lat"), lax.axis_size("lon")
    pairs = []
    for j in range(around):
        pairs += [(i * around + j, i * around + (j ^ 1)) for i in (0, count - 1)]
        for i in range(1, count - 1, 2):
            pairs += [(i * around + j, (i + 1) * around + j), ((i + 1) * around + j, i * around + j)]
    return lax.ppermute(cells, ("lat", "lon"), pairs)


def lat_picker(got_a, got_b):
    top_is_a = is_odd("lat") == 1
    index = lax.axis_index("lat")
    inner = (index > 0) & (index < lax.axis_size("lat") - 1)

    def pick(first, last, top):
        a, b = got_a[first:last, :], got_b[first:last, :]
        return jnp.where(top_is_a == top, a, jnp.where(inner, b, jnp.zeros_like(b)))

    return pick


def fetch(fields, cotangent, filters, reach, fields_here, cotangent_here, taps, filters_here, reach_here, raw, sems):
    copies = [
        pltpu.make_async_copy(src, dst, sems.at[n])
        for n, (src, dst) in enumerate(
            ((filters, filters_here), (reach, reach_here), (fields, fields_here), (cotangent, cotangent_here))
        )
    ]
    for copy in copies:
        copy.start()
    rows = taps.shape[0]
    raw[...] = jnp.zeros(raw.shape, F32)
    offset = jnp.abs(lax.broadcasted_iota(jnp.int32, (8 * KB, 128), 1) - LREACH)
    copies[0].wait()
    copies[1].wait()
    for k in range(KB):
        for a in range(3):
            line = filters_here[k, a].astype(F32)
            for r in range(rows):
                raw[r, 8 * k + a : 8 * k + a + 1, 0:TAPS] = line[r : r + 1]
    for r in range(rows):
        taps[r] = jnp.where(offset <= reach_here[r], raw[r], 0.0).astype(BF16)
    copies[2].wait()
    copies[3].wait()


def fill_lat(send, low, fields, cotangent, taps):
    rows, width, chans = fields.shape
    step = ceil_to(width, 16)
    send[0:width, :] = fields[low * (rows - 2)]
    send[step : step + width, :] = fields[low * (rows - 2) + 1]
    send[2 * step : 2 * step + width, :] = cotangent[low * (rows - 1)]
    own = taps[low * (rows - 1)]
    send[3 * step : 3 * step + 16, 0:128] = own[0:16]
    send[3 * step : 3 * step + 16, 128:256] = own[16:32]


def fill_lon(send_c, send_d, near, far):
    odd = is_odd("lon") == 1
    at = 0
    for first, last in zip(near, far, strict=True):
        size = first.shape[0]
        send_c[at : at + size, :] = jnp.where(odd, first, last)
        send_d[at : at + size, :] = jnp.where(odd, last, first)
        at += size


def pack_b(fields, cotangent, taps, send_b):
    fill_lat(send_b, is_odd("lat"), fields, cotangent, taps)


def pack_own(fields, cotangent, taps, send_a, send_c, send_d):
    rows, width, chans = fields.shape
    fill_lat(send_a, 1 - is_odd("lat"), fields, cotangent, taps)

    def edges(first, last, own):
        return jnp.concatenate([own[r, first:last, :].astype(F32) for r in range(rows)], axis=0).astype(BF16)

    near = edges(0, EDGE, fields), edges(0, LREACH, cotangent)
    far = edges(width - EDGE, width, fields), edges(width - LREACH, width, cotangent)
    fill_lon(send_c, send_d, near, far)


def pack_corners(width, got_a, got_b, send_c, send_d):
    step = (got_a.shape[0] - 16) // 3
    lat_rows = lat_picker(got_a, got_b)

    def edges(first, last, starts):
        parts = [lat_rows(at + first, at + last, top).astype(F32) for top in (True, False) for at in starts]
        return jnp.concatenate(parts, axis=0).astype(BF16)

    near = edges(0, EDGE, (0, step)), edges(0, LREACH, (2 * step,))
    far = edges(width - EDGE, width, (0, step)), edges(width - LREACH, width, (2 * step,))
    fill_lon(send_c, send_d, near, far)


def lay_taps(every, pitch, lanes):
    groups = every.shape[0] // 8

    def places(shape, dim):
        col = lax.broadcasted_iota(jnp.int32, shape, dim)
        turned = col >= lanes
        inner = jnp.where(turned, col - lanes, col)
        part = jnp.where(inner >= pitch, 1, 0) + jnp.where(inner >= 2 * pitch, 1, 0)
        return turned, inner - pitch * part, part

    turned, place, _ = places((128, 2 * lanes), 1)
    tap = lax.broadcasted_iota(jnp.int32, (128, 2 * lanes), 0)
    wanted = jnp.where(turned, 2 * LREACH - place, place)
    table = jnp.where((tap == wanted) & (tap < TAPS), 1.0, 0.0).astype(BF16)
    spread = jnp.dot(every, table, preferred_element_type=F32).reshape(groups, 8, 2 * lanes)
    turned, _, part = places((groups, 8, 2 * lanes), 2)
    lat_tap = lax.broadcasted_iota(jnp.int32, (groups, 8, 2 * lanes), 1)
    chosen = jnp.where(turned, 2 - part, part) == lat_tap
    return jnp.sum(jnp.where(chosen, spread, 0.0), axis=1)


def build_bands(every, forward, backward, size, pitch, lanes):
    lines = lay_taps(every, pitch, lanes)
    rows = every.shape[0] // (8 * KB) - 2
    lane = lax.broadcasted_iota(jnp.int32, (1, lanes), 1)

    def slant(line):
        return pltpu.roll(jnp.broadcast_to(line, (size, lanes)), 0, 1, stride=1, stride_axis=0).astype(BF16)

    for i in range(rows + 2):
        for k in range(KB):
            at = KB * i + k
            forward[i, size * k : size * (k + 1), :] = slant(lines[at : at + 1, 0:lanes])
    for i in range(rows):
        for k in range(KB):
            near = [lines[KB * (i + t) + k : KB * (i + t) + k + 1, lanes:] for t in range(3)]
            line = jnp.where(lane < pitch, near[0], jnp.where(lane < 2 * pitch, near[1], near[2]))
            backward[i, size * k : size * (k + 1), :] = slant(line)


def gelu_parts(pre):
    size = jnp.abs(pre)
    bell = jnp.exp(-0.5 * pre * pre)
    t = 1.0 / (1.0 + 0.23164188836 * size)
    poly = t * (0.127414796 + t * (-0.142248368 + t * (0.7107068705 + t * (-0.7265760135 + t * 0.5307027145))))
    tail = poly * bell
    cdf = jnp.where(pre >= 0.0, 1.0 - tail, tail)
    return pre * cdf, cdf + pre * bell * 0.3989422804014327


def contract_last(left, right):
    return lax.dot_general(left, right, (((1,), (1,)), ((), ())), preferred_element_type=F32)


def mlp(hidden, upstream, w_up, w_down, first, last):
    pre = jnp.dot(hidden[...], w_up[...], preferred_element_type=F32)
    active, slope = gelu_parts(pre)
    out = hidden[first:last, :].astype(F32) + jnp.dot(
        active[first:last].astype(BF16), w_down[...], preferred_element_type=F32
    )
    grad_active = (contract_last(upstream[...], w_down[...]) * slope).astype(BF16)
    return out, (upstream[...].astype(F32) + contract_last(grad_active, w_up[...])).astype(BF16)


def middle_kernel(
    fields, cotangent, taps, got_a, got_b, w_mix, w_up, w_down,
    result, field_grad, edge_grads, edge_forward, edge_backward,
    forward, backward, wide, narrow, basis, hidden, upstream, grads, grad_mixed,
):
    rows, width, chans = fields.shape
    step = ceil_to(width, 16)
    pick = lat_picker(got_a, got_b)
    ext = rows + 2
    rest = EDGE
    span = BLOCK + rest

    def lat_rows(at, size, top):
        return pick(at, at + size, top)

    def taps_of(top):
        both = lat_rows(3 * step, 16, top)
        return [both[:, 0:128], both[:, 128:256]]

    every = jnp.concatenate(taps_of(True) + [taps[r] for r in range(rows)] + taps_of(False), axis=0)
    build_bands(every, forward, backward, BLOCK, PITCH, LANES)
    build_bands(every, edge_forward, edge_backward, EDGE, EDGE_PITCH, EDGE_LANES)

    fill = PITCH + EDGE - width
    for i in range(rows + 4):
        if i < 2:
            line = lat_rows(step * i, width, True)
        elif i < rows + 2:
            line = fields[i - 2]
        else:
            line = lat_rows(step * (i - rows - 2), width, False)
        wide[PITCH * i : PITCH * (i + 1), :] = line[0:PITCH]
        tail = jnp.concatenate([line[BLOCK:].astype(F32), jnp.zeros((fill, chans), F32)], axis=0)
        narrow[EDGE_PITCH * i : EDGE_PITCH * (i + 1), :] = tail.astype(BF16)
    wide[PITCH * (rows + 4) :, :] = jnp.zeros((LANES - 3 * PITCH, chans), BF16)
    narrow[EDGE_PITCH * (rows + 4) :, :] = jnp.zeros((EDGE_LANES - 3 * EDGE_PITCH, chans), BF16)

    for i in range(ext):
        at = span * i
        moved = jnp.dot(forward[i], wide[PITCH * i : PITCH * i + LANES, :], preferred_element_type=F32).astype(BF16)
        other = jnp.dot(
            edge_forward[i], narrow[EDGE_PITCH * i : EDGE_PITCH * i + EDGE_LANES, :], preferred_element_type=F32
        ).astype(BF16)
        for k in range(KB):
            basis[at : at + BLOCK, chans * k : chans * (k + 1)] = moved[BLOCK * k : BLOCK * (k + 1)]
            basis[at + BLOCK : at + span, chans * k : chans * (k + 1)] = other[rest * k : rest * (k + 1)]
    stacked = jnp.concatenate([w_mix[:, chans * k : chans * (k + 1)] for k in range(KB)], axis=0)
    spatial = jnp.dot(basis[...], stacked, preferred_element_type=F32)
    for i in range(ext):
        at = PITCH * (i + 1)
        first = wide[at : at + PITCH, :].astype(F32)[LREACH : LREACH + BLOCK]
        at = EDGE_PITCH * (i + 1)
        second = narrow[at : at + EDGE_PITCH, :].astype(F32)[LREACH : LREACH + rest]
        here = span * i
        mine = jnp.concatenate([first, second], axis=0) + spatial[here : here + span]
        hidden[here : here + span, :] = mine.astype(BF16)
        if i == 0:
            up = lat_rows(2 * step, width, True)
        elif i < ext - 1:
            up = cotangent[i - 1]
        else:
            up = lat_rows(2 * step, width, False)
        upstream[here : here + span, :] = up.astype(F32)[LREACH : LREACH + span].astype(BF16)
    out, grad = mlp(hidden, upstream, w_up, w_down, span, span * (rows + 1))
    result[...] = out.reshape(result.shape).astype(BF16)
    grads[0 : span * ext, :] = grad
    grads[span * ext :, :] = jnp.zeros((LANES - 3 * PITCH, chans), BF16)
    far = width - EDGE - 2 * LREACH
    for i in range(ext):
        mine = grad[span * i : span * (i + 1)]
        edge_grads[0, EDGE * i : EDGE * (i + 1), :] = mine[0:EDGE]
        edge_grads[1, EDGE * i : EDGE * (i + 1), :] = mine.astype(F32)[far : far + EDGE].astype(BF16)

    for i in range(rows):
        moved = jnp.dot(backward[i], grads[PITCH * i : PITCH * i + LANES, :], preferred_element_type=F32).astype(BF16)
        for k in range(KB):
            grad_mixed[BLOCK * i : BLOCK * (i + 1), chans * k : chans * (k + 1)] = moved[BLOCK * k : BLOCK * (k + 1)]
    back = contract_last(grad_mixed[...], w_mix[...])
    for i in range(rows):
        at = PITCH * (i + 1)
        own = grads[at : at + PITCH, :].astype(F32)[LREACH : LREACH + BLOCK]
        field_grad[i] = (own + back[BLOCK * i : BLOCK * (i + 1)]).astype(BF16)


def edge_kernel(
    middle_result, middle_grad, edge_grads, edge_forward, edge_backward,
    send_c, send_d, got_c, got_d, corner_send_c, corner_send_d, corner_got_c, corner_got_d, w_mix, w_up, w_down,
    result, field_grad, source, basis, hidden, upstream, grads, grad_mixed,
):
    rows, width, chans = result.shape
    ext = rows + 2
    left_is_c = is_odd("lon") == 1
    own = (send_c, send_d), (got_c, got_d)
    corners = (corner_send_c, corner_send_d), (corner_got_c, corner_got_d)

    def both_sides(at, arrays):
        (sent_c, sent_d), (came_c, came_d) = [[x[at : at + EDGE, :] for x in pair] for pair in arrays]
        left = jnp.where(left_is_c, came_c, came_d), jnp.where(left_is_c, sent_c, sent_d)
        right = jnp.where(left_is_c, sent_d, sent_c), jnp.where(left_is_c, came_d, came_c)
        return left, right

    for i in range(rows + 4):
        if 2 <= i < rows + 2:
            sides = both_sides(EDGE * (i - 2), own)
        else:
            sides = both_sides(EDGE * (i if i < 2 else i - rows), corners)
        at = EDGE_PITCH * i
        for part, (first, second) in enumerate(sides):
            source[at : at + EDGE, chans * part : chans * (part + 1)] = first
            source[at + EDGE : at + 2 * EDGE, chans * part : chans * (part + 1)] = second
    source[EDGE_PITCH * (rows + 4) :, :] = jnp.zeros((EDGE_LANES - 3 * EDGE_PITCH, 2 * chans), BF16)

    for i in range(ext):
        if 0 < i < ext - 1:
            sides = both_sides(EDGE * rows + EDGE * ((i - 1) // 2), own)
            inside = LREACH * ((i - 1) % 2)
        else:
            sides = both_sides(EDGE * 4, corners)
            inside = 0 if i == 0 else LREACH
        for part, halves in enumerate(sides):
            here = EDGE * (2 * i + part)
            whole = [x.astype(F32)[inside : inside + LREACH] for x in halves]
            upstream[here : here + EDGE, :] = jnp.concatenate(whole, axis=0).astype(BF16)

    def spread(band, cells, at, out):
        moved = jnp.dot(band, cells, preferred_element_type=F32).astype(BF16)
        for part in range(2):
            for k in range(KB):
                out[at + EDGE * part : at + EDGE * (part + 1), chans * k : chans * (k + 1)] = moved[
                    EDGE * k : EDGE * (k + 1), chans * part : chans * (part + 1)
                ]

    for i in range(ext):
        spread(edge_forward[i], source[EDGE_PITCH * i : EDGE_PITCH * i + EDGE_LANES, :], 2 * EDGE * i, basis)
    stacked = jnp.concatenate([w_mix[:, chans * k : chans * (k + 1)] for k in range(KB)], axis=0)
    spatial = jnp.dot(basis[...], stacked, preferred_element_type=F32)
    for i in range(ext):
        at = EDGE_PITCH * (i + 1)
        cells = source[at : at + EDGE_PITCH, :].astype(F32)[LREACH : LREACH + EDGE]
        for part in range(2):
            here = EDGE * (2 * i + part)
            hidden[here : here + EDGE, :] = (
                cells[:, chans * part : chans * (part + 1)] + spatial[here : here + EDGE]
            ).astype(BF16)
    out, grad = mlp(hidden, upstream, w_up, w_down, 2 * EDGE, 2 * EDGE * (rows + 1))
    for i in range(rows):
        here = 2 * EDGE * i
        left = out[here + LREACH : here + EDGE]
        right = out[here + EDGE : here + EDGE + LREACH]
        middle = middle_result[i].astype(F32)[0 : width - 2 * LREACH]
        result[i] = jnp.concatenate([left, middle, right], axis=0).astype(BF16)

    for i in range(ext):
        at = EDGE_PITCH * i
        here = 2 * EDGE * i
        grads[at : at + EDGE, 0:chans] = grad[here : here + EDGE]
        grads[at + EDGE : at + 2 * EDGE, 0:chans] = edge_grads[0, EDGE * i : EDGE * (i + 1), :]
        grads[at : at + EDGE, chans:] = edge_grads[1, EDGE * i : EDGE * (i + 1), :]
        grads[at + EDGE : at + 2 * EDGE, chans:] = grad[here + EDGE : here + 2 * EDGE]
    grads[EDGE_PITCH * ext :, :] = jnp.zeros((EDGE_LANES - 3 * EDGE_PITCH, 2 * chans), BF16)
    for i in range(rows):
        spread(edge_backward[i], grads[EDGE_PITCH * i : EDGE_PITCH * i + EDGE_LANES, :], 2 * EDGE * i, grad_mixed)
    back = contract_last(grad_mixed[...], w_mix[...])
    for i in range(rows):
        at = EDGE_PITCH * (i + 1)
        own = grads[at : at + EDGE_PITCH, :].astype(F32)[LREACH : LREACH + EDGE]
        here = 2 * EDGE * i
        left = own[:, 0:chans] + back[here : here + EDGE]
        right = own[:, chans:] + back[here + EDGE : here + 2 * EDGE]
        middle = middle_grad[i].astype(F32)[0 : width - 2 * EDGE]
        field_grad[i] = jnp.concatenate([left, middle, right], axis=0).astype(BF16)


def store(result, field_grad, result_out, field_grad_out, sems):
    copies = [
        pltpu.make_async_copy(result, result_out, sems.at[0]),
        pltpu.make_async_copy(field_grad, field_grad_out, sems.at[1]),
    ]
    for copy in copies:
        copy.start()
    for copy in copies:
        copy.wait()


def on_device(fields, w_mix, filters, reach, w_up, w_down, cotangent):
    rows, width, chans = fields.shape
    step = ceil_to(width, 16)
    ext = rows + 2
    span = BLOCK + EDGE
    pad = LANES - 3 * PITCH
    edge_pad = EDGE_LANES - 3 * EDGE_PITCH

    def shaped(*shape):
        return jax.ShapeDtypeStruct(shape, BF16)

    turned = shaped(width, rows, chans)
    fields_here, cotangent_here, taps = call(
        fetch,
        (turned, turned, shaped(rows, 8 * KB, 128)),
        [hbm()] * 4,
        [
            pltpu.VMEM((KB, 3, rows, TAPS), BF16),
            pltpu.SMEM((rows,), jnp.int32),
            pltpu.VMEM((rows, 8 * KB, 128), F32),
            pltpu.SemaphoreType.DMA((4,)),
        ],
        (1000, 1000000),
        *(
            pltpu.with_memory_space_constraint(x, pltpu.HBM)
            for x in (fields.transpose(1, 0, 2), cotangent.transpose(1, 0, 2), filters.transpose(0, 2, 1, 3), reach)
        ),
    )
    fields = fields_here.transpose(1, 0, 2)
    cotangent = cotangent_here.transpose(1, 0, 2)
    sent = shaped(3 * step + 16, chans)
    send_b = call(pack_b, sent, [vmem()] * 3, [], (1000, 1000000), fields, cotangent, taps)
    got_b = swap_inner_lat(send_b)
    edge = shaped((EDGE + LREACH) * rows, chans)
    send_a, send_c, send_d = call(
        pack_own, (sent, edge, edge), [vmem()] * 3, [], (2000000000, 5000000), fields, cotangent, taps
    )
    got_a = swap(send_a, "lat", 0)
    got_d = swap(send_d, "lon", 1)
    got_c = swap(send_c, "lon", 0)
    corner = shaped(4 * EDGE + 2 * LREACH, chans)
    corner_send_c, corner_send_d = call(
        functools.partial(pack_corners, width), (corner, corner), [vmem()] * 2, [], (1000, 1000000), got_a, got_b
    )
    corner_got_d = swap(corner_send_d, "lon", 1)
    corner_got_c = swap(corner_send_c, "lon", 0)
    middle_result, middle_grad, edge_grads, edge_forward, edge_backward = call(
        middle_kernel,
        (
            shaped(rows, span, chans),
            shaped(rows, BLOCK, chans),
            shaped(2, EDGE * ext, chans),
            shaped(ext, KB * EDGE, EDGE_LANES),
            shaped(rows, KB * EDGE, EDGE_LANES),
        ),
        [vmem()] * 8,
        [
            pltpu.VMEM((ext, KB * BLOCK, LANES), BF16),
            pltpu.VMEM((rows, KB * BLOCK, LANES), BF16),
            pltpu.VMEM((PITCH * (rows + 4) + pad, chans), BF16),
            pltpu.VMEM((EDGE_PITCH * (rows + 4) + edge_pad, chans), BF16),
            pltpu.VMEM((span * ext, KB * chans), BF16),
            pltpu.VMEM((span * ext, chans), BF16),
            pltpu.VMEM((span * ext, chans), BF16),
            pltpu.VMEM((span * ext + pad, chans), BF16),
            pltpu.VMEM((BLOCK * rows, KB * chans), BF16),
        ],
        (2000000000, 5000000),
        fields, cotangent, taps, got_a, got_b, w_mix, w_up, w_down,
    )
    out = shaped(rows, width, chans)
    result, field_grad = call(
        edge_kernel,
        (out, out),
        [vmem()] * 16,
        [
            pltpu.VMEM((EDGE_PITCH * (rows + 4) + edge_pad, 2 * chans), BF16),
            pltpu.VMEM((2 * EDGE * ext, KB * chans), BF16),
            pltpu.VMEM((2 * EDGE * ext, chans), BF16),
            pltpu.VMEM((2 * EDGE * ext, chans), BF16),
            pltpu.VMEM((EDGE_PITCH * ext + edge_pad, 2 * chans), BF16),
            pltpu.VMEM((2 * EDGE * rows, KB * chans), BF16),
        ],
        (500000000, 3000000),
        middle_result, middle_grad, edge_grads, edge_forward, edge_backward,
        send_c, send_d, got_c, got_d, corner_send_c, corner_send_d, corner_got_c, corner_got_d, w_mix, w_up, w_down,
    )
    result, field_grad = call(
        store,
        (turned, turned),
        [vmem()] * 2,
        [pltpu.SemaphoreType.DMA((2,))],
        (1000, 700000),
        result.transpose(1, 0, 2), field_grad.transpose(1, 0, 2),
        out_specs=(hbm(), hbm()),
    )
    return result.transpose(1, 0, 2), field_grad.transpose(1, 0, 2)


def solution(mesh):
    return jax.shard_map(
        on_device,
        mesh=mesh,
        in_specs=(
            P("lat", "lon", None),
            P(),
            P(None, "lat", None, None),
            P("lat"),
            P(),
            P(),
            P("lat", "lon", None),
        ),
        out_specs=(P("lat", "lon", None), P("lat", "lon", None)),
        check_vma=False,
    )
```

```python
import functools

import jax
import jax.numpy as jnp
from jax import lax
from jax.experimental import pallas as pl
from jax.experimental.pallas import tpu as pltpu
from jax.sharding import PartitionSpec as P

KB = 4
LREACH = 8
TAPS = 2 * LREACH + 1
BLOCK = 64
PITCH = BLOCK + 2 * LREACH
EDGE = 2 * LREACH
EDGE_PITCH = 2 * EDGE
LANES = 256
EDGE_LANES = 128
F32 = jnp.float32
BF16 = jnp.bfloat16
VMEM_BYTES = 48 * 1024 * 1024


def ceil_to(size, unit):
    return -(-size // unit) * unit


def vmem():
    return pl.BlockSpec(memory_space=pltpu.VMEM)


def hbm():
    return pl.BlockSpec(memory_space=pltpu.HBM)


def is_odd(axis):
    return lax.rem(lax.axis_index(axis), 2)


def call(kernel, outs, in_specs, scratch, cost, *args, out_specs=None):
    return pl.pallas_call(
        kernel,
        out_shape=outs,
        in_specs=in_specs,
        out_specs=out_specs or jax.tree.map(lambda _: vmem(), outs),
        scratch_shapes=scratch,
        compiler_params=pltpu.CompilerParams(vmem_limit_bytes=VMEM_BYTES),
        cost_estimate=pl.CostEstimate(flops=cost[0], bytes_accessed=cost[1], transcendentals=0),
    )(*args)


def swap(cells, axis, shift):
    count = lax.axis_size(axis)
    pairs = []
    for first in range(shift, count, 2):
        second = (first + 1) % count
        pairs += [(first, second), (second, first)]
    return lax.ppermute(cells, axis, pairs)


def swap_inner_lat(cells):
    count, around = lax.axis_size("lat"), lax.axis_size("lon")
    pairs = []
    for j in range(around):
        pairs += [(i * around + j, i * around + (j + around // 2) % around) for i in (0, count - 1)]
        for i in range(1, count - 1, 2):
            pairs += [(i * around + j, (i + 1) * around + j), ((i + 1) * around + j, i * around + j)]
    return lax.ppermute(cells, ("lat", "lon"), pairs)


def lat_picker(got_a, got_b):
    top_is_a = is_odd("lat") == 1
    index = lax.axis_index("lat")
    inner = (index > 0) & (index < lax.axis_size("lat") - 1)

    def pick(first, last, top):
        a, b = got_a[first:last, :], got_b[first:last, :]
        return jnp.where(top_is_a == top, a, jnp.where(inner, b, jnp.zeros_like(b)))

    return pick


def fetch(fields, cotangent, filters, reach, fields_here, cotangent_here, taps, filters_here, reach_here, raw, sems):
    copies = [
        pltpu.make_async_copy(src, dst, sems.at[n])
        for n, (src, dst) in enumerate(
            ((filters, filters_here), (reach, reach_here), (fields, fields_here), (cotangent, cotangent_here))
        )
    ]
    for copy in copies:
        copy.start()
    rows = taps.shape[0]
    raw[...] = jnp.zeros(raw.shape, F32)
    offset = jnp.abs(lax.broadcasted_iota(jnp.int32, (8 * KB, 128), 1) - LREACH)
    copies[0].wait()
    copies[1].wait()
    for k in range(KB):
        for a in range(3):
            line = filters_here[k, a].astype(F32)
            for r in range(rows):
                raw[r, 8 * k + a : 8 * k + a + 1, 0:TAPS] = line[r : r + 1]
    for r in range(rows):
        taps[r] = jnp.where(offset <= reach_here[r], raw[r], 0.0).astype(BF16)
    copies[2].wait()
    copies[3].wait()


def fill_lat(send, low, fields, cotangent, taps):
    rows, width, chans = fields.shape
    step = ceil_to(width, 16)
    send[0:width, :] = fields[low * (rows - 2)]
    send[step : step + width, :] = fields[low * (rows - 2) + 1]
    send[2 * step : 2 * step + width, :] = cotangent[low * (rows - 1)]
    own = taps[low * (rows - 1)]
    send[3 * step : 3 * step + 16, 0:128] = own[0:16]
    send[3 * step : 3 * step + 16, 128:256] = own[16:32]


def fill_lon(send_c, send_d, near, far):
    odd = is_odd("lon") == 1
    at = 0
    for first, last in zip(near, far, strict=True):
        size = first.shape[0]
        send_c[at : at + size, :] = jnp.where(odd, first, last)
        send_d[at : at + size, :] = jnp.where(odd, last, first)
        at += size


def pack_b(fields, cotangent, taps, send_b):
    fill_lat(send_b, is_odd("lat"), fields, cotangent, taps)


def pack_own(fields, cotangent, taps, send_a, send_c, send_d):
    rows, width, chans = fields.shape
    fill_lat(send_a, 1 - is_odd("lat"), fields, cotangent, taps)

    def edges(first, last, own):
        return jnp.concatenate([own[r, first:last, :].astype(F32) for r in range(rows)], axis=0).astype(BF16)

    near = edges(0, EDGE, fields), edges(0, LREACH, cotangent)
    far = edges(width - EDGE, width, fields), edges(width - LREACH, width, cotangent)
    fill_lon(send_c, send_d, near, far)


def pack_corners(width, got_a, got_b, send_c, send_d):
    step = (got_a.shape[0] - 16) // 3
    lat_rows = lat_picker(got_a, got_b)

    def edges(first, last, starts):
        parts = [lat_rows(at + first, at + last, top).astype(F32) for top in (True, False) for at in starts]
        return jnp.concatenate(parts, axis=0).astype(BF16)

    near = edges(0, EDGE, (0, step)), edges(0, LREACH, (2 * step,))
    far = edges(width - EDGE, width, (0, step)), edges(width - LREACH, width, (2 * step,))
    fill_lon(send_c, send_d, near, far)


def lay_taps(every, pitch, lanes):
    groups = every.shape[0] // 8

    def places(shape, dim):
        col = lax.broadcasted_iota(jnp.int32, shape, dim)
        turned = col >= lanes
        inner = jnp.where(turned, col - lanes, col)
        part = jnp.where(inner >= pitch, 1, 0) + jnp.where(inner >= 2 * pitch, 1, 0)
        return turned, inner - pitch * part, part

    turned, place, _ = places((128, 2 * lanes), 1)
    tap = lax.broadcasted_iota(jnp.int32, (128, 2 * lanes), 0)
    wanted = jnp.where(turned, 2 * LREACH - place, place)
    table = jnp.where((tap == wanted) & (tap < TAPS), 1.0, 0.0).astype(BF16)
    spread = jnp.dot(every, table, preferred_element_type=F32).reshape(groups, 8, 2 * lanes)
    turned, _, part = places((groups, 8, 2 * lanes), 2)
    lat_tap = lax.broadcasted_iota(jnp.int32, (groups, 8, 2 * lanes), 1)
    chosen = jnp.where(turned, 2 - part, part) == lat_tap
    return jnp.sum(jnp.where(chosen, spread, 0.0), axis=1)


def build_bands(every, forward, backward, size, pitch, lanes):
    lines = lay_taps(every, pitch, lanes)
    rows = every.shape[0] // (8 * KB) - 2
    lane = lax.broadcasted_iota(jnp.int32, (1, lanes), 1)

    def slant(line):
        return pltpu.roll(jnp.broadcast_to(line, (size, lanes)), 0, 1, stride=1, stride_axis=0).astype(BF16)

    for i in range(rows + 2):
        for k in range(KB):
            at = KB * i + k
            forward[i, size * k : size * (k + 1), :] = slant(lines[at : at + 1, 0:lanes])
    for i in range(rows):
        for k in range(KB):
            near = [lines[KB * (i + t) + k : KB * (i + t) + k + 1, lanes:] for t in range(3)]
            line = jnp.where(lane < pitch, near[0], jnp.where(lane < 2 * pitch, near[1], near[2]))
            backward[i, size * k : size * (k + 1), :] = slant(line)


def gelu_parts(pre):
    size = jnp.abs(pre)
    bell = jnp.exp(-0.5 * pre * pre)
    t = 1.0 / (1.0 + 0.23164188836 * size)
    poly = t * (0.127414796 + t * (-0.142248368 + t * (0.7107068705 + t * (-0.7265760135 + t * 0.5307027145))))
    tail = poly * bell
    cdf = jnp.where(pre >= 0.0, 1.0 - tail, tail)
    return pre * cdf, cdf + pre * bell * 0.3989422804014327


def contract_last(left, right):
    return lax.dot_general(left, right, (((1,), (1,)), ((), ())), preferred_element_type=F32)


def mlp(hidden, upstream, w_up, w_down, first, last):
    pre = jnp.dot(hidden[...], w_up[...], preferred_element_type=F32)
    active, slope = gelu_parts(pre)
    out = hidden[first:last, :].astype(F32) + jnp.dot(
        active[first:last].astype(BF16), w_down[...], preferred_element_type=F32
    )
    grad_active = (contract_last(upstream[...], w_down[...]) * slope).astype(BF16)
    return out, (upstream[...].astype(F32) + contract_last(grad_active, w_up[...])).astype(BF16)


def middle_kernel(
    fields, cotangent, taps, got_a, got_b, w_mix, w_up, w_down,
    result, field_grad, edge_grads, edge_forward, edge_backward,
    forward, backward, wide, narrow, basis, hidden, upstream, grads, grad_mixed,
):
    rows, width, chans = fields.shape
    step = ceil_to(width, 16)
    pick = lat_picker(got_a, got_b)
    ext = rows + 2
    rest = EDGE
    span = BLOCK + rest

    def lat_rows(at, size, top):
        return pick(at, at + size, top)

    def taps_of(top):
        both = lat_rows(3 * step, 16, top)
        return [both[:, 0:128], both[:, 128:256]]

    every = jnp.concatenate(taps_of(True) + [taps[r] for r in range(rows)] + taps_of(False), axis=0)
    build_bands(every, forward, backward, BLOCK, PITCH, LANES)
    build_bands(every, edge_forward, edge_backward, EDGE, EDGE_PITCH, EDGE_LANES)

    fill = PITCH + EDGE - width
    for i in range(rows + 4):
        if i < 2:
            line = lat_rows(step * i, width, True)
        elif i < rows + 2:
            line = fields[i - 2]
        else:
            line = lat_rows(step * (i - rows - 2), width, False)
        wide[PITCH * i : PITCH * (i + 1), :] = line[0:PITCH]
        tail = jnp.concatenate([line[BLOCK:].astype(F32), jnp.zeros((fill, chans), F32)], axis=0)
        narrow[EDGE_PITCH * i : EDGE_PITCH * (i + 1), :] = tail.astype(BF16)
    wide[PITCH * (rows + 4) :, :] = jnp.zeros((LANES - 3 * PITCH, chans), BF16)
    narrow[EDGE_PITCH * (rows + 4) :, :] = jnp.zeros((EDGE_LANES - 3 * EDGE_PITCH, chans), BF16)

    for i in range(ext):
        at = span * i
        moved = jnp.dot(forward[i], wide[PITCH * i : PITCH * i + LANES, :], preferred_element_type=F32).astype(BF16)
        other = jnp.dot(
            edge_forward[i], narrow[EDGE_PITCH * i : EDGE_PITCH * i + EDGE_LANES, :], preferred_element_type=F32
        ).astype(BF16)
        for k in range(KB):
            basis[at : at + BLOCK, chans * k : chans * (k + 1)] = moved[BLOCK * k : BLOCK * (k + 1)]
            basis[at + BLOCK : at + span, chans * k : chans * (k + 1)] = other[rest * k : rest * (k + 1)]
    stacked = jnp.concatenate([w_mix[:, chans * k : chans * (k + 1)] for k in range(KB)], axis=0)
    spatial = jnp.dot(basis[...], stacked, preferred_element_type=F32)
    for i in range(ext):
        at = PITCH * (i + 1)
        first = wide[at : at + PITCH, :].astype(F32)[LREACH : LREACH + BLOCK]
        at = EDGE_PITCH * (i + 1)
        second = narrow[at : at + EDGE_PITCH, :].astype(F32)[LREACH : LREACH + rest]
        here = span * i
        mine = jnp.concatenate([first, second], axis=0) + spatial[here : here + span]
        hidden[here : here + span, :] = mine.astype(BF16)
        if i == 0:
            up = lat_rows(2 * step, width, True)
        elif i < ext - 1:
            up = cotangent[i - 1]
        else:
            up = lat_rows(2 * step, width, False)
        upstream[here : here + span, :] = up.astype(F32)[LREACH : LREACH + span].astype(BF16)
    out, grad = mlp(hidden, upstream, w_up, w_down, span, span * (rows + 1))
    result[...] = out.reshape(result.shape).astype(BF16)
    grads[0 : span * ext, :] = grad
    grads[span * ext :, :] = jnp.zeros((LANES - 3 * PITCH, chans), BF16)
    far = width - EDGE - 2 * LREACH
    for i in range(ext):
        mine = grad[span * i : span * (i + 1)]
        edge_grads[0, EDGE * i : EDGE * (i + 1), :] = mine[0:EDGE]
        edge_grads[1, EDGE * i : EDGE * (i + 1), :] = mine.astype(F32)[far : far + EDGE].astype(BF16)

    for i in range(rows):
        moved = jnp.dot(backward[i], grads[PITCH * i : PITCH * i + LANES, :], preferred_element_type=F32).astype(BF16)
        for k in range(KB):
            grad_mixed[BLOCK * i : BLOCK * (i + 1), chans * k : chans * (k + 1)] = moved[BLOCK * k : BLOCK * (k + 1)]
    back = contract_last(grad_mixed[...], w_mix[...])
    for i in range(rows):
        at = PITCH * (i + 1)
        own = grads[at : at + PITCH, :].astype(F32)[LREACH : LREACH + BLOCK]
        field_grad[i] = (own + back[BLOCK * i : BLOCK * (i + 1)]).astype(BF16)


def edge_kernel(
    middle_result, middle_grad, edge_grads, edge_forward, edge_backward,
    send_c, send_d, got_c, got_d, corner_send_c, corner_send_d, corner_got_c, corner_got_d, w_mix, w_up, w_down,
    result, field_grad, source, basis, hidden, upstream, grads, grad_mixed,
):
    rows, width, chans = result.shape
    ext = rows + 2
    left_is_c = is_odd("lon") == 1
    own = (send_c, send_d), (got_c, got_d)
    corners = (corner_send_c, corner_send_d), (corner_got_c, corner_got_d)

    def both_sides(at, arrays):
        (sent_c, sent_d), (came_c, came_d) = [[x[at : at + EDGE, :] for x in pair] for pair in arrays]
        left = jnp.where(left_is_c, came_c, came_d), jnp.where(left_is_c, sent_c, sent_d)
        right = jnp.where(left_is_c, sent_d, sent_c), jnp.where(left_is_c, came_d, came_c)
        return left, right

    for i in range(rows + 4):
        if 2 <= i < rows + 2:
            sides = both_sides(EDGE * (i - 2), own)
        else:
            sides = both_sides(EDGE * (i if i < 2 else i - rows), corners)
        at = EDGE_PITCH * i
        for part, (first, second) in enumerate(sides):
            source[at : at + EDGE, chans * part : chans * (part + 1)] = first
            source[at + EDGE : at + 2 * EDGE, chans * part : chans * (part + 1)] = second
    source[EDGE_PITCH * (rows + 4) :, :] = jnp.zeros((EDGE_LANES - 3 * EDGE_PITCH, 2 * chans), BF16)

    for i in range(ext):
        if 0 < i < ext - 1:
            sides = both_sides(EDGE * rows + EDGE * ((i - 1) // 2), own)
            inside = LREACH * ((i - 1) % 2)
        else:
            sides = both_sides(EDGE * 4, corners)
            inside = 0 if i == 0 else LREACH
        for part, halves in enumerate(sides):
            here = EDGE * (2 * i + part)
            whole = [x.astype(F32)[inside : inside + LREACH] for x in halves]
            upstream[here : here + EDGE, :] = jnp.concatenate(whole, axis=0).astype(BF16)

    def spread(band, cells, at, out):
        moved = jnp.dot(band, cells, preferred_element_type=F32).astype(BF16)
        for part in range(2):
            for k in range(KB):
                out[at + EDGE * part : at + EDGE * (part + 1), chans * k : chans * (k + 1)] = moved[
                    EDGE * k : EDGE * (k + 1), chans * part : chans * (part + 1)
                ]

    for i in range(ext):
        spread(edge_forward[i], source[EDGE_PITCH * i : EDGE_PITCH * i + EDGE_LANES, :], 2 * EDGE * i, basis)
    stacked = jnp.concatenate([w_mix[:, chans * k : chans * (k + 1)] for k in range(KB)], axis=0)
    spatial = jnp.dot(basis[...], stacked, preferred_element_type=F32)
    for i in range(ext):
        at = EDGE_PITCH * (i + 1)
        cells = source[at : at + EDGE_PITCH, :].astype(F32)[LREACH : LREACH + EDGE]
        for part in range(2):
            here = EDGE * (2 * i + part)
            hidden[here : here + EDGE, :] = (
                cells[:, chans * part : chans * (part + 1)] + spatial[here : here + EDGE]
            ).astype(BF16)
    out, grad = mlp(hidden, upstream, w_up, w_down, 2 * EDGE, 2 * EDGE * (rows + 1))
    for i in range(rows):
        here = 2 * EDGE * i
        left = out[here + LREACH : here + EDGE]
        right = out[here + EDGE : here + EDGE + LREACH]
        middle = middle_result[i].astype(F32)[0 : width - 2 * LREACH]
        result[i] = jnp.concatenate([left, middle, right], axis=0).astype(BF16)

    for i in range(ext):
        at = EDGE_PITCH * i
        here = 2 * EDGE * i
        grads[at : at + EDGE, 0:chans] = grad[here : here + EDGE]
        grads[at + EDGE : at + 2 * EDGE, 0:chans] = edge_grads[0, EDGE * i : EDGE * (i + 1), :]
        grads[at : at + EDGE, chans:] = edge_grads[1, EDGE * i : EDGE * (i + 1), :]
        grads[at + EDGE : at + 2 * EDGE, chans:] = grad[here + EDGE : here + 2 * EDGE]
    grads[EDGE_PITCH * ext :, :] = jnp.zeros((EDGE_LANES - 3 * EDGE_PITCH, 2 * chans), BF16)
    for i in range(rows):
        spread(edge_backward[i], grads[EDGE_PITCH * i : EDGE_PITCH * i + EDGE_LANES, :], 2 * EDGE * i, grad_mixed)
    back = contract_last(grad_mixed[...], w_mix[...])
    for i in range(rows):
        at = EDGE_PITCH * (i + 1)
        own = grads[at : at + EDGE_PITCH, :].astype(F32)[LREACH : LREACH + EDGE]
        here = 2 * EDGE * i
        left = own[:, 0:chans] + back[here : here + EDGE]
        right = own[:, chans:] + back[here + EDGE : here + 2 * EDGE]
        middle = middle_grad[i].astype(F32)[0 : width - 2 * EDGE]
        field_grad[i] = jnp.concatenate([left, middle, right], axis=0).astype(BF16)


def store(result, field_grad, result_out, field_grad_out, sems):
    copies = [
        pltpu.make_async_copy(result, result_out, sems.at[0]),
        pltpu.make_async_copy(field_grad, field_grad_out, sems.at[1]),
    ]
    for copy in copies:
        copy.start()
    for copy in copies:
        copy.wait()


def on_device(fields, w_mix, filters, reach, w_up, w_down, cotangent):
    rows, width, chans = fields.shape
    step = ceil_to(width, 16)
    ext = rows + 2
    span = BLOCK + EDGE
    pad = LANES - 3 * PITCH
    edge_pad = EDGE_LANES - 3 * EDGE_PITCH

    def shaped(*shape):
        return jax.ShapeDtypeStruct(shape, BF16)

    turned = shaped(width, rows, chans)
    fields_here, cotangent_here, taps = call(
        fetch,
        (turned, turned, shaped(rows, 8 * KB, 128)),
        [hbm()] * 4,
        [
            pltpu.VMEM((KB, 3, rows, TAPS), BF16),
            pltpu.SMEM((rows,), jnp.int32),
            pltpu.VMEM((rows, 8 * KB, 128), F32),
            pltpu.SemaphoreType.DMA((4,)),
        ],
        (1000, 1000000),
        *(
            pltpu.with_memory_space_constraint(x, pltpu.HBM)
            for x in (fields.transpose(1, 0, 2), cotangent.transpose(1, 0, 2), filters.transpose(0, 2, 1, 3), reach)
        ),
    )
    fields = fields_here.transpose(1, 0, 2)
    cotangent = cotangent_here.transpose(1, 0, 2)
    sent = shaped(3 * step + 16, chans)
    send_b = call(pack_b, sent, [vmem()] * 3, [], (1000, 1000000), fields, cotangent, taps)
    got_b = swap_inner_lat(send_b)
    edge = shaped((EDGE + LREACH) * rows, chans)
    send_a, send_c, send_d = call(
        pack_own, (sent, edge, edge), [vmem()] * 3, [], (2000000000, 5000000), fields, cotangent, taps
    )
    got_a = swap(send_a, "lat", 0)
    got_d = swap(send_d, "lon", 1)
    got_c = swap(send_c, "lon", 0)
    corner = shaped(4 * EDGE + 2 * LREACH, chans)
    corner_send_c, corner_send_d = call(
        functools.partial(pack_corners, width), (corner, corner), [vmem()] * 2, [], (1000, 1000000), got_a, got_b
    )
    corner_got_d = swap(corner_send_d, "lon", 1)
    corner_got_c = swap(corner_send_c, "lon", 0)
    middle_result, middle_grad, edge_grads, edge_forward, edge_backward = call(
        middle_kernel,
        (
            shaped(rows, span, chans),
            shaped(rows, BLOCK, chans),
            shaped(2, EDGE * ext, chans),
            shaped(ext, KB * EDGE, EDGE_LANES),
            shaped(rows, KB * EDGE, EDGE_LANES),
        ),
        [vmem()] * 8,
        [
            pltpu.VMEM((ext, KB * BLOCK, LANES), BF16),
            pltpu.VMEM((rows, KB * BLOCK, LANES), BF16),
            pltpu.VMEM((PITCH * (rows + 4) + pad, chans), BF16),
            pltpu.VMEM((EDGE_PITCH * (rows + 4) + edge_pad, chans), BF16),
            pltpu.VMEM((span * ext, KB * chans), BF16),
            pltpu.VMEM((span * ext, chans), BF16),
            pltpu.VMEM((span * ext, chans), BF16),
            pltpu.VMEM((span * ext + pad, chans), BF16),
            pltpu.VMEM((BLOCK * rows, KB * chans), BF16),
        ],
        (2000000000, 5000000),
        fields, cotangent, taps, got_a, got_b, w_mix, w_up, w_down,
    )
    out = shaped(rows, width, chans)
    result, field_grad = call(
        edge_kernel,
        (out, out),
        [vmem()] * 16,
        [
            pltpu.VMEM((EDGE_PITCH * (rows + 4) + edge_pad, 2 * chans), BF16),
            pltpu.VMEM((2 * EDGE * ext, KB * chans), BF16),
            pltpu.VMEM((2 * EDGE * ext, chans), BF16),
            pltpu.VMEM((2 * EDGE * ext, chans), BF16),
            pltpu.VMEM((EDGE_PITCH * ext + edge_pad, 2 * chans), BF16),
            pltpu.VMEM((2 * EDGE * rows, KB * chans), BF16),
        ],
        (500000000, 3000000),
        middle_result, middle_grad, edge_grads, edge_forward, edge_backward,
        send_c, send_d, got_c, got_d, corner_send_c, corner_send_d, corner_got_c, corner_got_d, w_mix, w_up, w_down,
    )
    result, field_grad = call(
        store,
        (turned, turned),
        [vmem()] * 2,
        [pltpu.SemaphoreType.DMA((2,))],
        (1000, 700000),
        result.transpose(1, 0, 2), field_grad.transpose(1, 0, 2),
        out_specs=(hbm(), hbm()),
    )
    return result.transpose(1, 0, 2), field_grad.transpose(1, 0, 2)


def solution(mesh):
    return jax.shard_map(
        on_device,
        mesh=mesh,
        in_specs=(
            P("lat", "lon", None),
            P(),
            P(None, "lat", None, None),
            P("lat"),
            P(),
            P(),
            P("lat", "lon", None),
        ),
        out_specs=(P("lat", "lon", None), P("lat", "lon", None)),
        check_vma=False,
    )
```

```python
import functools

import jax
import jax.numpy as jnp
from jax import lax
from jax.experimental import pallas as pl
from jax.experimental.pallas import tpu as pltpu
from jax.sharding import PartitionSpec as P

KB = 4
LREACH = 8
TAPS = 2 * LREACH + 1
BLOCK = 64
PITCH = BLOCK + 2 * LREACH
EDGE = 2 * LREACH
EDGE_PITCH = 2 * EDGE
LANES = 256
EDGE_LANES = 128
F32 = jnp.float32
BF16 = jnp.bfloat16
VMEM_BYTES = 48 * 1024 * 1024


def ceil_to(size, unit):
    return -(-size // unit) * unit


def vmem():
    return pl.BlockSpec(memory_space=pltpu.VMEM)


def hbm():
    return pl.BlockSpec(memory_space=pltpu.HBM)


def is_odd(axis):
    return lax.rem(lax.axis_index(axis), 2)


def call(kernel, outs, in_specs, scratch, cost, *args, out_specs=None):
    return pl.pallas_call(
        kernel,
        out_shape=outs,
        in_specs=in_specs,
        out_specs=out_specs or jax.tree.map(lambda _: vmem(), outs),
        scratch_shapes=scratch,
        compiler_params=pltpu.CompilerParams(vmem_limit_bytes=VMEM_BYTES),
        cost_estimate=pl.CostEstimate(flops=cost[0], bytes_accessed=cost[1], transcendentals=0),
    )(*args)


def swap(cells, axis, shift):
    count = lax.axis_size(axis)
    pairs = []
    for first in range(shift, count, 2):
        second = (first + 1) % count
        pairs += [(first, second), (second, first)]
    return lax.ppermute(cells, axis, pairs)


def swap_inner_lat(cells):
    count, around = lax.axis_size("lat"), lax.axis_size("lon")
    pairs = []
    for j in range(around):
        pairs += [(i * around + j, i * around + (j + around // 2) % around) for i in (0, count - 1)]
        for i in range(1, count - 1, 2):
            pairs += [(i * around + j, (i + 1) * around + j), ((i + 1) * around + j, i * around + j)]
    return lax.ppermute(cells, ("lat", "lon"), pairs)


def lat_picker(got_a, got_b):
    top_is_a = is_odd("lat") == 1
    index = lax.axis_index("lat")
    inner = (index > 0) & (index < lax.axis_size("lat") - 1)

    def pick(first, last, top):
        a, b = got_a[first:last, :], got_b[first:last, :]
        return jnp.where(top_is_a == top, a, jnp.where(inner, b, jnp.zeros_like(b)))

    return pick


def fetch(fields, cotangent, filters, reach, fields_here, cotangent_here, taps, filters_here, reach_here, raw, sems):
    copies = [
        pltpu.make_async_copy(src, dst, sems.at[n])
        for n, (src, dst) in enumerate(
            ((filters, filters_here), (reach, reach_here), (fields, fields_here), (cotangent, cotangent_here))
        )
    ]
    for copy in copies:
        copy.start()
    rows = taps.shape[0]
    raw[...] = jnp.zeros(raw.shape, F32)
    offset = jnp.abs(lax.broadcasted_iota(jnp.int32, (8 * KB, 128), 1) - LREACH)
    copies[0].wait()
    copies[1].wait()
    for k in range(KB):
        for a in range(3):
            line = filters_here[k, a].astype(F32)
            for r in range(rows):
                raw[r, 8 * k + a : 8 * k + a + 1, 0:TAPS] = line[r : r + 1]
    for r in range(rows):
        taps[r] = jnp.where(offset <= reach_here[r], raw[r], 0.0).astype(BF16)
    copies[2].wait()
    copies[3].wait()


def fill_lat(send, low, fields, cotangent, taps):
    rows, width, chans = fields.shape
    step = ceil_to(width, 16)
    send[0:width, :] = fields[low * (rows - 2)]
    send[step : step + width, :] = fields[low * (rows - 2) + 1]
    send[2 * step : 2 * step + width, :] = cotangent[low * (rows - 1)]
    own = taps[low * (rows - 1)]
    send[3 * step : 3 * step + 16, 0:128] = own[0:16]
    send[3 * step : 3 * step + 16, 128:256] = own[16:32]


def fill_lon(send_c, send_d, near, far):
    odd = is_odd("lon") == 1
    at = 0
    for first, last in zip(near, far, strict=True):
        size = first.shape[0]
        send_c[at : at + size, :] = jnp.where(odd, first, last)
        send_d[at : at + size, :] = jnp.where(odd, last, first)
        at += size


def pack_b(fields, cotangent, taps, send_b):
    fill_lat(send_b, is_odd("lat"), fields, cotangent, taps)


def pack_own(fields, cotangent, taps, send_a, send_c, send_d):
    rows, width, chans = fields.shape
    fill_lat(send_a, 1 - is_odd("lat"), fields, cotangent, taps)

    def edges(first, last, own):
        return jnp.concatenate([own[r, first:last, :].astype(F32) for r in range(rows)], axis=0).astype(BF16)

    near = edges(0, EDGE, fields), edges(0, LREACH, cotangent)
    far = edges(width - EDGE, width, fields), edges(width - LREACH, width, cotangent)
    fill_lon(send_c, send_d, near, far)


def pack_corners(width, got_a, got_b, send_c, send_d):
    step = (got_a.shape[0] - 16) // 3
    lat_rows = lat_picker(got_a, got_b)

    def edges(first, last, starts):
        parts = [lat_rows(at + first, at + last, top).astype(F32) for top in (True, False) for at in starts]
        return jnp.concatenate(parts, axis=0).astype(BF16)

    near = edges(0, EDGE, (0, step)), edges(0, LREACH, (2 * step,))
    far = edges(width - EDGE, width, (0, step)), edges(width - LREACH, width, (2 * step,))
    fill_lon(send_c, send_d, near, far)


def lay_taps(every, pitch, lanes):
    groups = every.shape[0] // 8

    def places(shape, dim):
        col = lax.broadcasted_iota(jnp.int32, shape, dim)
        turned = col >= lanes
        inner = jnp.where(turned, col - lanes, col)
        part = jnp.where(inner >= pitch, 1, 0) + jnp.where(inner >= 2 * pitch, 1, 0)
        return turned, inner - pitch * part, part

    turned, place, _ = places((128, 2 * lanes), 1)
    tap = lax.broadcasted_iota(jnp.int32, (128, 2 * lanes), 0)
    wanted = jnp.where(turned, 2 * LREACH - place, place)
    table = jnp.where((tap == wanted) & (tap < TAPS), 1.0, 0.0).astype(BF16)
    spread = jnp.dot(every, table, preferred_element_type=F32).reshape(groups, 8, 2 * lanes)
    turned, _, part = places((groups, 8, 2 * lanes), 2)
    lat_tap = lax.broadcasted_iota(jnp.int32, (groups, 8, 2 * lanes), 1)
    chosen = jnp.where(turned, 2 - part, part) == lat_tap
    return jnp.sum(jnp.where(chosen, spread, 0.0), axis=1)


def build_bands(every, forward, backward, size, pitch, lanes):
    lines = lay_taps(every, pitch, lanes)
    rows = every.shape[0] // (8 * KB) - 2
    lane = lax.broadcasted_iota(jnp.int32, (1, lanes), 1)

    def slant(line):
        return pltpu.roll(jnp.broadcast_to(line, (size, lanes)), 0, 1, stride=1, stride_axis=0).astype(BF16)

    for i in range(rows + 2):
        for k in range(KB):
            at = KB * i + k
            forward[i, size * k : size * (k + 1), :] = slant(lines[at : at + 1, 0:lanes])
    for i in range(rows):
        for k in range(KB):
            near = [lines[KB * (i + t) + k : KB * (i + t) + k + 1, lanes:] for t in range(3)]
            line = jnp.where(lane < pitch, near[0], jnp.where(lane < 2 * pitch, near[1], near[2]))
            backward[i, size * k : size * (k + 1), :] = slant(line)


def gelu_parts(pre):
    size = jnp.abs(pre)
    bell = jnp.exp(-0.5 * pre * pre)
    t = 1.0 / (1.0 + 0.23164188836 * size)
    poly = t * (0.127414796 + t * (-0.142248368 + t * (0.7107068705 + t * (-0.7265760135 + t * 0.5307027145))))
    tail = poly * bell
    cdf = jnp.where(pre >= 0.0, 1.0 - tail, tail)
    return pre * cdf, cdf + pre * bell * 0.3989422804014327


def contract_last(left, right):
    return lax.dot_general(left, right, (((1,), (1,)), ((), ())), preferred_element_type=F32)


def mlp(hidden, upstream, w_up, w_down, first, last):
    pre = jnp.dot(hidden[...], w_up[...], preferred_element_type=F32)
    active, slope = gelu_parts(pre)
    out = hidden[first:last, :].astype(F32) + jnp.dot(
        active[first:last].astype(BF16), w_down[...], preferred_element_type=F32
    )
    grad_active = (contract_last(upstream[...], w_down[...]) * slope).astype(BF16)
    return out, (upstream[...].astype(F32) + contract_last(grad_active, w_up[...])).astype(BF16)


def middle_kernel(
    fields, cotangent, taps, got_a, got_b, w_mix, w_up, w_down,
    result, field_grad, edge_grads, edge_forward, edge_backward,
    forward, backward, wide, narrow, basis, hidden, upstream, grads, grad_mixed,
):
    rows, width, chans = fields.shape
    step = ceil_to(width, 16)
    pick = lat_picker(got_a, got_b)
    ext = rows + 2
    rest = EDGE
    span = BLOCK + rest

    def lat_rows(at, size, top):
        return pick(at, at + size, top)

    def taps_of(top):
        both = lat_rows(3 * step, 16, top)
        return [both[:, 0:128], both[:, 128:256]]

    every = jnp.concatenate(taps_of(True) + [taps[r] for r in range(rows)] + taps_of(False), axis=0)
    build_bands(every, forward, backward, BLOCK, PITCH, LANES)
    build_bands(every, edge_forward, edge_backward, EDGE, EDGE_PITCH, EDGE_LANES)

    fill = PITCH + EDGE - width
    for i in range(rows + 4):
        if i < 2:
            line = lat_rows(step * i, width, True)
        elif i < rows + 2:
            line = fields[i - 2]
        else:
            line = lat_rows(step * (i - rows - 2), width, False)
        wide[PITCH * i : PITCH * (i + 1), :] = line[0:PITCH]
        tail = jnp.concatenate([line[BLOCK:].astype(F32), jnp.zeros((fill, chans), F32)], axis=0)
        narrow[EDGE_PITCH * i : EDGE_PITCH * (i + 1), :] = tail.astype(BF16)
    wide[PITCH * (rows + 4) :, :] = jnp.zeros((LANES - 3 * PITCH, chans), BF16)
    narrow[EDGE_PITCH * (rows + 4) :, :] = jnp.zeros((EDGE_LANES - 3 * EDGE_PITCH, chans), BF16)

    for i in range(ext):
        at = span * i
        moved = jnp.dot(forward[i], wide[PITCH * i : PITCH * i + LANES, :], preferred_element_type=F32).astype(BF16)
        other = jnp.dot(
            edge_forward[i], narrow[EDGE_PITCH * i : EDGE_PITCH * i + EDGE_LANES, :], preferred_element_type=F32
        ).astype(BF16)
        for k in range(KB):
            basis[at : at + BLOCK, chans * k : chans * (k + 1)] = moved[BLOCK * k : BLOCK * (k + 1)]
            basis[at + BLOCK : at + span, chans * k : chans * (k + 1)] = other[rest * k : rest * (k + 1)]
    stacked = jnp.concatenate([w_mix[:, chans * k : chans * (k + 1)] for k in range(KB)], axis=0)
    spatial = jnp.dot(basis[...], stacked, preferred_element_type=F32)
    for i in range(ext):
        at = PITCH * (i + 1)
        first = wide[at : at + PITCH, :].astype(F32)[LREACH : LREACH + BLOCK]
        at = EDGE_PITCH * (i + 1)
        second = narrow[at : at + EDGE_PITCH, :].astype(F32)[LREACH : LREACH + rest]
        here = span * i
        mine = jnp.concatenate([first, second], axis=0) + spatial[here : here + span]
        hidden[here : here + span, :] = mine.astype(BF16)
        if i == 0:
            up = lat_rows(2 * step, width, True)
        elif i < ext - 1:
            up = cotangent[i - 1]
        else:
            up = lat_rows(2 * step, width, False)
        upstream[here : here + span, :] = up.astype(F32)[LREACH : LREACH + span].astype(BF16)
    out, grad = mlp(hidden, upstream, w_up, w_down, span, span * (rows + 1))
    result[...] = jnp.swapaxes(out.reshape(rows, span, chans).astype(BF16), 0, 1)
    grads[0 : span * ext, :] = grad
    grads[span * ext :, :] = jnp.zeros((LANES - 3 * PITCH, chans), BF16)
    far = width - EDGE - 2 * LREACH
    for i in range(ext):
        mine = grad[span * i : span * (i + 1)]
        edge_grads[0, EDGE * i : EDGE * (i + 1), :] = mine[0:EDGE]
        edge_grads[1, EDGE * i : EDGE * (i + 1), :] = mine.astype(F32)[far : far + EDGE].astype(BF16)

    for i in range(rows):
        moved = jnp.dot(backward[i], grads[PITCH * i : PITCH * i + LANES, :], preferred_element_type=F32).astype(BF16)
        for k in range(KB):
            grad_mixed[BLOCK * i : BLOCK * (i + 1), chans * k : chans * (k + 1)] = moved[BLOCK * k : BLOCK * (k + 1)]
    back = contract_last(grad_mixed[...], w_mix[...])
    lines = []
    for i in range(rows):
        at = PITCH * (i + 1)
        own = grads[at : at + PITCH, :].astype(F32)[LREACH : LREACH + BLOCK]
        lines.append((own + back[BLOCK * i : BLOCK * (i + 1)]).astype(BF16))
    field_grad[...] = jnp.swapaxes(jnp.stack(lines), 0, 1)


def edge_kernel(
    middle_result, middle_grad, edge_grads, edge_forward, edge_backward,
    send_c, send_d, got_c, got_d, corner_send_c, corner_send_d, corner_got_c, corner_got_d, w_mix, w_up, w_down,
    result, field_grad, source, basis, hidden, upstream, grads, grad_mixed, result_edges, grad_edges, sems,
):
    width, rows, chans = result.shape
    ext = rows + 2
    copies = []

    def store(here, out, first, size):
        copies.append(pltpu.make_async_copy(here.at[pl.ds(0, size)], out.at[pl.ds(first, size)], sems.at[len(copies)]))
        copies[-1].start()

    store(middle_result, result, LREACH, width - 2 * LREACH)
    store(middle_grad, field_grad, EDGE, width - 2 * EDGE)
    left_is_c = is_odd("lon") == 1
    own = (send_c, send_d), (got_c, got_d)
    corners = (corner_send_c, corner_send_d), (corner_got_c, corner_got_d)

    def both_sides(at, arrays):
        (sent_c, sent_d), (came_c, came_d) = [[x[at : at + EDGE, :] for x in pair] for pair in arrays]
        left = jnp.where(left_is_c, came_c, came_d), jnp.where(left_is_c, sent_c, sent_d)
        right = jnp.where(left_is_c, sent_d, sent_c), jnp.where(left_is_c, came_d, came_c)
        return left, right

    for i in range(rows + 4):
        if 2 <= i < rows + 2:
            sides = both_sides(EDGE * (i - 2), own)
        else:
            sides = both_sides(EDGE * (i if i < 2 else i - rows), corners)
        at = EDGE_PITCH * i
        for part, (first, second) in enumerate(sides):
            source[at : at + EDGE, chans * part : chans * (part + 1)] = first
            source[at + EDGE : at + 2 * EDGE, chans * part : chans * (part + 1)] = second
    source[EDGE_PITCH * (rows + 4) :, :] = jnp.zeros((EDGE_LANES - 3 * EDGE_PITCH, 2 * chans), BF16)

    for i in range(ext):
        if 0 < i < ext - 1:
            sides = both_sides(EDGE * rows + EDGE * ((i - 1) // 2), own)
            inside = LREACH * ((i - 1) % 2)
        else:
            sides = both_sides(EDGE * 4, corners)
            inside = 0 if i == 0 else LREACH
        for part, halves in enumerate(sides):
            here = EDGE * (2 * i + part)
            whole = [x.astype(F32)[inside : inside + LREACH] for x in halves]
            upstream[here : here + EDGE, :] = jnp.concatenate(whole, axis=0).astype(BF16)

    def spread(band, cells, at, out):
        moved = jnp.dot(band, cells, preferred_element_type=F32).astype(BF16)
        for part in range(2):
            for k in range(KB):
                out[at + EDGE * part : at + EDGE * (part + 1), chans * k : chans * (k + 1)] = moved[
                    EDGE * k : EDGE * (k + 1), chans * part : chans * (part + 1)
                ]

    for i in range(ext):
        spread(edge_forward[i], source[EDGE_PITCH * i : EDGE_PITCH * i + EDGE_LANES, :], 2 * EDGE * i, basis)
    stacked = jnp.concatenate([w_mix[:, chans * k : chans * (k + 1)] for k in range(KB)], axis=0)
    spatial = jnp.dot(basis[...], stacked, preferred_element_type=F32)
    for i in range(ext):
        at = EDGE_PITCH * (i + 1)
        cells = source[at : at + EDGE_PITCH, :].astype(F32)[LREACH : LREACH + EDGE]
        for part in range(2):
            here = EDGE * (2 * i + part)
            hidden[here : here + EDGE, :] = (
                cells[:, chans * part : chans * (part + 1)] + spatial[here : here + EDGE]
            ).astype(BF16)
    out, grad = mlp(hidden, upstream, w_up, w_down, 2 * EDGE, 2 * EDGE * (rows + 1))
    for part in range(2):
        inside = 0 if part else LREACH
        lines = [out[at + inside : at + inside + LREACH] for at in (EDGE * (2 * i + part) for i in range(rows))]
        result_edges[part] = jnp.swapaxes(jnp.stack(lines), 0, 1).astype(BF16)
        store(result_edges.at[part], result, part * (width - LREACH), LREACH)

    for i in range(ext):
        at = EDGE_PITCH * i
        here = 2 * EDGE * i
        grads[at : at + EDGE, 0:chans] = grad[here : here + EDGE]
        grads[at + EDGE : at + 2 * EDGE, 0:chans] = edge_grads[0, EDGE * i : EDGE * (i + 1), :]
        grads[at : at + EDGE, chans:] = edge_grads[1, EDGE * i : EDGE * (i + 1), :]
        grads[at + EDGE : at + 2 * EDGE, chans:] = grad[here + EDGE : here + 2 * EDGE]
    grads[EDGE_PITCH * ext :, :] = jnp.zeros((EDGE_LANES - 3 * EDGE_PITCH, 2 * chans), BF16)
    for i in range(rows):
        spread(edge_backward[i], grads[EDGE_PITCH * i : EDGE_PITCH * i + EDGE_LANES, :], 2 * EDGE * i, grad_mixed)
    back = contract_last(grad_mixed[...], w_mix[...])
    for part in range(2):
        lines = []
        for i in range(rows):
            at = EDGE_PITCH * (i + 1)
            own = grads[at : at + EDGE_PITCH, chans * part : chans * (part + 1)].astype(F32)[LREACH : LREACH + EDGE]
            here = EDGE * (2 * i + part)
            lines.append(own + back[here : here + EDGE])
        grad_edges[part] = jnp.swapaxes(jnp.stack(lines), 0, 1).astype(BF16)
        store(grad_edges.at[part], field_grad, part * (width - EDGE), EDGE)
    for copy in copies:
        copy.wait()


def on_device(fields, w_mix, filters, reach, w_up, w_down, cotangent):
    rows, width, chans = fields.shape
    step = ceil_to(width, 16)
    ext = rows + 2
    span = BLOCK + EDGE
    pad = LANES - 3 * PITCH
    edge_pad = EDGE_LANES - 3 * EDGE_PITCH

    def shaped(*shape):
        return jax.ShapeDtypeStruct(shape, BF16)

    turned = shaped(width, rows, chans)
    fields_here, cotangent_here, taps = call(
        fetch,
        (turned, turned, shaped(rows, 8 * KB, 128)),
        [hbm()] * 4,
        [
            pltpu.VMEM((KB, 3, rows, TAPS), BF16),
            pltpu.SMEM((rows,), jnp.int32),
            pltpu.VMEM((rows, 8 * KB, 128), F32),
            pltpu.SemaphoreType.DMA((4,)),
        ],
        (1000, 1000000),
        *(
            pltpu.with_memory_space_constraint(x, pltpu.HBM)
            for x in (fields.transpose(1, 0, 2), cotangent.transpose(1, 0, 2), filters.transpose(0, 2, 1, 3), reach)
        ),
    )
    fields = fields_here.transpose(1, 0, 2)
    cotangent = cotangent_here.transpose(1, 0, 2)
    sent = shaped(3 * step + 16, chans)
    send_b = call(pack_b, sent, [vmem()] * 3, [], (1000, 1000000), fields, cotangent, taps)
    got_b = swap_inner_lat(send_b)
    edge = shaped((EDGE + LREACH) * rows, chans)
    send_a, send_c, send_d = call(
        pack_own, (sent, edge, edge), [vmem()] * 3, [], (2000000000, 5000000), fields, cotangent, taps
    )
    got_a = swap(send_a, "lat", 0)
    got_d = swap(send_d, "lon", 1)
    got_c = swap(send_c, "lon", 0)
    corner = shaped(4 * EDGE + 2 * LREACH, chans)
    corner_send_c, corner_send_d = call(
        functools.partial(pack_corners, width), (corner, corner), [vmem()] * 2, [], (1000, 1000000), got_a, got_b
    )
    corner_got_d = swap(corner_send_d, "lon", 1)
    corner_got_c = swap(corner_send_c, "lon", 0)
    middle_result, middle_grad, edge_grads, edge_forward, edge_backward = call(
        middle_kernel,
        (
            shaped(span, rows, chans),
            shaped(BLOCK, rows, chans),
            shaped(2, EDGE * ext, chans),
            shaped(ext, KB * EDGE, EDGE_LANES),
            shaped(rows, KB * EDGE, EDGE_LANES),
        ),
        [vmem()] * 8,
        [
            pltpu.VMEM((ext, KB * BLOCK, LANES), BF16),
            pltpu.VMEM((rows, KB * BLOCK, LANES), BF16),
            pltpu.VMEM((PITCH * (rows + 4) + pad, chans), BF16),
            pltpu.VMEM((EDGE_PITCH * (rows + 4) + edge_pad, chans), BF16),
            pltpu.VMEM((span * ext, KB * chans), BF16),
            pltpu.VMEM((span * ext, chans), BF16),
            pltpu.VMEM((span * ext, chans), BF16),
            pltpu.VMEM((span * ext + pad, chans), BF16),
            pltpu.VMEM((BLOCK * rows, KB * chans), BF16),
        ],
        (2000000000, 5000000),
        fields, cotangent, taps, got_a, got_b, w_mix, w_up, w_down,
    )
    result, field_grad = call(
        edge_kernel,
        (turned, turned),
        [vmem()] * 16,
        [
            pltpu.VMEM((EDGE_PITCH * (rows + 4) + edge_pad, 2 * chans), BF16),
            pltpu.VMEM((2 * EDGE * ext, KB * chans), BF16),
            pltpu.VMEM((2 * EDGE * ext, chans), BF16),
            pltpu.VMEM((2 * EDGE * ext, chans), BF16),
            pltpu.VMEM((EDGE_PITCH * ext + edge_pad, 2 * chans), BF16),
            pltpu.VMEM((2 * EDGE * rows, KB * chans), BF16),
            pltpu.VMEM((2, LREACH, rows, chans), BF16),
            pltpu.VMEM((2, EDGE, rows, chans), BF16),
            pltpu.SemaphoreType.DMA((6,)),
        ],
        (500000000, 3000000),
        middle_result, middle_grad, edge_grads, edge_forward, edge_backward,
        send_c, send_d, got_c, got_d, corner_send_c, corner_send_d, corner_got_c, corner_got_d, w_mix, w_up, w_down,
        out_specs=(hbm(), hbm()),
    )
    return result.transpose(1, 0, 2), field_grad.transpose(1, 0, 2)


def solution(mesh):
    return jax.shard_map(
        on_device,
        mesh=mesh,
        in_specs=(
            P("lat", "lon", None),
            P(),
            P(None, "lat", None, None),
            P("lat"),
            P(),
            P(),
            P("lat", "lon", None),
        ),
        out_specs=(P("lat", "lon", None), P("lat", "lon", None)),
        check_vma=False,
    )
```

```python
import functools

import jax
import jax.numpy as jnp
from jax import lax
from jax.experimental import pallas as pl
from jax.experimental.pallas import tpu as pltpu
from jax.sharding import PartitionSpec as P

KB = 4
LREACH = 8
TAPS = 2 * LREACH + 1
BLOCK = 64
PITCH = BLOCK + 2 * LREACH
EDGE = 2 * LREACH
EDGE_PITCH = 2 * EDGE
LANES = 256
EDGE_LANES = 128
F32 = jnp.float32
BF16 = jnp.bfloat16
VMEM_BYTES = 48 * 1024 * 1024


def ceil_to(size, unit):
    return -(-size // unit) * unit


def vmem():
    return pl.BlockSpec(memory_space=pltpu.VMEM)


def hbm():
    return pl.BlockSpec(memory_space=pltpu.HBM)


def is_odd(axis):
    return lax.rem(lax.axis_index(axis), 2)


def call(kernel, outs, in_specs, scratch, cost, *args, out_specs=None):
    return pl.pallas_call(
        kernel,
        out_shape=outs,
        in_specs=in_specs,
        out_specs=out_specs or jax.tree.map(lambda _: vmem(), outs),
        scratch_shapes=scratch,
        compiler_params=pltpu.CompilerParams(vmem_limit_bytes=VMEM_BYTES),
        cost_estimate=pl.CostEstimate(flops=cost[0], bytes_accessed=cost[1], transcendentals=0),
    )(*args)


def swap(cells, axis, shift):
    count = lax.axis_size(axis)
    pairs = []
    for first in range(shift, count, 2):
        second = (first + 1) % count
        pairs += [(first, second), (second, first)]
    return lax.ppermute(cells, axis, pairs)


def swap_inner_lat(cells):
    count, around = lax.axis_size("lat"), lax.axis_size("lon")
    pairs = []
    for j in range(around):
        pairs += [(i * around + j, i * around + (j + around // 2) % around) for i in (0, count - 1)]
        for i in range(1, count - 1, 2):
            pairs += [(i * around + j, (i + 1) * around + j), ((i + 1) * around + j, i * around + j)]
    return lax.ppermute(cells, ("lat", "lon"), pairs)


def lat_picker(got_a, got_b):
    top_is_a = is_odd("lat") == 1
    index = lax.axis_index("lat")
    inner = (index > 0) & (index < lax.axis_size("lat") - 1)

    def pick(first, last, top):
        a, b = got_a[first:last, :], got_b[first:last, :]
        return jnp.where(top_is_a == top, a, jnp.where(inner, b, jnp.zeros_like(b)))

    return pick


def fetch(fields, cotangent, filters, reach, fields_here, cotangent_here, taps, filters_here, reach_here, raw, sems):
    copies = [
        pltpu.make_async_copy(src, dst, sems.at[n])
        for n, (src, dst) in enumerate(
            ((filters, filters_here), (reach, reach_here), (fields, fields_here), (cotangent, cotangent_here))
        )
    ]
    for copy in copies:
        copy.start()
    rows = taps.shape[0]
    raw[...] = jnp.zeros(raw.shape, F32)
    offset = jnp.abs(lax.broadcasted_iota(jnp.int32, (8 * KB, 128), 1) - LREACH)
    copies[0].wait()
    copies[1].wait()
    for k in range(KB):
        for a in range(3):
            line = filters_here[k, a].astype(F32)
            for r in range(rows):
                raw[r, 8 * k + a : 8 * k + a + 1, 0:TAPS] = line[r : r + 1]
    for r in range(rows):
        taps[r] = jnp.where(offset <= reach_here[r], raw[r], 0.0).astype(BF16)
    copies[2].wait()
    copies[3].wait()


def fill_lat(send, low, fields, cotangent, taps):
    rows, width, chans = fields.shape
    step = ceil_to(width, 16)
    send[0:width, :] = fields[low * (rows - 2)]
    send[step : step + width, :] = fields[low * (rows - 2) + 1]
    send[2 * step : 2 * step + width, :] = cotangent[low * (rows - 1)]
    own = taps[low * (rows - 1)]
    send[3 * step : 3 * step + 16, 0:128] = own[0:16]
    send[3 * step : 3 * step + 16, 128:256] = own[16:32]


def fill_lon(send_c, send_d, near, far):
    odd = is_odd("lon") == 1
    at = 0
    for first, last in zip(near, far, strict=True):
        size = first.shape[0]
        send_c[at : at + size, :] = jnp.where(odd, first, last)
        send_d[at : at + size, :] = jnp.where(odd, last, first)
        at += size


def pack_lat(fields, cotangent, taps, sent, send_a, send_b):
    odd = is_odd("lat")
    fill_lat(send_a, 1 - odd, fields, cotangent, taps)
    fill_lat(send_b, odd, fields, cotangent, taps)


def pack_own(fields, cotangent, send_c, send_d):
    rows, width, chans = fields.shape

    def edges(first, last, own):
        return jnp.concatenate([own[r, first:last, :].astype(F32) for r in range(rows)], axis=0).astype(BF16)

    near = edges(0, EDGE, fields), edges(0, LREACH, cotangent)
    far = edges(width - EDGE, width, fields), edges(width - LREACH, width, cotangent)
    fill_lon(send_c, send_d, near, far)


def pack_corners(rows, got_c, got_d, inner, send_a, send_b):
    odd = is_odd("lat")
    left_is_c = is_odd("lon") == 1
    for send, low in ((send_a, 1 - odd), (send_b, odd)):
        at = pl.multiple_of(low * (rows - 2) * EDGE, EDGE)
        c, d = got_c[pl.ds(at, 2 * EDGE), :], got_d[pl.ds(at, 2 * EDGE), :]
        send[0 : 2 * EDGE, :] = jnp.where(left_is_c, c, d)
        send[2 * EDGE : 4 * EDGE, :] = jnp.where(left_is_c, d, c)
        first, last = EDGE * rows, (EDGE + LREACH) * rows
        c, d = [
            jnp.where(low == 1, x[last - EDGE : last, :].astype(F32)[LREACH:], x[first : first + EDGE, :].astype(F32)[0:LREACH])
            for x in (got_c, got_d)
        ]
        both = [jnp.where(left_is_c, c, d), jnp.where(left_is_c, d, c)]
        send[4 * EDGE : 5 * EDGE, :] = jnp.concatenate(both, axis=0).astype(BF16)


def lay_taps(every, pitch, lanes):
    groups = every.shape[0] // 8

    def places(shape, dim):
        col = lax.broadcasted_iota(jnp.int32, shape, dim)
        turned = col >= lanes
        inner = jnp.where(turned, col - lanes, col)
        part = jnp.where(inner >= pitch, 1, 0) + jnp.where(inner >= 2 * pitch, 1, 0)
        return turned, inner - pitch * part, part

    turned, place, _ = places((128, 2 * lanes), 1)
    tap = lax.broadcasted_iota(jnp.int32, (128, 2 * lanes), 0)
    wanted = jnp.where(turned, 2 * LREACH - place, place)
    table = jnp.where((tap == wanted) & (tap < TAPS), 1.0, 0.0).astype(BF16)
    spread = jnp.dot(every, table, preferred_element_type=F32).reshape(groups, 8, 2 * lanes)
    turned, _, part = places((groups, 8, 2 * lanes), 2)
    lat_tap = lax.broadcasted_iota(jnp.int32, (groups, 8, 2 * lanes), 1)
    chosen = jnp.where(turned, 2 - part, part) == lat_tap
    return jnp.sum(jnp.where(chosen, spread, 0.0), axis=1)


def slant(line, size):
    lanes = line.shape[1]
    return pltpu.roll(jnp.broadcast_to(line, (size, lanes)), 0, 1, stride=1, stride_axis=0).astype(BF16)


def build_bands(every, size, pitch, lanes, forward, forward_rows, backward, backward_rows):
    lines = lay_taps(every, pitch, lanes)
    lane = lax.broadcasted_iota(jnp.int32, (1, lanes), 1)
    for place, i in enumerate(forward_rows):
        for k in range(KB):
            at = KB * i + k
            forward[place, size * k : size * (k + 1), :] = slant(lines[at : at + 1, 0:lanes], size)
    for place, i in enumerate(backward_rows):
        for k in range(KB):
            near = [lines[KB * (i + t - 1) + k : KB * (i + t - 1) + k + 1, lanes:] for t in range(3)]
            line = jnp.where(lane < pitch, near[0], jnp.where(lane < 2 * pitch, near[1], near[2]))
            backward[place, size * k : size * (k + 1), :] = slant(line, size)


def gelu_parts(pre):
    size = jnp.abs(pre)
    bell = jnp.exp(-0.5 * pre * pre)
    t = 1.0 / (1.0 + 0.23164188836 * size)
    poly = t * (0.127414796 + t * (-0.142248368 + t * (0.7107068705 + t * (-0.7265760135 + t * 0.5307027145))))
    tail = poly * bell
    cdf = jnp.where(pre >= 0.0, 1.0 - tail, tail)
    return pre * cdf, cdf + pre * bell * 0.3989422804014327


def contract_last(left, right):
    return lax.dot_general(left, right, (((1,), (1,)), ((), ())), preferred_element_type=F32)


def mlp(hidden, upstream, w_up, w_down, first, last):
    pre = jnp.dot(hidden[...], w_up[...], preferred_element_type=F32)
    active, slope = gelu_parts(pre)
    out = hidden[first:last, :].astype(F32) + jnp.dot(
        active[first:last].astype(BF16), w_down[...], preferred_element_type=F32
    )
    grad_active = (contract_last(upstream[...], w_down[...]) * slope).astype(BF16)
    return out, (upstream[...].astype(F32) + contract_last(grad_active, w_up[...])).astype(BF16)


SPAN = BLOCK + EDGE


def middle_rows(lines, cotangents, bands, edge_bands, firsts, w_mix, w_up, w_down, out_rows, scratch):
    wide, narrow, basis, hidden, upstream = scratch
    chans = w_up.shape[0]
    width = lines[0].shape[0]
    fill = PITCH + EDGE - width
    for f, line in enumerate(lines):
        wide[PITCH * f : PITCH * (f + 1), :] = line[0:PITCH]
        tail = jnp.concatenate([line[BLOCK:].astype(F32), jnp.zeros((fill, chans), F32)], axis=0)
        narrow[EDGE_PITCH * f : EDGE_PITCH * (f + 1), :] = tail.astype(BF16)
    wide[PITCH * len(lines) :, :] = jnp.zeros((LANES - 3 * PITCH, chans), BF16)
    narrow[EDGE_PITCH * len(lines) :, :] = jnp.zeros((EDGE_LANES - 3 * EDGE_PITCH, chans), BF16)
    for n, f in enumerate(firsts):
        at = SPAN * n
        moved = jnp.dot(bands[n], wide[PITCH * f : PITCH * f + LANES, :], preferred_element_type=F32).astype(BF16)
        other = jnp.dot(
            edge_bands[n], narrow[EDGE_PITCH * f : EDGE_PITCH * f + EDGE_LANES, :], preferred_element_type=F32
        ).astype(BF16)
        for k in range(KB):
            basis[at : at + BLOCK, chans * k : chans * (k + 1)] = moved[BLOCK * k : BLOCK * (k + 1)]
            basis[at + BLOCK : at + SPAN, chans * k : chans * (k + 1)] = other[EDGE * k : EDGE * (k + 1)]
    stacked = jnp.concatenate([w_mix[:, chans * k : chans * (k + 1)] for k in range(KB)], axis=0)
    spatial = jnp.dot(basis[...], stacked, preferred_element_type=F32)
    for n, f in enumerate(firsts):
        at = PITCH * (f + 1)
        first = wide[at : at + PITCH, :].astype(F32)[LREACH : LREACH + BLOCK]
        at = EDGE_PITCH * (f + 1)
        second = narrow[at : at + EDGE_PITCH, :].astype(F32)[LREACH : LREACH + EDGE]
        here = SPAN * n
        mine = jnp.concatenate([first, second], axis=0) + spatial[here : here + SPAN]
        hidden[here : here + SPAN, :] = mine.astype(BF16)
        upstream[here : here + SPAN, :] = cotangents[n].astype(F32)[LREACH : LREACH + SPAN].astype(BF16)
    return mlp(hidden, upstream, w_up, w_down, SPAN * out_rows[0], SPAN * out_rows[1])


def inner_kernel(
    fields, cotangent, taps, w_mix, w_up, w_down, sent,
    result, grads, forward, backward, edge_forward, edge_backward, *scratch,
):
    rows = fields.shape[0]
    every = jnp.concatenate([taps[r] for r in range(rows)], axis=0)
    own, inner = range(rows), range(1, rows - 1)
    build_bands(every, BLOCK, PITCH, LANES, forward, own, backward, inner)
    build_bands(every, EDGE, EDGE_PITCH, EDGE_LANES, edge_forward, own, edge_backward, inner)
    out, grad = middle_rows(
        [fields[r] for r in own],
        [cotangent[r] for r in inner],
        [forward[r] for r in inner],
        [edge_forward[r] for r in inner],
        [r - 1 for r in inner],
        w_mix, w_up, w_down, (0, rows - 2), scratch,
    )
    result[...] = out.reshape(result.shape).astype(BF16)
    grads[...] = grad


def middle_kernel(
    got_a, got_b, fields, cotangent, taps, inner_result, inner_grads, inner_forward, inner_backward,
    inner_edge_forward, w_mix, w_up, w_down,
    result, field_grad, edge_grads, edge_forward, edge_backward, halo,
    forward, backward, grads, grad_mixed, *scratch,
):
    rows, width, chans = fields.shape
    step = ceil_to(width, 16)
    pick = lat_picker(got_a, got_b)
    ext = rows + 2

    def taps_of(top):
        both = pick(3 * step, 3 * step + 16, top)
        return [both[:, 0:128], both[:, 128:256]]

    for part, (fields_at, cotangent_at) in enumerate(((0, 0), (width - EDGE, width - LREACH))):
        cells = [
            pick(step * n, step * n + width, top).astype(F32)[fields_at : fields_at + EDGE]
            for top in (True, False)
            for n in range(2)
        ]
        cells += [
            pick(2 * step, 2 * step + width, top).astype(F32)[cotangent_at : cotangent_at + LREACH] for top in (True, False)
        ]
        halo[part] = jnp.concatenate(cells, axis=0).astype(BF16)

    every = jnp.concatenate(taps_of(True) + [taps[r] for r in range(rows)] + taps_of(False), axis=0)
    ends = (0, ext - 1), (1, rows)
    build_bands(every, BLOCK, PITCH, LANES, forward, ends[0], backward, ends[1])
    build_bands(every, EDGE, EDGE_PITCH, EDGE_LANES, edge_forward, ends[0], edge_backward, ends[1])

    lines = [pick(step * n, step * n + width, True) for n in range(2)]
    lines += [fields[r] for r in range(rows)]
    lines += [pick(step * n, step * n + width, False) for n in range(2)]
    out, grad = middle_rows(
        lines,
        [pick(2 * step, 2 * step + width, True), cotangent[0], cotangent[rows - 1], pick(2 * step, 2 * step + width, False)],
        [forward[0], inner_forward[0], inner_forward[rows - 1], forward[1]],
        [edge_forward[0], inner_edge_forward[0], inner_edge_forward[rows - 1], edge_forward[1]],
        [0, 1, ext - 2, ext - 1],
        w_mix, w_up, w_down, (1, 3), scratch,
    )
    lines = [out[0:SPAN].astype(BF16)] + [inner_result[r] for r in range(rows - 2)] + [out[SPAN:].astype(BF16)]
    result[...] = jnp.swapaxes(jnp.stack(lines), 0, 1)
    grads[0 : 2 * SPAN, :] = grad[0 : 2 * SPAN]
    grads[2 * SPAN : (ext - 2) * SPAN, :] = inner_grads[...]
    grads[(ext - 2) * SPAN : ext * SPAN, :] = grad[2 * SPAN :]
    grads[SPAN * ext :, :] = jnp.zeros((LANES - 3 * PITCH, chans), BF16)
    far = width - EDGE - 2 * LREACH
    for i in range(ext):
        mine = grads[SPAN * i : SPAN * (i + 1), :]
        edge_grads[0, EDGE * i : EDGE * (i + 1), :] = mine[0:EDGE]
        edge_grads[1, EDGE * i : EDGE * (i + 1), :] = mine.astype(F32)[far : far + EDGE].astype(BF16)

    bands = [backward[0]] + [inner_backward[r] for r in range(rows - 2)] + [backward[1]]
    for i in range(rows):
        moved = jnp.dot(bands[i], grads[PITCH * i : PITCH * i + LANES, :], preferred_element_type=F32).astype(BF16)
        for k in range(KB):
            grad_mixed[BLOCK * i : BLOCK * (i + 1), chans * k : chans * (k + 1)] = moved[BLOCK * k : BLOCK * (k + 1)]
    back = contract_last(grad_mixed[...], w_mix[...])
    lines = []
    for i in range(rows):
        at = PITCH * (i + 1)
        own = grads[at : at + PITCH, :].astype(F32)[LREACH : LREACH + BLOCK]
        lines.append((own + back[BLOCK * i : BLOCK * (i + 1)]).astype(BF16))
    field_grad[...] = jnp.swapaxes(jnp.stack(lines), 0, 1)


def edge_kernel(
    middle_result, middle_grad, edge_grads, inner_edge_forward, inner_edge_backward, end_edge_forward, end_edge_backward,
    halo, send_c, send_d, got_c, got_d, corner_a, corner_b, w_mix, w_up, w_down,
    result, field_grad, source, basis, hidden, upstream, grads, grad_mixed, result_edges, grad_edges, sems,
):
    width, rows, chans = result.shape
    ext = rows + 2
    copies = []

    def store(here, out, first, size):
        copies.append(pltpu.make_async_copy(here.at[pl.ds(0, size)], out.at[pl.ds(first, size)], sems.at[len(copies)]))
        copies[-1].start()

    store(middle_result, result, LREACH, width - 2 * LREACH)
    store(middle_grad, field_grad, EDGE, width - 2 * EDGE)
    left_is_c = is_odd("lon") == 1
    edge_forward = [end_edge_forward[0]] + [inner_edge_forward[r] for r in range(rows)] + [end_edge_forward[1]]
    edge_backward = [end_edge_backward[0]] + [inner_edge_backward[r] for r in range(rows - 2)] + [end_edge_backward[1]]
    pick = lat_picker(corner_a, corner_b)

    def own_cells(at):
        sent_c, sent_d, came_c, came_d = [x[at : at + EDGE, :] for x in (send_c, send_d, got_c, got_d)]
        return (
            jnp.where(left_is_c, came_c, came_d),
            jnp.where(left_is_c, sent_c, sent_d),
            jnp.where(left_is_c, sent_d, sent_c),
            jnp.where(left_is_c, came_d, came_c),
        )

    for i in range(rows + 4):
        if 2 <= i < rows + 2:
            cells = own_cells(EDGE * (i - 2))
        else:
            top = i < 2
            n = i if top else i - rows - 2
            at = EDGE * (i if top else i - rows)
            left, right = [pick(EDGE * m, EDGE * (m + 1), top) for m in (n, n + 2)]
            cells = left, halo[0, at : at + EDGE, :], halo[1, at : at + EDGE, :], right
        at = EDGE_PITCH * i
        source[at : at + EDGE, 0:chans] = cells[0]
        source[at + EDGE : at + 2 * EDGE, 0:chans] = cells[1]
        source[at : at + EDGE, chans:] = cells[2]
        source[at + EDGE : at + 2 * EDGE, chans:] = cells[3]
    source[EDGE_PITCH * (rows + 4) :, :] = jnp.zeros((EDGE_LANES - 3 * EDGE_PITCH, 2 * chans), BF16)

    for i in range(ext):
        if 0 < i < ext - 1:
            inside = LREACH * ((i - 1) % 2)
            cells = own_cells(EDGE * rows + EDGE * ((i - 1) // 2))
            cells = [x.astype(F32)[inside : inside + LREACH] for x in cells]
        else:
            inside = 0 if i == 0 else LREACH
            near, far = [halo[part, 4 * EDGE : 5 * EDGE, :].astype(F32)[inside : inside + LREACH] for part in range(2)]
            both = pick(4 * EDGE, 5 * EDGE, i == 0).astype(F32)
            cells = both[0:LREACH], near, far, both[LREACH:]
        here = 2 * EDGE * i
        upstream[here : here + EDGE, :] = jnp.concatenate(cells[0:2], axis=0).astype(BF16)
        upstream[here + EDGE : here + 2 * EDGE, :] = jnp.concatenate(cells[2:4], axis=0).astype(BF16)

    def spread(band, cells, at, out):
        moved = jnp.dot(band, cells, preferred_element_type=F32).astype(BF16)
        for part in range(2):
            for k in range(KB):
                out[at + EDGE * part : at + EDGE * (part + 1), chans * k : chans * (k + 1)] = moved[
                    EDGE * k : EDGE * (k + 1), chans * part : chans * (part + 1)
                ]

    for i in range(ext):
        spread(edge_forward[i], source[EDGE_PITCH * i : EDGE_PITCH * i + EDGE_LANES, :], 2 * EDGE * i, basis)
    stacked = jnp.concatenate([w_mix[:, chans * k : chans * (k + 1)] for k in range(KB)], axis=0)
    spatial = jnp.dot(basis[...], stacked, preferred_element_type=F32)
    for i in range(ext):
        at = EDGE_PITCH * (i + 1)
        cells = source[at : at + EDGE_PITCH, :].astype(F32)[LREACH : LREACH + EDGE]
        for part in range(2):
            here = EDGE * (2 * i + part)
            hidden[here : here + EDGE, :] = (
                cells[:, chans * part : chans * (part + 1)] + spatial[here : here + EDGE]
            ).astype(BF16)
    out, grad = mlp(hidden, upstream, w_up, w_down, 2 * EDGE, 2 * EDGE * (rows + 1))
    for part in range(2):
        inside = 0 if part else LREACH
        lines = [out[at + inside : at + inside + LREACH] for at in (EDGE * (2 * i + part) for i in range(rows))]
        result_edges[part] = jnp.swapaxes(jnp.stack(lines), 0, 1).astype(BF16)
        store(result_edges.at[part], result, part * (width - LREACH), LREACH)

    for i in range(ext):
        at = EDGE_PITCH * i
        here = 2 * EDGE * i
        grads[at : at + EDGE, 0:chans] = grad[here : here + EDGE]
        grads[at + EDGE : at + 2 * EDGE, 0:chans] = edge_grads[0, EDGE * i : EDGE * (i + 1), :]
        grads[at : at + EDGE, chans:] = edge_grads[1, EDGE * i : EDGE * (i + 1), :]
        grads[at + EDGE : at + 2 * EDGE, chans:] = grad[here + EDGE : here + 2 * EDGE]
    grads[EDGE_PITCH * ext :, :] = jnp.zeros((EDGE_LANES - 3 * EDGE_PITCH, 2 * chans), BF16)
    for i in range(rows):
        spread(edge_backward[i], grads[EDGE_PITCH * i : EDGE_PITCH * i + EDGE_LANES, :], 2 * EDGE * i, grad_mixed)
    back = contract_last(grad_mixed[...], w_mix[...])
    for part in range(2):
        lines = []
        for i in range(rows):
            at = EDGE_PITCH * (i + 1)
            own = grads[at : at + EDGE_PITCH, chans * part : chans * (part + 1)].astype(F32)[LREACH : LREACH + EDGE]
            here = EDGE * (2 * i + part)
            lines.append(own + back[here : here + EDGE])
        grad_edges[part] = jnp.swapaxes(jnp.stack(lines), 0, 1).astype(BF16)
        store(grad_edges.at[part], field_grad, part * (width - EDGE), EDGE)
    for copy in copies:
        copy.wait()


def on_device(fields, w_mix, filters, reach, w_up, w_down, cotangent):
    rows, width, chans = fields.shape
    step = ceil_to(width, 16)
    ext = rows + 2
    pad = LANES - 3 * PITCH
    edge_pad = EDGE_LANES - 3 * EDGE_PITCH

    def shaped(*shape):
        return jax.ShapeDtypeStruct(shape, BF16)

    turned = shaped(width, rows, chans)
    fields_here, cotangent_here, taps = call(
        fetch,
        (turned, turned, shaped(rows, 8 * KB, 128)),
        [hbm()] * 4,
        [
            pltpu.VMEM((KB, 3, rows, TAPS), BF16),
            pltpu.SMEM((rows,), jnp.int32),
            pltpu.VMEM((rows, 8 * KB, 128), F32),
            pltpu.SemaphoreType.DMA((4,)),
        ],
        (1000, 1000000),
        *(
            pltpu.with_memory_space_constraint(x, pltpu.HBM)
            for x in (fields.transpose(1, 0, 2), cotangent.transpose(1, 0, 2), filters.transpose(0, 2, 1, 3), reach)
        ),
    )
    fields = fields_here.transpose(1, 0, 2)
    cotangent = cotangent_here.transpose(1, 0, 2)
    sent = shaped(3 * step + 16, chans)
    edge = shaped((EDGE + LREACH) * rows, chans)
    send_c, send_d = call(pack_own, (edge, edge), [vmem()] * 2, [], (1000, 1000000), fields, cotangent)
    got_c = swap(send_c, "lon", 0)
    got_d = swap(send_d, "lon", 1)
    send_a, send_b = call(
        pack_lat,
        (sent, sent),
        [vmem()] * 3 + [pl.BlockSpec(memory_space=pl.ANY)],
        [],
        (2000000000, 5000000),
        fields, cotangent, taps, send_c,
    )
    got_a = swap(send_a, "lat", 0)
    got_b = swap_inner_lat(send_b)

    def scratch(lines, out_lines):
        return [
            pltpu.VMEM((PITCH * lines + pad, chans), BF16),
            pltpu.VMEM((EDGE_PITCH * lines + edge_pad, chans), BF16),
            pltpu.VMEM((SPAN * out_lines, KB * chans), BF16),
            pltpu.VMEM((SPAN * out_lines, chans), BF16),
            pltpu.VMEM((SPAN * out_lines, chans), BF16),
        ]

    def bands(count):
        return shaped(count, KB * BLOCK, LANES)

    def edge_bands(count):
        return shaped(count, KB * EDGE, EDGE_LANES)

    inner_result, inner_grads, inner_forward, inner_backward, inner_edge_forward, inner_edge_backward = call(
        inner_kernel,
        (
            shaped(rows - 2, SPAN, chans),
            shaped(SPAN * (rows - 2), chans),
            bands(rows),
            bands(rows - 2),
            edge_bands(rows),
            edge_bands(rows - 2),
        ),
        [vmem()] * 6 + [pl.BlockSpec(memory_space=pl.ANY)],
        scratch(rows, rows - 2),
        (300000000, 1000000),
        fields, cotangent, taps, w_mix, w_up, w_down, send_b,
    )
    corner = shaped(5 * EDGE, chans)
    corner_a, corner_b = call(
        functools.partial(pack_corners, rows),
        (corner, corner),
        [vmem()] * 2 + [pl.BlockSpec(memory_space=pl.ANY)],
        [],
        (4000000000, 1000000),
        got_c, got_d, inner_result,
    )
    corner_a = swap(corner_a, "lat", 0)
    corner_b = swap_inner_lat(corner_b)
    middle_result, middle_grad, edge_grads, edge_forward, edge_backward, halo = call(
        middle_kernel,
        (
            shaped(SPAN, rows, chans),
            shaped(BLOCK, rows, chans),
            shaped(2, EDGE * ext, chans),
            edge_bands(2),
            edge_bands(2),
            shaped(2, 5 * EDGE, chans),
        ),
        [vmem()] * 13,
        [
            pltpu.VMEM((2, KB * BLOCK, LANES), BF16),
            pltpu.VMEM((2, KB * BLOCK, LANES), BF16),
            pltpu.VMEM((SPAN * ext + pad, chans), BF16),
            pltpu.VMEM((BLOCK * rows, KB * chans), BF16),
        ]
        + scratch(rows + 4, 4),
        (2000000000, 5000000),
        got_a, got_b, fields, cotangent, taps, inner_result, inner_grads, inner_forward, inner_backward,
        inner_edge_forward, w_mix, w_up, w_down,
    )
    result, field_grad = call(
        edge_kernel,
        (turned, turned),
        [vmem()] * 17,
        [
            pltpu.VMEM((EDGE_PITCH * (rows + 4) + edge_pad, 2 * chans), BF16),
            pltpu.VMEM((2 * EDGE * ext, KB * chans), BF16),
            pltpu.VMEM((2 * EDGE * ext, chans), BF16),
            pltpu.VMEM((2 * EDGE * ext, chans), BF16),
            pltpu.VMEM((EDGE_PITCH * ext + edge_pad, 2 * chans), BF16),
            pltpu.VMEM((2 * EDGE * rows, KB * chans), BF16),
            pltpu.VMEM((2, LREACH, rows, chans), BF16),
            pltpu.VMEM((2, EDGE, rows, chans), BF16),
            pltpu.SemaphoreType.DMA((6,)),
        ],
        (500000000, 3000000),
        middle_result, middle_grad, edge_grads, inner_edge_forward, inner_edge_backward, edge_forward, edge_backward,
        halo, send_c, send_d, got_c, got_d, corner_a, corner_b, w_mix, w_up, w_down,
        out_specs=(hbm(), hbm()),
    )
    return result.transpose(1, 0, 2), field_grad.transpose(1, 0, 2)


def solution(mesh):
    return jax.shard_map(
        on_device,
        mesh=mesh,
        in_specs=(
            P("lat", "lon", None),
            P(),
            P(None, "lat", None, None),
            P("lat"),
            P(),
            P(),
            P("lat", "lon", None),
        ),
        out_specs=(P("lat", "lon", None), P("lat", "lon", None)),
        check_vma=False,
    )
```

```python
import functools

import jax
import jax.numpy as jnp
from jax import lax
from jax.experimental import pallas as pl
from jax.experimental.pallas import tpu as pltpu
from jax.sharding import PartitionSpec as P

KB = 4
LREACH = 8
TAPS = 2 * LREACH + 1
BLOCK = 64
PITCH = BLOCK + 2 * LREACH
EDGE = 2 * LREACH
EDGE_PITCH = 2 * EDGE
LANES = 256
EDGE_LANES = 128
F32 = jnp.float32
BF16 = jnp.bfloat16
VMEM_BYTES = 48 * 1024 * 1024


def ceil_to(size, unit):
    return -(-size // unit) * unit


def vmem():
    return pl.BlockSpec(memory_space=pltpu.VMEM)


def hbm():
    return pl.BlockSpec(memory_space=pltpu.HBM)


def is_odd(axis):
    return lax.rem(lax.axis_index(axis), 2)


def call(kernel, outs, in_specs, scratch, cost, *args, out_specs=None):
    return pl.pallas_call(
        kernel,
        out_shape=outs,
        in_specs=in_specs,
        out_specs=out_specs or jax.tree.map(lambda _: vmem(), outs),
        scratch_shapes=scratch,
        compiler_params=pltpu.CompilerParams(vmem_limit_bytes=VMEM_BYTES),
        cost_estimate=pl.CostEstimate(flops=cost[0], bytes_accessed=cost[1], transcendentals=0),
    )(*args)


def swap(cells, axis, shift):
    count = lax.axis_size(axis)
    pairs = []
    for first in range(shift, count, 2):
        second = (first + 1) % count
        pairs += [(first, second), (second, first)]
    return lax.ppermute(cells, axis, pairs)


def swap_inner_lat(cells):
    count, around = lax.axis_size("lat"), lax.axis_size("lon")
    pairs = []
    for j in range(around):
        pairs += [(i * around + j, i * around + (j + around // 2) % around) for i in (0, count - 1)]
        for i in range(1, count - 1, 2):
            pairs += [(i * around + j, (i + 1) * around + j), ((i + 1) * around + j, i * around + j)]
    return lax.ppermute(cells, ("lat", "lon"), pairs)


def lat_picker(got_a, got_b):
    top_is_a = is_odd("lat") == 1
    index = lax.axis_index("lat")
    inner = (index > 0) & (index < lax.axis_size("lat") - 1)

    def pick(first, last, top):
        a, b = got_a[first:last, :], got_b[first:last, :]
        return jnp.where(top_is_a == top, a, jnp.where(inner, b, jnp.zeros_like(b)))

    return pick


def fetch(fields, cotangent, filters, reach, send_c, send_d, taps, fields_here, cotangent_here, filters_here, reach_here, raw, sems):
    width, rows, chans = fields.shape
    moves = [(filters, filters_here), (reach, reach_here)]
    for part in range(2):
        moves.append((fields.at[pl.ds(part * (width - EDGE), EDGE)], fields_here.at[part]))
        moves.append((cotangent.at[pl.ds(part * (width - LREACH), LREACH)], cotangent_here.at[part]))
    copies = [pltpu.make_async_copy(src, dst, sems.at[n]) for n, (src, dst) in enumerate(moves)]
    for copy in copies:
        copy.start()
    raw[...] = jnp.zeros(raw.shape, F32)
    offset = jnp.abs(lax.broadcasted_iota(jnp.int32, (8 * KB, 128), 1) - LREACH)
    copies[0].wait()
    copies[1].wait()
    for k in range(KB):
        for a in range(3):
            line = filters_here[k, a].astype(F32)
            for r in range(rows):
                raw[r, 8 * k + a : 8 * k + a + 1, 0:TAPS] = line[r : r + 1]
    for r in range(rows):
        taps[r] = jnp.where(offset <= reach_here[r], raw[r], 0.0).astype(BF16)
    for copy in copies[2:]:
        copy.wait()
    sides = []
    for part in range(2):
        cells = jnp.swapaxes(fields_here[part], 0, 1).reshape(EDGE * rows, chans)
        grads = jnp.swapaxes(cotangent_here[part].astype(F32), 0, 1).reshape(LREACH * rows, chans).astype(BF16)
        sides.append((cells, grads))
    fill_lon(send_c, send_d, *sides)


def fill_lat(send, low, fields, cotangent, taps):
    rows, width, chans = fields.shape
    step = ceil_to(width, 16)
    send[0:width, :] = fields[low * (rows - 2)]
    send[step : step + width, :] = fields[low * (rows - 2) + 1]
    send[2 * step : 2 * step + width, :] = cotangent[low * (rows - 1)]
    own = taps[low * (rows - 1)]
    send[3 * step : 3 * step + 16, 0:128] = own[0:16]
    send[3 * step : 3 * step + 16, 128:256] = own[16:32]


def fill_lon(send_c, send_d, near, far):
    odd = is_odd("lon") == 1
    at = 0
    for first, last in zip(near, far, strict=True):
        size = first.shape[0]
        send_c[at : at + size, :] = jnp.where(odd, first, last)
        send_d[at : at + size, :] = jnp.where(odd, last, first)
        at += size


def pack_lat(fields, cotangent, taps, send_a, send_b, fields_rows, cotangent_rows):
    fields_rows[...] = jnp.swapaxes(fields[...], 0, 1)
    cotangent_rows[...] = jnp.swapaxes(cotangent[...], 0, 1)
    odd = is_odd("lat")
    fill_lat(send_a, 1 - odd, fields_rows, cotangent_rows, taps)
    fill_lat(send_b, odd, fields_rows, cotangent_rows, taps)


def pack_corners(rows, got_d, got_c, inner, send_a, send_b):
    odd = is_odd("lat")
    left_is_c = is_odd("lon") == 1
    for send, low in ((send_a, 1 - odd), (send_b, odd)):
        at = pl.multiple_of(low * (rows - 2) * EDGE, EDGE)
        c, d = got_c[pl.ds(at, 2 * EDGE), :], got_d[pl.ds(at, 2 * EDGE), :]
        send[0 : 2 * EDGE, :] = jnp.where(left_is_c, c, d)
        send[2 * EDGE : 4 * EDGE, :] = jnp.where(left_is_c, d, c)
        first, last = EDGE * rows, (EDGE + LREACH) * rows
        c, d = [
            jnp.where(low == 1, x[last - EDGE : last, :].astype(F32)[LREACH:], x[first : first + EDGE, :].astype(F32)[0:LREACH])
            for x in (got_c, got_d)
        ]
        both = [jnp.where(left_is_c, c, d), jnp.where(left_is_c, d, c)]
        send[4 * EDGE : 5 * EDGE, :] = jnp.concatenate(both, axis=0).astype(BF16)


def lay_taps(every, pitch, lanes):
    groups = every.shape[0] // 8

    def places(shape, dim):
        col = lax.broadcasted_iota(jnp.int32, shape, dim)
        turned = col >= lanes
        inner = jnp.where(turned, col - lanes, col)
        part = jnp.where(inner >= pitch, 1, 0) + jnp.where(inner >= 2 * pitch, 1, 0)
        return turned, inner - pitch * part, part

    turned, place, _ = places((128, 2 * lanes), 1)
    tap = lax.broadcasted_iota(jnp.int32, (128, 2 * lanes), 0)
    wanted = jnp.where(turned, 2 * LREACH - place, place)
    table = jnp.where((tap == wanted) & (tap < TAPS), 1.0, 0.0).astype(BF16)
    spread = jnp.dot(every, table, preferred_element_type=F32).reshape(groups, 8, 2 * lanes)
    turned, _, part = places((groups, 8, 2 * lanes), 2)
    lat_tap = lax.broadcasted_iota(jnp.int32, (groups, 8, 2 * lanes), 1)
    chosen = jnp.where(turned, 2 - part, part) == lat_tap
    return jnp.sum(jnp.where(chosen, spread, 0.0), axis=1)


def slant(line, size):
    lanes = line.shape[1]
    return pltpu.roll(jnp.broadcast_to(line, (size, lanes)), 0, 1, stride=1, stride_axis=0).astype(BF16)


def build_bands(every, size, pitch, lanes, forward, forward_rows, backward, backward_rows):
    lines = lay_taps(every, pitch, lanes)
    lane = lax.broadcasted_iota(jnp.int32, (1, lanes), 1)
    for place, i in enumerate(forward_rows):
        for k in range(KB):
            at = KB * i + k
            forward[place, size * k : size * (k + 1), :] = slant(lines[at : at + 1, 0:lanes], size)
    for place, i in enumerate(backward_rows):
        for k in range(KB):
            near = [lines[KB * (i + t - 1) + k : KB * (i + t - 1) + k + 1, lanes:] for t in range(3)]
            line = jnp.where(lane < pitch, near[0], jnp.where(lane < 2 * pitch, near[1], near[2]))
            backward[place, size * k : size * (k + 1), :] = slant(line, size)


def gelu_parts(pre):
    size = jnp.abs(pre)
    bell = jnp.exp(-0.5 * pre * pre)
    t = 1.0 / (1.0 + 0.23164188836 * size)
    poly = t * (0.127414796 + t * (-0.142248368 + t * (0.7107068705 + t * (-0.7265760135 + t * 0.5307027145))))
    tail = poly * bell
    cdf = jnp.where(pre >= 0.0, 1.0 - tail, tail)
    return pre * cdf, cdf + pre * bell * 0.3989422804014327


def contract_last(left, right):
    return lax.dot_general(left, right, (((1,), (1,)), ((), ())), preferred_element_type=F32)


def mlp(hidden, upstream, w_up, w_down, first, last):
    arriving = contract_last(upstream[...], w_down[...])
    pre = jnp.dot(hidden[...], w_up[...], preferred_element_type=F32)
    active, slope = gelu_parts(pre)
    grad = (upstream[...].astype(F32) + contract_last((arriving * slope).astype(BF16), w_up[...])).astype(BF16)
    out = hidden[first:last, :].astype(F32) + jnp.dot(
        active[first:last].astype(BF16), w_down[...], preferred_element_type=F32
    )
    return out, grad


SPAN = BLOCK + EDGE


def middle_rows(lines, cotangents, bands, edge_bands, firsts, w_mix, w_up, w_down, out_rows, scratch):
    wide, narrow, basis, hidden, upstream = scratch
    chans = w_up.shape[0]
    width = lines[0].shape[0]
    fill = PITCH + EDGE - width
    for f, line in enumerate(lines):
        wide[PITCH * f : PITCH * (f + 1), :] = line[0:PITCH]
        tail = jnp.concatenate([line[BLOCK:].astype(F32), jnp.zeros((fill, chans), F32)], axis=0)
        narrow[EDGE_PITCH * f : EDGE_PITCH * (f + 1), :] = tail.astype(BF16)
    wide[PITCH * len(lines) :, :] = jnp.zeros((LANES - 3 * PITCH, chans), BF16)
    narrow[EDGE_PITCH * len(lines) :, :] = jnp.zeros((EDGE_LANES - 3 * EDGE_PITCH, chans), BF16)
    for n, f in enumerate(firsts):
        at = SPAN * n
        moved = jnp.dot(bands[n], wide[PITCH * f : PITCH * f + LANES, :], preferred_element_type=F32).astype(BF16)
        other = jnp.dot(
            edge_bands[n], narrow[EDGE_PITCH * f : EDGE_PITCH * f + EDGE_LANES, :], preferred_element_type=F32
        ).astype(BF16)
        for k in range(KB):
            basis[at : at + BLOCK, chans * k : chans * (k + 1)] = moved[BLOCK * k : BLOCK * (k + 1)]
            basis[at + BLOCK : at + SPAN, chans * k : chans * (k + 1)] = other[EDGE * k : EDGE * (k + 1)]
    stacked = jnp.concatenate([w_mix[:, chans * k : chans * (k + 1)] for k in range(KB)], axis=0)
    spatial = jnp.dot(basis[...], stacked, preferred_element_type=F32)
    for n, f in enumerate(firsts):
        at = PITCH * (f + 1)
        first = wide[at : at + PITCH, :].astype(F32)[LREACH : LREACH + BLOCK]
        at = EDGE_PITCH * (f + 1)
        second = narrow[at : at + EDGE_PITCH, :].astype(F32)[LREACH : LREACH + EDGE]
        here = SPAN * n
        mine = jnp.concatenate([first, second], axis=0) + spatial[here : here + SPAN]
        hidden[here : here + SPAN, :] = mine.astype(BF16)
        upstream[here : here + SPAN, :] = cotangents[n].astype(F32)[LREACH : LREACH + SPAN].astype(BF16)
    return mlp(hidden, upstream, w_up, w_down, SPAN * out_rows[0], SPAN * out_rows[1])


def inner_kernel(
    fields, cotangent, taps, w_mix, w_up, w_down, sent,
    result, grads, forward, backward, edge_forward, edge_backward, *scratch,
):
    rows = fields.shape[0]
    every = jnp.concatenate([taps[r] for r in range(rows)], axis=0)
    own, inner = range(rows), range(1, rows - 1)
    build_bands(every, BLOCK, PITCH, LANES, forward, own, backward, inner)
    build_bands(every, EDGE, EDGE_PITCH, EDGE_LANES, edge_forward, own, edge_backward, inner)
    out, grad = middle_rows(
        [fields[r] for r in own],
        [cotangent[r] for r in inner],
        [forward[r] for r in inner],
        [edge_forward[r] for r in inner],
        [r - 1 for r in inner],
        w_mix, w_up, w_down, (0, rows - 2), scratch,
    )
    result[...] = out.reshape(result.shape).astype(BF16)
    grads[...] = grad


def middle_kernel(
    got_a, got_b, fields, cotangent, taps, inner_result, inner_grads, inner_forward, inner_edge_forward,
    w_mix, w_up, w_down,
    result, grads, edge_grads, backward, edge_forward, edge_backward, halo,
    forward, *scratch,
):
    rows, width, chans = fields.shape
    step = ceil_to(width, 16)
    pick = lat_picker(got_a, got_b)
    ext = rows + 2

    def taps_of(top):
        both = pick(3 * step, 3 * step + 16, top)
        return [both[:, 0:128], both[:, 128:256]]

    for part, (fields_at, cotangent_at) in enumerate(((0, 0), (width - EDGE, width - LREACH))):
        cells = [
            pick(step * n, step * n + width, top).astype(F32)[fields_at : fields_at + EDGE]
            for top in (True, False)
            for n in range(2)
        ]
        cells += [
            pick(2 * step, 2 * step + width, top).astype(F32)[cotangent_at : cotangent_at + LREACH] for top in (True, False)
        ]
        halo[part] = jnp.concatenate(cells, axis=0).astype(BF16)

    every = jnp.concatenate(taps_of(True) + [taps[r] for r in range(rows)] + taps_of(False), axis=0)
    ends = (0, ext - 1), (1, rows)
    build_bands(every, BLOCK, PITCH, LANES, forward, ends[0], backward, ends[1])
    build_bands(every, EDGE, EDGE_PITCH, EDGE_LANES, edge_forward, ends[0], edge_backward, ends[1])

    lines = [pick(step * n, step * n + width, True) for n in range(2)]
    lines += [fields[r] for r in range(rows)]
    lines += [pick(step * n, step * n + width, False) for n in range(2)]
    out, grad = middle_rows(
        lines,
        [pick(2 * step, 2 * step + width, True), cotangent[0], cotangent[rows - 1], pick(2 * step, 2 * step + width, False)],
        [forward[0], inner_forward[0], inner_forward[rows - 1], forward[1]],
        [edge_forward[0], inner_edge_forward[0], inner_edge_forward[rows - 1], edge_forward[1]],
        [0, 1, ext - 2, ext - 1],
        w_mix, w_up, w_down, (1, 3), scratch,
    )
    result[0] = out[0:SPAN].astype(BF16)
    result[1 : rows - 1] = inner_result[...]
    result[rows - 1] = out[SPAN:].astype(BF16)
    grads[0 : 2 * SPAN, :] = grad[0 : 2 * SPAN]
    grads[2 * SPAN : (ext - 2) * SPAN, :] = inner_grads[...]
    grads[(ext - 2) * SPAN : ext * SPAN, :] = grad[2 * SPAN :]
    grads[SPAN * ext :, :] = jnp.zeros((LANES - 3 * PITCH, chans), BF16)
    far = width - EDGE - 2 * LREACH
    for i in range(ext):
        mine = grads[SPAN * i : SPAN * (i + 1), :]
        edge_grads[0, EDGE * i : EDGE * (i + 1), :] = mine[0:EDGE]
        edge_grads[1, EDGE * i : EDGE * (i + 1), :] = mine.astype(F32)[far : far + EDGE].astype(BF16)


def edge_kernel(
    middle_result, middle_grads, edge_grads, inner_backward, end_backward, inner_edge_forward, inner_edge_backward, end_edge_forward, end_edge_backward,
    halo, send_c, send_d, got_d, got_c, corner_a, corner_b, w_mix, w_up, w_down,
    result, field_grad, source, basis, hidden, upstream, grads, grad_mixed, result_edges, grad_edges,
    middle_grad_mixed, turned_result, turned_grad, sems,
):
    width, rows, chans = result.shape
    ext = rows + 2
    copies = []

    def store(here, out, first, size):
        copies.append(pltpu.make_async_copy(here.at[pl.ds(0, size)], out.at[pl.ds(first, size)], sems.at[len(copies)]))
        copies[-1].start()

    left_is_c = is_odd("lon") == 1
    edge_forward = [end_edge_forward[0]] + [inner_edge_forward[r] for r in range(rows)] + [end_edge_forward[1]]
    edge_backward = [end_edge_backward[0]] + [inner_edge_backward[r] for r in range(rows - 2)] + [end_edge_backward[1]]
    pick = lat_picker(corner_a, corner_b)

    def own_cells(at):
        sent_c, sent_d, came_c, came_d = [x[at : at + EDGE, :] for x in (send_c, send_d, got_c, got_d)]
        return (
            jnp.where(left_is_c, came_c, came_d),
            jnp.where(left_is_c, sent_c, sent_d),
            jnp.where(left_is_c, sent_d, sent_c),
            jnp.where(left_is_c, came_d, came_c),
        )

    for i in range(rows + 4):
        if 2 <= i < rows + 2:
            cells = own_cells(EDGE * (i - 2))
        else:
            top = i < 2
            n = i if top else i - rows - 2
            at = EDGE * (i if top else i - rows)
            left, right = [pick(EDGE * m, EDGE * (m + 1), top) for m in (n, n + 2)]
            cells = left, halo[0, at : at + EDGE, :], halo[1, at : at + EDGE, :], right
        at = EDGE_PITCH * i
        source[at : at + EDGE, 0:chans] = cells[0]
        source[at + EDGE : at + 2 * EDGE, 0:chans] = cells[1]
        source[at : at + EDGE, chans:] = cells[2]
        source[at + EDGE : at + 2 * EDGE, chans:] = cells[3]
    source[EDGE_PITCH * (rows + 4) :, :] = jnp.zeros((EDGE_LANES - 3 * EDGE_PITCH, 2 * chans), BF16)

    for i in range(ext):
        if 0 < i < ext - 1:
            inside = LREACH * ((i - 1) % 2)
            cells = own_cells(EDGE * rows + EDGE * ((i - 1) // 2))
            cells = [x.astype(F32)[inside : inside + LREACH] for x in cells]
        else:
            inside = 0 if i == 0 else LREACH
            near, far = [halo[part, 4 * EDGE : 5 * EDGE, :].astype(F32)[inside : inside + LREACH] for part in range(2)]
            both = pick(4 * EDGE, 5 * EDGE, i == 0).astype(F32)
            cells = both[0:LREACH], near, far, both[LREACH:]
        here = 2 * EDGE * i
        upstream[here : here + EDGE, :] = jnp.concatenate(cells[0:2], axis=0).astype(BF16)
        upstream[here + EDGE : here + 2 * EDGE, :] = jnp.concatenate(cells[2:4], axis=0).astype(BF16)

    def spread(band, cells, at, out):
        moved = jnp.dot(band, cells, preferred_element_type=F32).astype(BF16)
        for part in range(2):
            for k in range(KB):
                out[at + EDGE * part : at + EDGE * (part + 1), chans * k : chans * (k + 1)] = moved[
                    EDGE * k : EDGE * (k + 1), chans * part : chans * (part + 1)
                ]

    for i in range(ext):
        spread(edge_forward[i], source[EDGE_PITCH * i : EDGE_PITCH * i + EDGE_LANES, :], 2 * EDGE * i, basis)
    bands = [end_backward[0]] + [inner_backward[r] for r in range(rows - 2)] + [end_backward[1]]
    for i in range(rows):
        moved = jnp.dot(bands[i], middle_grads[PITCH * i : PITCH * i + LANES, :], preferred_element_type=F32).astype(BF16)
        for k in range(KB):
            middle_grad_mixed[BLOCK * i : BLOCK * (i + 1), chans * k : chans * (k + 1)] = moved[BLOCK * k : BLOCK * (k + 1)]
    turned_result[...] = jnp.swapaxes(middle_result[...], 0, 1)
    store(turned_result, result, LREACH, width - 2 * LREACH)
    stacked = jnp.concatenate([w_mix[:, chans * k : chans * (k + 1)] for k in range(KB)], axis=0)
    spatial = jnp.dot(basis[...], stacked, preferred_element_type=F32)
    for i in range(ext):
        at = EDGE_PITCH * (i + 1)
        cells = source[at : at + EDGE_PITCH, :].astype(F32)[LREACH : LREACH + EDGE]
        for part in range(2):
            here = EDGE * (2 * i + part)
            hidden[here : here + EDGE, :] = (
                cells[:, chans * part : chans * (part + 1)] + spatial[here : here + EDGE]
            ).astype(BF16)
    back = contract_last(middle_grad_mixed[...], w_mix[...])
    lines = []
    for i in range(rows):
        at = PITCH * (i + 1)
        own = middle_grads[at : at + PITCH, :].astype(F32)[LREACH : LREACH + BLOCK]
        lines.append((own + back[BLOCK * i : BLOCK * (i + 1)]).astype(BF16))
    turned_grad[...] = jnp.swapaxes(jnp.stack(lines), 0, 1)
    store(turned_grad, field_grad, EDGE, width - 2 * EDGE)
    out, grad = mlp(hidden, upstream, w_up, w_down, 2 * EDGE, 2 * EDGE * (rows + 1))
    for part in range(2):
        inside = 0 if part else LREACH
        lines = [out[at + inside : at + inside + LREACH] for at in (EDGE * (2 * i + part) for i in range(rows))]
        result_edges[part] = jnp.swapaxes(jnp.stack(lines), 0, 1).astype(BF16)
        store(result_edges.at[part], result, part * (width - LREACH), LREACH)

    for i in range(ext):
        at = EDGE_PITCH * i
        here = 2 * EDGE * i
        grads[at : at + EDGE, 0:chans] = grad[here : here + EDGE]
        grads[at + EDGE : at + 2 * EDGE, 0:chans] = edge_grads[0, EDGE * i : EDGE * (i + 1), :]
        grads[at : at + EDGE, chans:] = edge_grads[1, EDGE * i : EDGE * (i + 1), :]
        grads[at + EDGE : at + 2 * EDGE, chans:] = grad[here + EDGE : here + 2 * EDGE]
    grads[EDGE_PITCH * ext :, :] = jnp.zeros((EDGE_LANES - 3 * EDGE_PITCH, 2 * chans), BF16)
    for i in range(rows):
        spread(edge_backward[i], grads[EDGE_PITCH * i : EDGE_PITCH * i + EDGE_LANES, :], 2 * EDGE * i, grad_mixed)
    back = contract_last(grad_mixed[...], w_mix[...])
    for part in range(2):
        lines = []
        for i in range(rows):
            at = EDGE_PITCH * (i + 1)
            own = grads[at : at + EDGE_PITCH, chans * part : chans * (part + 1)].astype(F32)[LREACH : LREACH + EDGE]
            here = EDGE * (2 * i + part)
            lines.append(own + back[here : here + EDGE])
        grad_edges[part] = jnp.swapaxes(jnp.stack(lines), 0, 1).astype(BF16)
        store(grad_edges.at[part], field_grad, part * (width - EDGE), EDGE)
    for copy in copies:
        copy.wait()


def on_device(fields, w_mix, filters, reach, w_up, w_down, cotangent):
    rows, width, chans = fields.shape
    step = ceil_to(width, 16)
    ext = rows + 2
    pad = LANES - 3 * PITCH
    edge_pad = EDGE_LANES - 3 * EDGE_PITCH

    def shaped(*shape):
        return jax.ShapeDtypeStruct(shape, BF16)

    turned = shaped(width, rows, chans)
    whole = shaped(rows, width, chans)
    sent = shaped(3 * step + 16, chans)
    edge = shaped((EDGE + LREACH) * rows, chans)
    fields = fields.transpose(1, 0, 2)
    cotangent = cotangent.transpose(1, 0, 2)
    send_c, send_d, taps = call(
        fetch,
        (edge, edge, shaped(rows, 8 * KB, 128)),
        [hbm()] * 4,
        [
            pltpu.VMEM((2, EDGE, rows, chans), BF16),
            pltpu.VMEM((2, LREACH, rows, chans), BF16),
            pltpu.VMEM((KB, 3, rows, TAPS), BF16),
            pltpu.SMEM((rows,), jnp.int32),
            pltpu.VMEM((rows, 8 * KB, 128), F32),
            pltpu.SemaphoreType.DMA((6,)),
        ],
        (1000, 1000000),
        *(
            pltpu.with_memory_space_constraint(x, pltpu.HBM)
            for x in (fields, cotangent, filters.transpose(0, 2, 1, 3), reach)
        ),
    )
    got_c = swap(send_c, "lon", 0)
    got_d = swap(send_d, "lon", 1)
    send_a, send_b, fields, cotangent = call(
        pack_lat, (sent, sent, whole, whole), [vmem()] * 3, [], (2000000000, 5000000), fields, cotangent, taps
    )
    got_a = swap(send_a, "lat", 0)
    got_b = swap_inner_lat(send_b)

    def scratch(lines, out_lines):
        return [
            pltpu.VMEM((PITCH * lines + pad, chans), BF16),
            pltpu.VMEM((EDGE_PITCH * lines + edge_pad, chans), BF16),
            pltpu.VMEM((SPAN * out_lines, KB * chans), BF16),
            pltpu.VMEM((SPAN * out_lines, chans), BF16),
            pltpu.VMEM((SPAN * out_lines, chans), BF16),
        ]

    def bands(count):
        return shaped(count, KB * BLOCK, LANES)

    def edge_bands(count):
        return shaped(count, KB * EDGE, EDGE_LANES)

    inner_result, inner_grads, inner_forward, inner_backward, inner_edge_forward, inner_edge_backward = call(
        inner_kernel,
        (
            shaped(rows - 2, SPAN, chans),
            shaped(SPAN * (rows - 2), chans),
            bands(rows),
            bands(rows - 2),
            edge_bands(rows),
            edge_bands(rows - 2),
        ),
        [vmem()] * 6 + [pl.BlockSpec(memory_space=pl.ANY)],
        scratch(rows, rows - 2),
        (300000000, 1000000),
        fields, cotangent, taps, w_mix, w_up, w_down, send_a,
    )
    corner = shaped(5 * EDGE, chans)
    corner_a, corner_b = call(
        functools.partial(pack_corners, rows),
        (corner, corner),
        [vmem()] * 2 + [pl.BlockSpec(memory_space=pl.ANY)],
        [],
        (4000000000, 1000000),
        got_d, got_c, inner_result,
    )
    corner_a = swap(corner_a, "lat", 0)
    corner_b = swap_inner_lat(corner_b)
    middle_result, middle_grads, edge_grads, backward, edge_forward, edge_backward, halo = call(
        middle_kernel,
        (
            shaped(rows, SPAN, chans),
            shaped(SPAN * ext + pad, chans),
            shaped(2, EDGE * ext, chans),
            bands(2),
            edge_bands(2),
            edge_bands(2),
            shaped(2, 5 * EDGE, chans),
        ),
        [vmem()] * 12,
        [pltpu.VMEM((2, KB * BLOCK, LANES), BF16)] + scratch(rows + 4, 4),
        (2000000000, 5000000),
        got_a, got_b, fields, cotangent, taps, inner_result, inner_grads, inner_forward, inner_edge_forward,
        w_mix, w_up, w_down,
    )
    result, field_grad = call(
        edge_kernel,
        (turned, turned),
        [vmem()] * 19,
        [
            pltpu.VMEM((EDGE_PITCH * (rows + 4) + edge_pad, 2 * chans), BF16),
            pltpu.VMEM((2 * EDGE * ext, KB * chans), BF16),
            pltpu.VMEM((2 * EDGE * ext, chans), BF16),
            pltpu.VMEM((2 * EDGE * ext, chans), BF16),
            pltpu.VMEM((EDGE_PITCH * ext + edge_pad, 2 * chans), BF16),
            pltpu.VMEM((2 * EDGE * rows, KB * chans), BF16),
            pltpu.VMEM((2, LREACH, rows, chans), BF16),
            pltpu.VMEM((2, EDGE, rows, chans), BF16),
            pltpu.VMEM((BLOCK * rows, KB * chans), BF16),
            pltpu.VMEM((SPAN, rows, chans), BF16),
            pltpu.VMEM((BLOCK, rows, chans), BF16),
            pltpu.SemaphoreType.DMA((6,)),
        ],
        (500000000, 3000000),
        middle_result, middle_grads, edge_grads, inner_backward, backward, inner_edge_forward, inner_edge_backward, edge_forward, edge_backward,
        halo, send_c, send_d, got_d, got_c, corner_a, corner_b, w_mix, w_up, w_down,
        out_specs=(hbm(), hbm()),
    )
    return result.transpose(1, 0, 2), field_grad.transpose(1, 0, 2)


def solution(mesh):
    return jax.shard_map(
        on_device,
        mesh=mesh,
        in_specs=(
            P("lat", "lon", None),
            P(),
            P(None, "lat", None, None),
            P("lat"),
            P(),
            P(),
            P("lat", "lon", None),
        ),
        out_specs=(P("lat", "lon", None), P("lat", "lon", None)),
        check_vma=False,
    )
```

```python
import functools

import jax
import jax.numpy as jnp
from jax import lax
from jax.experimental import pallas as pl
from jax.experimental.pallas import tpu as pltpu
from jax.sharding import PartitionSpec as P

KB = 4
LREACH = 8
TAPS = 2 * LREACH + 1
BLOCK = 64
PITCH = BLOCK + 2 * LREACH
EDGE = 2 * LREACH
EDGE_PITCH = 2 * EDGE
LANES = 256
TAP_LANES = 128
F32 = jnp.float32
BF16 = jnp.bfloat16
VMEM_BYTES = 48 * 1024 * 1024


def ceil_to(size, unit):
    return -(-size // unit) * unit


def vmem():
    return pl.BlockSpec(memory_space=pltpu.VMEM)


def hbm():
    return pl.BlockSpec(memory_space=pltpu.HBM)


def is_odd(axis):
    return lax.rem(lax.axis_index(axis), 2)


def call(kernel, outs, in_specs, scratch, cost, *args, out_specs=None):
    return pl.pallas_call(
        kernel,
        out_shape=outs,
        in_specs=in_specs,
        out_specs=out_specs or jax.tree.map(lambda _: vmem(), outs),
        scratch_shapes=scratch,
        compiler_params=pltpu.CompilerParams(vmem_limit_bytes=VMEM_BYTES),
        cost_estimate=pl.CostEstimate(flops=cost[0], bytes_accessed=cost[1], transcendentals=0),
    )(*args)


def swap(cells, axis, shift):
    count = lax.axis_size(axis)
    pairs = []
    for first in range(shift, count, 2):
        second = (first + 1) % count
        pairs += [(first, second), (second, first)]
    return lax.ppermute(cells, axis, pairs)


def swap_inner_lat(cells):
    count, around = lax.axis_size("lat"), lax.axis_size("lon")
    pairs = []
    for j in range(around):
        pairs += [(i * around + j, i * around + (j + around // 2) % around) for i in (0, count - 1)]
        for i in range(1, count - 1, 2):
            pairs += [(i * around + j, (i + 1) * around + j), ((i + 1) * around + j, i * around + j)]
    return lax.ppermute(cells, ("lat", "lon"), pairs)


def lat_picker(got_a, got_b):
    top_is_a = is_odd("lat") == 1
    index = lax.axis_index("lat")
    inner = (index > 0) & (index < lax.axis_size("lat") - 1)

    def pick(first, last, top):
        a, b = got_a[first:last, :], got_b[first:last, :]
        return jnp.where(top_is_a == top, a, jnp.where(inner, b, jnp.zeros_like(b)))

    return pick


def fetch(fields, cotangent, filters, reach, send_c, send_d, taps, fields_here, cotangent_here, filters_here, reach_here, raw, sems):
    width, rows, chans = fields.shape
    moves = [(filters, filters_here), (reach, reach_here)]
    for part in range(2):
        moves.append((fields.at[pl.ds(part * (width - EDGE), EDGE)], fields_here.at[part]))
        moves.append((cotangent.at[pl.ds(part * (width - LREACH), LREACH)], cotangent_here.at[part]))
    copies = [pltpu.make_async_copy(src, dst, sems.at[n]) for n, (src, dst) in enumerate(moves)]
    for copy in copies:
        copy.start()
    raw[...] = jnp.zeros(raw.shape, F32)
    offset = jnp.abs(lax.broadcasted_iota(jnp.int32, (8 * KB, 128), 1) - LREACH)
    copies[0].wait()
    copies[1].wait()
    for k in range(KB):
        for a in range(3):
            line = filters_here[k, a].astype(F32)
            for r in range(rows):
                raw[r, 8 * k + a : 8 * k + a + 1, 0:TAPS] = line[r : r + 1]
    for r in range(rows):
        taps[r] = jnp.where(offset <= reach_here[r], raw[r], 0.0).astype(BF16)
    for copy in copies[2:]:
        copy.wait()
    sides = []
    for part in range(2):
        cells = jnp.swapaxes(fields_here[part], 0, 1).reshape(EDGE * rows, chans)
        grads = jnp.swapaxes(cotangent_here[part].astype(F32), 0, 1).reshape(LREACH * rows, chans).astype(BF16)
        sides.append((cells, grads))
    fill_lon(send_c, send_d, *sides)


def fill_lat(send, low, fields, cotangent, taps):
    rows, width, chans = fields.shape
    step = ceil_to(width, 16)
    send[0:width, :] = fields[low * (rows - 2)]
    send[step : step + width, :] = fields[low * (rows - 2) + 1]
    send[2 * step : 2 * step + width, :] = cotangent[low * (rows - 1)]
    own = taps[low * (rows - 1)]
    send[3 * step : 3 * step + 16, 0:128] = own[0:16]
    send[3 * step : 3 * step + 16, 128:256] = own[16:32]


def fill_lon(send_c, send_d, near, far):
    odd = is_odd("lon") == 1
    at = 0
    for first, last in zip(near, far, strict=True):
        size = first.shape[0]
        send_c[at : at + size, :] = jnp.where(odd, first, last)
        send_d[at : at + size, :] = jnp.where(odd, last, first)
        at += size


def pack_lat(fields, cotangent, taps, send_a, send_b, fields_rows, cotangent_rows):
    fields_rows[...] = jnp.swapaxes(fields[...], 0, 1)
    cotangent_rows[...] = jnp.swapaxes(cotangent[...], 0, 1)
    odd = is_odd("lat")
    fill_lat(send_a, 1 - odd, fields_rows, cotangent_rows, taps)
    fill_lat(send_b, odd, fields_rows, cotangent_rows, taps)


def pack_corners(rows, got_d, got_c, inner, send_a, send_b):
    odd = is_odd("lat")
    left_is_c = is_odd("lon") == 1
    for send, low in ((send_a, 1 - odd), (send_b, odd)):
        at = pl.multiple_of(low * (rows - 2) * EDGE, EDGE)
        c, d = got_c[pl.ds(at, 2 * EDGE), :], got_d[pl.ds(at, 2 * EDGE), :]
        send[0 : 2 * EDGE, :] = jnp.where(left_is_c, c, d)
        send[2 * EDGE : 4 * EDGE, :] = jnp.where(left_is_c, d, c)
        first, last = EDGE * rows, (EDGE + LREACH) * rows
        c, d = [
            jnp.where(low == 1, x[last - EDGE : last, :].astype(F32)[LREACH:], x[first : first + EDGE, :].astype(F32)[0:LREACH])
            for x in (got_c, got_d)
        ]
        both = [jnp.where(left_is_c, c, d), jnp.where(left_is_c, d, c)]
        send[4 * EDGE : 5 * EDGE, :] = jnp.concatenate(both, axis=0).astype(BF16)


def lay_taps(every, pitch, lanes):
    groups = every.shape[0] // 8

    def places(shape, dim):
        col = lax.broadcasted_iota(jnp.int32, shape, dim)
        turned = col >= lanes
        inner = jnp.where(turned, col - lanes, col)
        part = jnp.where(inner >= pitch, 1, 0) + jnp.where(inner >= 2 * pitch, 1, 0)
        return turned, inner - pitch * part, part

    turned, place, _ = places((128, 2 * lanes), 1)
    tap = lax.broadcasted_iota(jnp.int32, (128, 2 * lanes), 0)
    wanted = jnp.where(turned, 2 * LREACH - place, place)
    table = jnp.where((tap == wanted) & (tap < TAPS), 1.0, 0.0).astype(BF16)
    spread = jnp.dot(every, table, preferred_element_type=F32).reshape(groups, 8, 2 * lanes)
    turned, _, part = places((groups, 8, 2 * lanes), 2)
    lat_tap = lax.broadcasted_iota(jnp.int32, (groups, 8, 2 * lanes), 1)
    chosen = jnp.where(turned, 2 - part, part) == lat_tap
    return jnp.sum(jnp.where(chosen, spread, 0.0), axis=1)


def slant(line, size, shift):
    lanes = line.shape[1]
    return pltpu.roll(jnp.broadcast_to(line, (size, lanes)), shift, 1, stride=1, stride_axis=0).astype(BF16)


def build_bands(every, size, pitch, first, forward, forward_rows, backward, backward_rows):
    edge = size == EDGE
    lanes = TAP_LANES if edge else LANES
    lines = lay_taps(every, pitch, lanes)
    lane = lax.broadcasted_iota(jnp.int32, (1, lanes), 1)

    def lean(line, row):
        if edge:
            line = jnp.concatenate([line, jnp.zeros((1, LANES - lanes), F32)], axis=1)
        return slant(line, size, pitch * row if edge else 0)

    for place, i in enumerate(forward_rows):
        for k in range(KB):
            at = KB * i + k
            forward[place, size * k : size * (k + 1), :] = lean(lines[at : at + 1, 0:lanes], i + first)
    for place, i in enumerate(backward_rows):
        for k in range(KB):
            near = [lines[KB * (i + t - 1) + k : KB * (i + t - 1) + k + 1, lanes:] for t in range(3)]
            line = jnp.where(lane < pitch, near[0], jnp.where(lane < 2 * pitch, near[1], near[2]))
            backward[place, size * k : size * (k + 1), :] = lean(line, i + first - 1)


def gelu_parts(pre):
    size = jnp.abs(pre)
    bell = jnp.exp(-0.5 * pre * pre)
    t = 1.0 / (1.0 + 0.23164188836 * size)
    poly = t * (0.127414796 + t * (-0.142248368 + t * (0.7107068705 + t * (-0.7265760135 + t * 0.5307027145))))
    tail = poly * bell
    cdf = jnp.where(pre >= 0.0, 1.0 - tail, tail)
    return pre * cdf, cdf + pre * bell * 0.3989422804014327


def contract_last(left, right):
    return lax.dot_general(left, right, (((1,), (1,)), ((), ())), preferred_element_type=F32)


def mlp(hidden, upstream, w_up, w_down, first, last):
    arriving = contract_last(upstream[...], w_down[...])
    pre = jnp.dot(hidden[...], w_up[...], preferred_element_type=F32)
    active, slope = gelu_parts(pre)
    grad = (upstream[...].astype(F32) + contract_last((arriving * slope).astype(BF16), w_up[...])).astype(BF16)
    out = hidden[first:last, :].astype(F32) + jnp.dot(
        active[first:last].astype(BF16), w_down[...], preferred_element_type=F32
    )
    return out, grad


SPAN = BLOCK + EDGE


def middle_rows(lines, start, cotangents, bands, edge_bands, firsts, w_mix, w_up, w_down, out_rows, scratch):
    wide, narrow, basis, hidden, upstream = scratch
    chans = w_up.shape[0]
    width = lines[0].shape[0]
    fill = PITCH + EDGE - width
    if start:
        narrow[...] = jnp.zeros(narrow.shape, BF16)
    for f, line in enumerate(lines):
        wide[PITCH * f : PITCH * (f + 1), :] = line[0:PITCH]
        tail = jnp.concatenate([line[BLOCK:].astype(F32), jnp.zeros((fill, chans), F32)], axis=0)
        narrow[EDGE_PITCH * (start + f) : EDGE_PITCH * (start + f + 1), :] = tail.astype(BF16)
    wide[PITCH * len(lines) :, :] = jnp.zeros((LANES - 3 * PITCH, chans), BF16)
    others = jnp.dot(jnp.concatenate(edge_bands, axis=0), narrow[...], preferred_element_type=F32).astype(BF16)
    for n, f in enumerate(firsts):
        at = SPAN * n
        moved = jnp.dot(bands[n], wide[PITCH * f : PITCH * f + LANES, :], preferred_element_type=F32).astype(BF16)
        other = others[KB * EDGE * n : KB * EDGE * (n + 1)]
        for k in range(KB):
            basis[at : at + BLOCK, chans * k : chans * (k + 1)] = moved[BLOCK * k : BLOCK * (k + 1)]
            basis[at + BLOCK : at + SPAN, chans * k : chans * (k + 1)] = other[EDGE * k : EDGE * (k + 1)]
    stacked = jnp.concatenate([w_mix[:, chans * k : chans * (k + 1)] for k in range(KB)], axis=0)
    spatial = jnp.dot(basis[...], stacked, preferred_element_type=F32)
    for n, f in enumerate(firsts):
        at = PITCH * (f + 1)
        first = wide[at : at + PITCH, :].astype(F32)[LREACH : LREACH + BLOCK]
        at = EDGE_PITCH * (start + f + 1)
        second = narrow[at : at + EDGE_PITCH, :].astype(F32)[LREACH : LREACH + EDGE]
        here = SPAN * n
        mine = jnp.concatenate([first, second], axis=0) + spatial[here : here + SPAN]
        hidden[here : here + SPAN, :] = mine.astype(BF16)
        upstream[here : here + SPAN, :] = cotangents[n].astype(F32)[LREACH : LREACH + SPAN].astype(BF16)
    return mlp(hidden, upstream, w_up, w_down, SPAN * out_rows[0], SPAN * out_rows[1])


def inner_kernel(
    fields, cotangent, taps, w_mix, w_up, w_down, sent,
    result, grads, forward, backward, edge_forward, edge_backward, *scratch,
):
    rows = fields.shape[0]
    every = jnp.concatenate([taps[r] for r in range(rows)], axis=0)
    own, inner = range(rows), range(1, rows - 1)
    build_bands(every, BLOCK, PITCH, 1, forward, own, backward, inner)
    build_bands(every, EDGE, EDGE_PITCH, 1, edge_forward, own, edge_backward, inner)
    out, grad = middle_rows(
        [fields[r] for r in own],
        2,
        [cotangent[r] for r in inner],
        [forward[r] for r in inner],
        [edge_forward[r] for r in inner],
        [r - 1 for r in inner],
        w_mix, w_up, w_down, (0, rows - 2), scratch,
    )
    result[...] = out.reshape(result.shape).astype(BF16)
    grads[...] = grad


def middle_kernel(
    got_a, got_b, fields, cotangent, taps, inner_result, inner_grads, inner_forward, inner_edge_forward,
    w_mix, w_up, w_down,
    result, grads, edge_grads, backward, edge_forward, edge_backward, halo,
    forward, *scratch,
):
    rows, width, chans = fields.shape
    step = ceil_to(width, 16)
    pick = lat_picker(got_a, got_b)
    ext = rows + 2

    def taps_of(top):
        both = pick(3 * step, 3 * step + 16, top)
        return [both[:, 0:128], both[:, 128:256]]

    for part, (fields_at, cotangent_at) in enumerate(((0, 0), (width - EDGE, width - LREACH))):
        cells = [
            pick(step * n, step * n + width, top).astype(F32)[fields_at : fields_at + EDGE]
            for top in (True, False)
            for n in range(2)
        ]
        cells += [
            pick(2 * step, 2 * step + width, top).astype(F32)[cotangent_at : cotangent_at + LREACH] for top in (True, False)
        ]
        halo[part] = jnp.concatenate(cells, axis=0).astype(BF16)

    every = jnp.concatenate(taps_of(True) + [taps[r] for r in range(rows)] + taps_of(False), axis=0)
    ends = (0, ext - 1), (1, rows)
    build_bands(every, BLOCK, PITCH, 0, forward, ends[0], backward, ends[1])
    build_bands(every, EDGE, EDGE_PITCH, 0, edge_forward, ends[0], edge_backward, ends[1])

    lines = [pick(step * n, step * n + width, True) for n in range(2)]
    lines += [fields[r] for r in range(rows)]
    lines += [pick(step * n, step * n + width, False) for n in range(2)]
    out, grad = middle_rows(
        lines,
        0,
        [pick(2 * step, 2 * step + width, True), cotangent[0], cotangent[rows - 1], pick(2 * step, 2 * step + width, False)],
        [forward[0], inner_forward[0], inner_forward[rows - 1], forward[1]],
        [edge_forward[0], inner_edge_forward[0], inner_edge_forward[rows - 1], edge_forward[1]],
        [0, 1, ext - 2, ext - 1],
        w_mix, w_up, w_down, (1, 3), scratch,
    )
    result[0] = out[0:SPAN].astype(BF16)
    result[1 : rows - 1] = inner_result[...]
    result[rows - 1] = out[SPAN:].astype(BF16)
    grads[0 : 2 * SPAN, :] = grad[0 : 2 * SPAN]
    grads[2 * SPAN : (ext - 2) * SPAN, :] = inner_grads[...]
    grads[(ext - 2) * SPAN : ext * SPAN, :] = grad[2 * SPAN :]
    grads[SPAN * ext :, :] = jnp.zeros((LANES - 3 * PITCH, chans), BF16)
    far = width - EDGE - 2 * LREACH
    for i in range(ext):
        mine = grads[SPAN * i : SPAN * (i + 1), :]
        edge_grads[0, EDGE * i : EDGE * (i + 1), :] = mine[0:EDGE]
        edge_grads[1, EDGE * i : EDGE * (i + 1), :] = mine.astype(F32)[far : far + EDGE].astype(BF16)


def edge_kernel(
    middle_result, middle_grads, edge_grads, inner_backward, end_backward, inner_edge_forward, inner_edge_backward, end_edge_forward, end_edge_backward,
    halo, send_c, send_d, got_d, got_c, corner_a, corner_b, w_mix, w_up, w_down,
    result, field_grad, source, basis, hidden, upstream, grads, grad_mixed, result_edges, grad_edges,
    middle_grad_mixed, turned_result, turned_grad, sems,
):
    width, rows, chans = result.shape
    ext = rows + 2
    copies = []

    def store(here, out, first, size):
        copies.append(pltpu.make_async_copy(here.at[pl.ds(0, size)], out.at[pl.ds(first, size)], sems.at[len(copies)]))
        copies[-1].start()

    left_is_c = is_odd("lon") == 1
    edge_forward = [end_edge_forward[0]] + [inner_edge_forward[r] for r in range(rows)] + [end_edge_forward[1]]
    edge_backward = [end_edge_backward[0]] + [inner_edge_backward[r] for r in range(rows - 2)] + [end_edge_backward[1]]
    pick = lat_picker(corner_a, corner_b)

    def own_cells(at):
        sent_c, sent_d, came_c, came_d = [x[at : at + EDGE, :] for x in (send_c, send_d, got_c, got_d)]
        return (
            jnp.where(left_is_c, came_c, came_d),
            jnp.where(left_is_c, sent_c, sent_d),
            jnp.where(left_is_c, sent_d, sent_c),
            jnp.where(left_is_c, came_d, came_c),
        )

    for i in range(rows + 4):
        if 2 <= i < rows + 2:
            cells = own_cells(EDGE * (i - 2))
        else:
            top = i < 2
            n = i if top else i - rows - 2
            at = EDGE * (i if top else i - rows)
            left, right = [pick(EDGE * m, EDGE * (m + 1), top) for m in (n, n + 2)]
            cells = left, halo[0, at : at + EDGE, :], halo[1, at : at + EDGE, :], right
        at = EDGE_PITCH * i
        source[at : at + EDGE, 0:chans] = cells[0]
        source[at + EDGE : at + 2 * EDGE, 0:chans] = cells[1]
        source[at : at + EDGE, chans:] = cells[2]
        source[at + EDGE : at + 2 * EDGE, chans:] = cells[3]

    for i in range(ext):
        if 0 < i < ext - 1:
            inside = LREACH * ((i - 1) % 2)
            cells = own_cells(EDGE * rows + EDGE * ((i - 1) // 2))
            cells = [x.astype(F32)[inside : inside + LREACH] for x in cells]
        else:
            inside = 0 if i == 0 else LREACH
            near, far = [halo[part, 4 * EDGE : 5 * EDGE, :].astype(F32)[inside : inside + LREACH] for part in range(2)]
            both = pick(4 * EDGE, 5 * EDGE, i == 0).astype(F32)
            cells = both[0:LREACH], near, far, both[LREACH:]
        here = 2 * EDGE * i
        upstream[here : here + EDGE, :] = jnp.concatenate(cells[0:2], axis=0).astype(BF16)
        upstream[here + EDGE : here + 2 * EDGE, :] = jnp.concatenate(cells[2:4], axis=0).astype(BF16)

    def spread(bands, cells, out):
        moved = jnp.dot(jnp.concatenate(bands, axis=0), cells, preferred_element_type=F32).astype(BF16)
        for i in range(len(bands)):
            for part in range(2):
                at = EDGE * (2 * i + part)
                for k in range(KB):
                    here = EDGE * (KB * i + k)
                    out[at : at + EDGE, chans * k : chans * (k + 1)] = moved[
                        here : here + EDGE, chans * part : chans * (part + 1)
                    ]

    spread(edge_forward, source[...], basis)
    bands = [end_backward[0]] + [inner_backward[r] for r in range(rows - 2)] + [end_backward[1]]
    for i in range(rows):
        moved = jnp.dot(bands[i], middle_grads[PITCH * i : PITCH * i + LANES, :], preferred_element_type=F32).astype(BF16)
        for k in range(KB):
            middle_grad_mixed[BLOCK * i : BLOCK * (i + 1), chans * k : chans * (k + 1)] = moved[BLOCK * k : BLOCK * (k + 1)]
    turned_result[...] = jnp.swapaxes(middle_result[...], 0, 1)
    store(turned_result, result, LREACH, width - 2 * LREACH)
    stacked = jnp.concatenate([w_mix[:, chans * k : chans * (k + 1)] for k in range(KB)], axis=0)
    spatial = jnp.dot(basis[...], stacked, preferred_element_type=F32)
    for i in range(ext):
        at = EDGE_PITCH * (i + 1)
        cells = source[at : at + EDGE_PITCH, :].astype(F32)[LREACH : LREACH + EDGE]
        for part in range(2):
            here = EDGE * (2 * i + part)
            hidden[here : here + EDGE, :] = (
                cells[:, chans * part : chans * (part + 1)] + spatial[here : here + EDGE]
            ).astype(BF16)
    back = contract_last(middle_grad_mixed[...], w_mix[...])
    lines = []
    for i in range(rows):
        at = PITCH * (i + 1)
        own = middle_grads[at : at + PITCH, :].astype(F32)[LREACH : LREACH + BLOCK]
        lines.append((own + back[BLOCK * i : BLOCK * (i + 1)]).astype(BF16))
    turned_grad[...] = jnp.swapaxes(jnp.stack(lines), 0, 1)
    store(turned_grad, field_grad, EDGE, width - 2 * EDGE)
    out, grad = mlp(hidden, upstream, w_up, w_down, 2 * EDGE, 2 * EDGE * (rows + 1))
    for part in range(2):
        inside = 0 if part else LREACH
        lines = [out[at + inside : at + inside + LREACH] for at in (EDGE * (2 * i + part) for i in range(rows))]
        result_edges[part] = jnp.swapaxes(jnp.stack(lines), 0, 1).astype(BF16)
        store(result_edges.at[part], result, part * (width - LREACH), LREACH)

    for i in range(ext):
        at = EDGE_PITCH * i
        here = 2 * EDGE * i
        grads[at : at + EDGE, 0:chans] = grad[here : here + EDGE]
        grads[at + EDGE : at + 2 * EDGE, 0:chans] = edge_grads[0, EDGE * i : EDGE * (i + 1), :]
        grads[at : at + EDGE, chans:] = edge_grads[1, EDGE * i : EDGE * (i + 1), :]
        grads[at + EDGE : at + 2 * EDGE, chans:] = grad[here + EDGE : here + 2 * EDGE]
    grads[EDGE_PITCH * ext :, :] = jnp.zeros((LANES - EDGE_PITCH * ext, 2 * chans), BF16)
    spread(edge_backward, grads[...], grad_mixed)
    back = contract_last(grad_mixed[...], w_mix[...])
    for part in range(2):
        lines = []
        for i in range(rows):
            at = EDGE_PITCH * (i + 1)
            own = grads[at : at + EDGE_PITCH, chans * part : chans * (part + 1)].astype(F32)[LREACH : LREACH + EDGE]
            here = EDGE * (2 * i + part)
            lines.append(own + back[here : here + EDGE])
        grad_edges[part] = jnp.swapaxes(jnp.stack(lines), 0, 1).astype(BF16)
        store(grad_edges.at[part], field_grad, part * (width - EDGE), EDGE)
    for copy in copies:
        copy.wait()


def on_device(fields, w_mix, filters, reach, w_up, w_down, cotangent):
    rows, width, chans = fields.shape
    step = ceil_to(width, 16)
    ext = rows + 2
    pad = LANES - 3 * PITCH

    def shaped(*shape):
        return jax.ShapeDtypeStruct(shape, BF16)

    turned = shaped(width, rows, chans)
    whole = shaped(rows, width, chans)
    sent = shaped(3 * step + 16, chans)
    edge = shaped((EDGE + LREACH) * rows, chans)
    fields = fields.transpose(1, 0, 2)
    cotangent = cotangent.transpose(1, 0, 2)
    send_c, send_d, taps = call(
        fetch,
        (edge, edge, shaped(rows, 8 * KB, 128)),
        [hbm()] * 4,
        [
            pltpu.VMEM((2, EDGE, rows, chans), BF16),
            pltpu.VMEM((2, LREACH, rows, chans), BF16),
            pltpu.VMEM((KB, 3, rows, TAPS), BF16),
            pltpu.SMEM((rows,), jnp.int32),
            pltpu.VMEM((rows, 8 * KB, 128), F32),
            pltpu.SemaphoreType.DMA((6,)),
        ],
        (1000, 1000000),
        *(
            pltpu.with_memory_space_constraint(x, pltpu.HBM)
            for x in (fields, cotangent, filters.transpose(0, 2, 1, 3), reach)
        ),
    )
    got_c = swap(send_c, "lon", 0)
    got_d = swap(send_d, "lon", 1)
    send_a, send_b, fields, cotangent = call(
        pack_lat, (sent, sent, whole, whole), [vmem()] * 3, [], (2000000000, 5000000), fields, cotangent, taps
    )
    got_a = swap(send_a, "lat", 0)
    got_b = swap_inner_lat(send_b)

    def scratch(lines, out_lines):
        return [
            pltpu.VMEM((PITCH * lines + pad, chans), BF16),
            pltpu.VMEM((LANES, chans), BF16),
            pltpu.VMEM((SPAN * out_lines, KB * chans), BF16),
            pltpu.VMEM((SPAN * out_lines, chans), BF16),
            pltpu.VMEM((SPAN * out_lines, chans), BF16),
        ]

    def bands(count):
        return shaped(count, KB * BLOCK, LANES)

    def edge_bands(count):
        return shaped(count, KB * EDGE, LANES)

    inner_result, inner_grads, inner_forward, inner_backward, inner_edge_forward, inner_edge_backward = call(
        inner_kernel,
        (
            shaped(rows - 2, SPAN, chans),
            shaped(SPAN * (rows - 2), chans),
            bands(rows),
            bands(rows - 2),
            edge_bands(rows),
            edge_bands(rows - 2),
        ),
        [vmem()] * 6 + [pl.BlockSpec(memory_space=pl.ANY)],
        scratch(rows, rows - 2),
        (300000000, 1000000),
        fields, cotangent, taps, w_mix, w_up, w_down, send_a,
    )
    corner = shaped(5 * EDGE, chans)
    corner_a, corner_b = call(
        functools.partial(pack_corners, rows),
        (corner, corner),
        [vmem()] * 2 + [pl.BlockSpec(memory_space=pl.ANY)],
        [],
        (4000000000, 1000000),
        got_d, got_c, inner_result,
    )
    corner_a = swap(corner_a, "lat", 0)
    corner_b = swap_inner_lat(corner_b)
    middle_result, middle_grads, edge_grads, backward, edge_forward, edge_backward, halo = call(
        middle_kernel,
        (
            shaped(rows, SPAN, chans),
            shaped(SPAN * ext + pad, chans),
            shaped(2, EDGE * ext, chans),
            bands(2),
            edge_bands(2),
            edge_bands(2),
            shaped(2, 5 * EDGE, chans),
        ),
        [vmem()] * 12,
        [pltpu.VMEM((2, KB * BLOCK, LANES), BF16)] + scratch(rows + 4, 4),
        (2000000000, 5000000),
        got_a, got_b, fields, cotangent, taps, inner_result, inner_grads, inner_forward, inner_edge_forward,
        w_mix, w_up, w_down,
    )
    result, field_grad = call(
        edge_kernel,
        (turned, turned),
        [vmem()] * 19,
        [
            pltpu.VMEM((LANES, 2 * chans), BF16),
            pltpu.VMEM((2 * EDGE * ext, KB * chans), BF16),
            pltpu.VMEM((2 * EDGE * ext, chans), BF16),
            pltpu.VMEM((2 * EDGE * ext, chans), BF16),
            pltpu.VMEM((LANES, 2 * chans), BF16),
            pltpu.VMEM((2 * EDGE * rows, KB * chans), BF16),
            pltpu.VMEM((2, LREACH, rows, chans), BF16),
            pltpu.VMEM((2, EDGE, rows, chans), BF16),
            pltpu.VMEM((BLOCK * rows, KB * chans), BF16),
            pltpu.VMEM((SPAN, rows, chans), BF16),
            pltpu.VMEM((BLOCK, rows, chans), BF16),
            pltpu.SemaphoreType.DMA((6,)),
        ],
        (500000000, 3000000),
        middle_result, middle_grads, edge_grads, inner_backward, backward, inner_edge_forward, inner_edge_backward, edge_forward, edge_backward,
        halo, send_c, send_d, got_d, got_c, corner_a, corner_b, w_mix, w_up, w_down,
        out_specs=(hbm(), hbm()),
    )
    return result.transpose(1, 0, 2), field_grad.transpose(1, 0, 2)


def solution(mesh):
    return jax.shard_map(
        on_device,
        mesh=mesh,
        in_specs=(
            P("lat", "lon", None),
            P(),
            P(None, "lat", None, None),
            P("lat"),
            P(),
            P(),
            P("lat", "lon", None),
        ),
        out_specs=(P("lat", "lon", None), P("lat", "lon", None)),
        check_vma=False,
    )
```

```python
import functools

import jax
import jax.numpy as jnp
from jax import lax
from jax.experimental import pallas as pl
from jax.experimental.pallas import tpu as pltpu
from jax.sharding import PartitionSpec as P

KB = 4
LREACH = 8
TAPS = 2 * LREACH + 1
BLOCK = 64
PITCH = BLOCK + 2 * LREACH
EDGE = 2 * LREACH
EDGE_PITCH = 2 * EDGE
LANES = 256
TAP_LANES = 128
F32 = jnp.float32
BF16 = jnp.bfloat16
VMEM_BYTES = 48 * 1024 * 1024


def ceil_to(size, unit):
    return -(-size // unit) * unit


def vmem():
    return pl.BlockSpec(memory_space=pltpu.VMEM)


def hbm():
    return pl.BlockSpec(memory_space=pltpu.HBM)


def is_odd(axis):
    return lax.rem(lax.axis_index(axis), 2)


def call(kernel, outs, in_specs, scratch, cost, *args, out_specs=None):
    return pl.pallas_call(
        kernel,
        out_shape=outs,
        in_specs=in_specs,
        out_specs=out_specs or jax.tree.map(lambda _: vmem(), outs),
        scratch_shapes=scratch,
        compiler_params=pltpu.CompilerParams(vmem_limit_bytes=VMEM_BYTES),
        cost_estimate=pl.CostEstimate(flops=cost[0], bytes_accessed=cost[1], transcendentals=0),
    )(*args)


def swap(cells, axis, shift):
    count = lax.axis_size(axis)
    pairs = []
    for first in range(shift, count, 2):
        second = (first + 1) % count
        pairs += [(first, second), (second, first)]
    return lax.ppermute(cells, axis, pairs)


def swap_inner_lat(cells):
    count, around = lax.axis_size("lat"), lax.axis_size("lon")
    pairs = []
    for j in range(around):
        pairs += [(i * around + j, i * around + (j + around // 2) % around) for i in (0, count - 1)]
        for i in range(1, count - 1, 2):
            pairs += [(i * around + j, (i + 1) * around + j), ((i + 1) * around + j, i * around + j)]
    return lax.ppermute(cells, ("lat", "lon"), pairs)


def lat_picker(got_a, got_b):
    top_is_a = is_odd("lat") == 1
    index = lax.axis_index("lat")
    inner = (index > 0) & (index < lax.axis_size("lat") - 1)

    def pick(first, last, top):
        a, b = got_a[first:last, :], got_b[first:last, :]
        return jnp.where(top_is_a == top, a, jnp.where(inner, b, jnp.zeros_like(b)))

    return pick


def fetch(fields, cotangent, filters, reach, send_c, send_d, taps, fields_here, cotangent_here, filters_here, reach_here, raw, sems):
    width, rows, chans = fields.shape
    moves = [(filters, filters_here), (reach, reach_here)]
    for part in range(2):
        moves.append((fields.at[pl.ds(part * (width - EDGE), EDGE)], fields_here.at[part]))
        moves.append((cotangent.at[pl.ds(part * (width - LREACH), LREACH)], cotangent_here.at[part]))
    copies = [pltpu.make_async_copy(src, dst, sems.at[n]) for n, (src, dst) in enumerate(moves)]
    for copy in copies:
        copy.start()
    raw[...] = jnp.zeros(raw.shape, F32)
    offset = jnp.abs(lax.broadcasted_iota(jnp.int32, (8 * KB, 128), 1) - LREACH)
    copies[0].wait()
    copies[1].wait()
    for k in range(KB):
        for a in range(3):
            line = filters_here[k, a].astype(F32)
            for r in range(rows):
                raw[r, 8 * k + a : 8 * k + a + 1, 0:TAPS] = line[r : r + 1]
    for r in range(rows):
        taps[r] = jnp.where(offset <= reach_here[r], raw[r], 0.0).astype(BF16)
    for copy in copies[2:]:
        copy.wait()
    sides = []
    for part in range(2):
        cells = jnp.swapaxes(fields_here[part], 0, 1).reshape(EDGE * rows, chans)
        grads = jnp.swapaxes(cotangent_here[part].astype(F32), 0, 1).reshape(LREACH * rows, chans).astype(BF16)
        sides.append((cells, grads))
    fill_lon(send_c, send_d, *sides)


def fill_lat(send, low, fields, cotangent, taps):
    rows, width, chans = fields.shape
    step = ceil_to(width, 16)
    send[0:width, :] = fields[low * (rows - 2)]
    send[step : step + width, :] = fields[low * (rows - 2) + 1]
    send[2 * step : 2 * step + width, :] = cotangent[low * (rows - 1)]
    own = taps[low * (rows - 1)]
    send[3 * step : 3 * step + 16, 0:128] = own[0:16]
    send[3 * step : 3 * step + 16, 128:256] = own[16:32]


def fill_lon(send_c, send_d, near, far):
    odd = is_odd("lon") == 1
    at = 0
    for first, last in zip(near, far, strict=True):
        size = first.shape[0]
        send_c[at : at + size, :] = jnp.where(odd, first, last)
        send_d[at : at + size, :] = jnp.where(odd, last, first)
        at += size


def pack_lat(fields, cotangent, taps, send_a, send_b, fields_rows, cotangent_rows):
    fields_rows[...] = jnp.swapaxes(fields[...], 0, 1)
    cotangent_rows[...] = jnp.swapaxes(cotangent[...], 0, 1)
    odd = is_odd("lat")
    fill_lat(send_a, 1 - odd, fields_rows, cotangent_rows, taps)
    fill_lat(send_b, odd, fields_rows, cotangent_rows, taps)


def pack_corners(rows, got_d, got_c, inner, send_a, send_b):
    odd = is_odd("lat")
    left_is_c = is_odd("lon") == 1
    for send, low in ((send_a, 1 - odd), (send_b, odd)):
        at = pl.multiple_of(low * (rows - 2) * EDGE, EDGE)
        c, d = got_c[pl.ds(at, 2 * EDGE), :], got_d[pl.ds(at, 2 * EDGE), :]
        send[0 : 2 * EDGE, :] = jnp.where(left_is_c, c, d)
        send[2 * EDGE : 4 * EDGE, :] = jnp.where(left_is_c, d, c)
        first, last = EDGE * rows, (EDGE + LREACH) * rows
        c, d = [
            jnp.where(low == 1, x[last - EDGE : last, :].astype(F32)[LREACH:], x[first : first + EDGE, :].astype(F32)[0:LREACH])
            for x in (got_c, got_d)
        ]
        both = [jnp.where(left_is_c, c, d), jnp.where(left_is_c, d, c)]
        send[4 * EDGE : 5 * EDGE, :] = jnp.concatenate(both, axis=0).astype(BF16)


def lay_taps(every, pitch, lanes):
    groups = every.shape[0] // 8

    def places(shape, dim):
        col = lax.broadcasted_iota(jnp.int32, shape, dim)
        turned = col >= lanes
        inner = jnp.where(turned, col - lanes, col)
        part = jnp.where(inner >= pitch, 1, 0) + jnp.where(inner >= 2 * pitch, 1, 0)
        return turned, inner - pitch * part, part

    turned, place, _ = places((128, 2 * lanes), 1)
    tap = lax.broadcasted_iota(jnp.int32, (128, 2 * lanes), 0)
    wanted = jnp.where(turned, 2 * LREACH - place, place)
    table = jnp.where((tap == wanted) & (tap < TAPS), 1.0, 0.0).astype(BF16)
    spread = jnp.dot(every, table, preferred_element_type=F32).reshape(groups, 8, 2 * lanes)
    turned, _, part = places((groups, 8, 2 * lanes), 2)
    lat_tap = lax.broadcasted_iota(jnp.int32, (groups, 8, 2 * lanes), 1)
    chosen = jnp.where(turned, 2 - part, part) == lat_tap
    return jnp.sum(jnp.where(chosen, spread, 0.0), axis=1)


def slant(line, size, shift):
    lanes = line.shape[1]
    return pltpu.roll(jnp.broadcast_to(line, (size, lanes)), shift, 1, stride=1, stride_axis=0).astype(BF16)


def build_bands(every, size, pitch, first, forward, forward_rows, backward, backward_rows):
    edge = size == EDGE
    lanes = TAP_LANES if edge else LANES
    lines = lay_taps(every, pitch, lanes)
    lane = lax.broadcasted_iota(jnp.int32, (1, lanes), 1)

    def lean(line, row):
        if edge:
            line = jnp.concatenate([line, jnp.zeros((1, LANES - lanes), F32)], axis=1)
        return slant(line, size, pitch * row if edge else 0)

    for place, i in enumerate(forward_rows):
        for k in range(KB):
            at = KB * i + k
            forward[place, size * k : size * (k + 1), :] = lean(lines[at : at + 1, 0:lanes], i + first)
    for place, i in enumerate(backward_rows):
        for k in range(KB):
            near = [lines[KB * (i + t - 1) + k : KB * (i + t - 1) + k + 1, lanes:] for t in range(3)]
            line = jnp.where(lane < pitch, near[0], jnp.where(lane < 2 * pitch, near[1], near[2]))
            backward[place, size * k : size * (k + 1), :] = lean(line, i + first - 1)


def gelu_parts(pre):
    size = jnp.abs(pre)
    bell = jnp.exp(-0.5 * pre * pre)
    t = 1.0 / (1.0 + 0.23164188836 * size)
    poly = t * (0.127414796 + t * (-0.142248368 + t * (0.7107068705 + t * (-0.7265760135 + t * 0.5307027145))))
    tail = poly * bell
    cdf = jnp.where(pre >= 0.0, 1.0 - tail, tail)
    return pre * cdf, cdf + pre * bell * 0.3989422804014327


def contract_last(left, right):
    return lax.dot_general(left, right, (((1,), (1,)), ((), ())), preferred_element_type=F32)


def mlp(hidden, upstream, w_up, w_down, first, last):
    arriving = contract_last(upstream[...], w_down[...])
    pre = jnp.dot(hidden[...], w_up[...], preferred_element_type=F32)
    active, slope = gelu_parts(pre)
    grad = (upstream[...].astype(F32) + contract_last((arriving * slope).astype(BF16), w_up[...])).astype(BF16)
    out = hidden[first:last, :].astype(F32) + jnp.dot(
        active[first:last].astype(BF16), w_down[...], preferred_element_type=F32
    )
    return out, grad


SPAN = BLOCK + EDGE


def middle_rows(lines, start, cotangents, bands, edge_bands, firsts, w_mix, w_up, w_down, out_rows, scratch):
    wide, narrow, basis, hidden, upstream = scratch
    chans = w_up.shape[0]
    width = lines[0].shape[0]
    fill = PITCH + EDGE - width
    if start:
        narrow[...] = jnp.zeros(narrow.shape, BF16)
    for f, line in enumerate(lines):
        wide[PITCH * f : PITCH * (f + 1), :] = line[0:PITCH]
        tail = jnp.concatenate([line[BLOCK:].astype(F32), jnp.zeros((fill, chans), F32)], axis=0)
        narrow[EDGE_PITCH * (start + f) : EDGE_PITCH * (start + f + 1), :] = tail.astype(BF16)
    wide[PITCH * len(lines) :, :] = jnp.zeros((LANES - 3 * PITCH, chans), BF16)
    others = jnp.dot(jnp.concatenate(edge_bands, axis=0), narrow[...], preferred_element_type=F32).astype(BF16)
    for n, f in enumerate(firsts):
        at = SPAN * n
        moved = jnp.dot(bands[n], wide[PITCH * f : PITCH * f + LANES, :], preferred_element_type=F32).astype(BF16)
        other = others[KB * EDGE * n : KB * EDGE * (n + 1)]
        for k in range(KB):
            basis[at : at + BLOCK, chans * k : chans * (k + 1)] = moved[BLOCK * k : BLOCK * (k + 1)]
            basis[at + BLOCK : at + SPAN, chans * k : chans * (k + 1)] = other[EDGE * k : EDGE * (k + 1)]
    stacked = jnp.concatenate([w_mix[:, chans * k : chans * (k + 1)] for k in range(KB)], axis=0)
    spatial = jnp.dot(basis[...], stacked, preferred_element_type=F32)
    for n, f in enumerate(firsts):
        at = PITCH * (f + 1)
        first = wide[at : at + PITCH, :].astype(F32)[LREACH : LREACH + BLOCK]
        at = EDGE_PITCH * (start + f + 1)
        second = narrow[at : at + EDGE_PITCH, :].astype(F32)[LREACH : LREACH + EDGE]
        here = SPAN * n
        mine = jnp.concatenate([first, second], axis=0) + spatial[here : here + SPAN]
        hidden[here : here + SPAN, :] = mine.astype(BF16)
        upstream[here : here + SPAN, :] = cotangents[n].astype(F32)[LREACH : LREACH + SPAN].astype(BF16)
    return mlp(hidden, upstream, w_up, w_down, SPAN * out_rows[0], SPAN * out_rows[1])


def inner_kernel(
    fields, cotangent, taps, w_mix, w_up, w_down, sent,
    result, grads, forward, backward, edge_forward, edge_backward, *scratch,
):
    rows = fields.shape[0]
    every = jnp.concatenate([taps[r] for r in range(rows)], axis=0)
    own, inner = range(rows), range(1, rows - 1)
    build_bands(every, BLOCK, PITCH, 1, forward, own, backward, inner)
    build_bands(every, EDGE, EDGE_PITCH, 1, edge_forward, own, edge_backward, inner)
    out, grad = middle_rows(
        [fields[r] for r in own],
        2,
        [cotangent[r] for r in inner],
        [forward[r] for r in inner],
        [edge_forward[r] for r in inner],
        [r - 1 for r in inner],
        w_mix, w_up, w_down, (0, rows - 2), scratch,
    )
    result[...] = out.reshape(result.shape).astype(BF16)
    grads[...] = grad


def middle_kernel(
    got_a, got_b, fields, cotangent, taps, inner_result, inner_grads, inner_forward, inner_backward,
    inner_edge_forward, w_mix, w_up, w_down,
    result, grads, grad_mixed, edge_grads, edge_forward, edge_backward, halo,
    forward, backward, *scratch,
):
    rows, width, chans = fields.shape
    step = ceil_to(width, 16)
    pick = lat_picker(got_a, got_b)
    ext = rows + 2

    def taps_of(top):
        both = pick(3 * step, 3 * step + 16, top)
        return [both[:, 0:128], both[:, 128:256]]

    for part, (fields_at, cotangent_at) in enumerate(((0, 0), (width - EDGE, width - LREACH))):
        cells = [
            pick(step * n, step * n + width, top).astype(F32)[fields_at : fields_at + EDGE]
            for top in (True, False)
            for n in range(2)
        ]
        cells += [
            pick(2 * step, 2 * step + width, top).astype(F32)[cotangent_at : cotangent_at + LREACH] for top in (True, False)
        ]
        halo[part] = jnp.concatenate(cells, axis=0).astype(BF16)

    every = jnp.concatenate(taps_of(True) + [taps[r] for r in range(rows)] + taps_of(False), axis=0)
    ends = (0, ext - 1), (1, rows)
    build_bands(every, BLOCK, PITCH, 0, forward, ends[0], backward, ends[1])
    build_bands(every, EDGE, EDGE_PITCH, 0, edge_forward, ends[0], edge_backward, ends[1])

    lines = [pick(step * n, step * n + width, True) for n in range(2)]
    lines += [fields[r] for r in range(rows)]
    lines += [pick(step * n, step * n + width, False) for n in range(2)]
    out, grad = middle_rows(
        lines,
        0,
        [pick(2 * step, 2 * step + width, True), cotangent[0], cotangent[rows - 1], pick(2 * step, 2 * step + width, False)],
        [forward[0], inner_forward[0], inner_forward[rows - 1], forward[1]],
        [edge_forward[0], inner_edge_forward[0], inner_edge_forward[rows - 1], edge_forward[1]],
        [0, 1, ext - 2, ext - 1],
        w_mix, w_up, w_down, (1, 3), scratch,
    )
    lines = [out[0:SPAN].astype(BF16)] + [inner_result[r] for r in range(rows - 2)] + [out[SPAN:].astype(BF16)]
    result[...] = jnp.swapaxes(jnp.stack(lines), 0, 1)
    grads[0 : 2 * SPAN, :] = grad[0 : 2 * SPAN]
    grads[2 * SPAN : (ext - 2) * SPAN, :] = inner_grads[...]
    grads[(ext - 2) * SPAN : ext * SPAN, :] = grad[2 * SPAN :]
    grads[SPAN * ext :, :] = jnp.zeros((LANES - 3 * PITCH, chans), BF16)
    far = width - EDGE - 2 * LREACH
    for i in range(ext):
        mine = grads[SPAN * i : SPAN * (i + 1), :]
        edge_grads[0, EDGE * i : EDGE * (i + 1), :] = mine[0:EDGE]
        edge_grads[1, EDGE * i : EDGE * (i + 1), :] = mine.astype(F32)[far : far + EDGE].astype(BF16)

    bands = [backward[0]] + [inner_backward[r] for r in range(rows - 2)] + [backward[1]]
    for i in range(rows):
        moved = jnp.dot(bands[i], grads[PITCH * i : PITCH * i + LANES, :], preferred_element_type=F32).astype(BF16)
        for k in range(KB):
            grad_mixed[BLOCK * i : BLOCK * (i + 1), chans * k : chans * (k + 1)] = moved[BLOCK * k : BLOCK * (k + 1)]


def edge_kernel(
    middle_result, middle_grads, middle_grad_mixed, edge_grads, inner_edge_forward, inner_edge_backward, end_edge_forward, end_edge_backward,
    halo, send_c, send_d, got_d, got_c, corner_a, corner_b, w_mix, w_up, w_down,
    result, field_grad, source, basis, hidden, upstream, grads, grad_mixed, result_edges, grad_edges, turned_grad, sems,
):
    width, rows, chans = result.shape
    ext = rows + 2
    copies = []

    def store(here, out, first, size):
        copies.append(pltpu.make_async_copy(here.at[pl.ds(0, size)], out.at[pl.ds(first, size)], sems.at[len(copies)]))
        copies[-1].start()

    store(middle_result, result, LREACH, width - 2 * LREACH)
    left_is_c = is_odd("lon") == 1
    edge_forward = [end_edge_forward[0]] + [inner_edge_forward[r] for r in range(rows)] + [end_edge_forward[1]]
    edge_backward = [end_edge_backward[0]] + [inner_edge_backward[r] for r in range(rows - 2)] + [end_edge_backward[1]]
    pick = lat_picker(corner_a, corner_b)

    def own_cells(at):
        sent_c, sent_d, came_c, came_d = [x[at : at + EDGE, :] for x in (send_c, send_d, got_c, got_d)]
        return (
            jnp.where(left_is_c, came_c, came_d),
            jnp.where(left_is_c, sent_c, sent_d),
            jnp.where(left_is_c, sent_d, sent_c),
            jnp.where(left_is_c, came_d, came_c),
        )

    for i in range(rows + 4):
        if 2 <= i < rows + 2:
            cells = own_cells(EDGE * (i - 2))
        else:
            top = i < 2
            n = i if top else i - rows - 2
            at = EDGE * (i if top else i - rows)
            left, right = [pick(EDGE * m, EDGE * (m + 1), top) for m in (n, n + 2)]
            cells = left, halo[0, at : at + EDGE, :], halo[1, at : at + EDGE, :], right
        at = EDGE_PITCH * i
        source[at : at + EDGE, 0:chans] = cells[0]
        source[at + EDGE : at + 2 * EDGE, 0:chans] = cells[1]
        source[at : at + EDGE, chans:] = cells[2]
        source[at + EDGE : at + 2 * EDGE, chans:] = cells[3]

    for i in range(ext):
        if 0 < i < ext - 1:
            inside = LREACH * ((i - 1) % 2)
            cells = own_cells(EDGE * rows + EDGE * ((i - 1) // 2))
            cells = [x.astype(F32)[inside : inside + LREACH] for x in cells]
        else:
            inside = 0 if i == 0 else LREACH
            near, far = [halo[part, 4 * EDGE : 5 * EDGE, :].astype(F32)[inside : inside + LREACH] for part in range(2)]
            both = pick(4 * EDGE, 5 * EDGE, i == 0).astype(F32)
            cells = both[0:LREACH], near, far, both[LREACH:]
        here = 2 * EDGE * i
        upstream[here : here + EDGE, :] = jnp.concatenate(cells[0:2], axis=0).astype(BF16)
        upstream[here + EDGE : here + 2 * EDGE, :] = jnp.concatenate(cells[2:4], axis=0).astype(BF16)

    def spread(bands, cells, out):
        moved = jnp.dot(jnp.concatenate(bands, axis=0), cells, preferred_element_type=F32).astype(BF16)
        for i in range(len(bands)):
            for part in range(2):
                at = EDGE * (2 * i + part)
                for k in range(KB):
                    here = EDGE * (KB * i + k)
                    out[at : at + EDGE, chans * k : chans * (k + 1)] = moved[
                        here : here + EDGE, chans * part : chans * (part + 1)
                    ]

    spread(edge_forward, source[...], basis)
    stacked = jnp.concatenate([w_mix[:, chans * k : chans * (k + 1)] for k in range(KB)], axis=0)
    spatial = jnp.dot(basis[...], stacked, preferred_element_type=F32)
    for i in range(ext):
        at = EDGE_PITCH * (i + 1)
        cells = source[at : at + EDGE_PITCH, :].astype(F32)[LREACH : LREACH + EDGE]
        for part in range(2):
            here = EDGE * (2 * i + part)
            hidden[here : here + EDGE, :] = (
                cells[:, chans * part : chans * (part + 1)] + spatial[here : here + EDGE]
            ).astype(BF16)
    out, grad = mlp(hidden, upstream, w_up, w_down, 2 * EDGE, 2 * EDGE * (rows + 1))
    for i in range(ext):
        at = EDGE_PITCH * i
        here = 2 * EDGE * i
        grads[at : at + EDGE, 0:chans] = grad[here : here + EDGE]
        grads[at + EDGE : at + 2 * EDGE, 0:chans] = edge_grads[0, EDGE * i : EDGE * (i + 1), :]
        grads[at : at + EDGE, chans:] = edge_grads[1, EDGE * i : EDGE * (i + 1), :]
        grads[at + EDGE : at + 2 * EDGE, chans:] = grad[here + EDGE : here + 2 * EDGE]
    grads[EDGE_PITCH * ext :, :] = jnp.zeros((LANES - EDGE_PITCH * ext, 2 * chans), BF16)
    back = contract_last(middle_grad_mixed[...], w_mix[...])
    lines = []
    for i in range(rows):
        at = PITCH * (i + 1)
        own = middle_grads[at : at + PITCH, :].astype(F32)[LREACH : LREACH + BLOCK]
        lines.append((own + back[BLOCK * i : BLOCK * (i + 1)]).astype(BF16))
    turned_grad[...] = jnp.swapaxes(jnp.stack(lines), 0, 1)
    store(turned_grad, field_grad, EDGE, width - 2 * EDGE)
    spread(edge_backward, grads[...], grad_mixed)
    back = contract_last(grad_mixed[...], w_mix[...])
    for part in range(2):
        inside = 0 if part else LREACH
        lines = [out[at + inside : at + inside + LREACH] for at in (EDGE * (2 * i + part) for i in range(rows))]
        result_edges[part] = jnp.swapaxes(jnp.stack(lines), 0, 1).astype(BF16)
        store(result_edges.at[part], result, part * (width - LREACH), LREACH)

    for part in range(2):
        lines = []
        for i in range(rows):
            at = EDGE_PITCH * (i + 1)
            own = grads[at : at + EDGE_PITCH, chans * part : chans * (part + 1)].astype(F32)[LREACH : LREACH + EDGE]
            here = EDGE * (2 * i + part)
            lines.append(own + back[here : here + EDGE])
        grad_edges[part] = jnp.swapaxes(jnp.stack(lines), 0, 1).astype(BF16)
        store(grad_edges.at[part], field_grad, part * (width - EDGE), EDGE)
    for copy in copies:
        copy.wait()


def on_device(fields, w_mix, filters, reach, w_up, w_down, cotangent):
    rows, width, chans = fields.shape
    step = ceil_to(width, 16)
    ext = rows + 2
    pad = LANES - 3 * PITCH

    def shaped(*shape):
        return jax.ShapeDtypeStruct(shape, BF16)

    turned = shaped(width, rows, chans)
    whole = shaped(rows, width, chans)
    sent = shaped(3 * step + 16, chans)
    edge = shaped((EDGE + LREACH) * rows, chans)
    fields = fields.transpose(1, 0, 2)
    cotangent = cotangent.transpose(1, 0, 2)
    send_c, send_d, taps = call(
        fetch,
        (edge, edge, shaped(rows, 8 * KB, 128)),
        [hbm()] * 4,
        [
            pltpu.VMEM((2, EDGE, rows, chans), BF16),
            pltpu.VMEM((2, LREACH, rows, chans), BF16),
            pltpu.VMEM((KB, 3, rows, TAPS), BF16),
            pltpu.SMEM((rows,), jnp.int32),
            pltpu.VMEM((rows, 8 * KB, 128), F32),
            pltpu.SemaphoreType.DMA((6,)),
        ],
        (1000, 1000000),
        *(
            pltpu.with_memory_space_constraint(x, pltpu.HBM)
            for x in (fields, cotangent, filters.transpose(0, 2, 1, 3), reach)
        ),
    )
    got_c = swap(send_c, "lon", 0)
    got_d = swap(send_d, "lon", 1)
    send_a, send_b, fields, cotangent = call(
        pack_lat, (sent, sent, whole, whole), [vmem()] * 3, [], (2000000000, 5000000), fields, cotangent, taps
    )
    got_a = swap(send_a, "lat", 0)
    got_b = swap_inner_lat(send_b)

    def scratch(lines, out_lines):
        return [
            pltpu.VMEM((PITCH * lines + pad, chans), BF16),
            pltpu.VMEM((LANES, chans), BF16),
            pltpu.VMEM((SPAN * out_lines, KB * chans), BF16),
            pltpu.VMEM((SPAN * out_lines, chans), BF16),
            pltpu.VMEM((SPAN * out_lines, chans), BF16),
        ]

    def bands(count):
        return shaped(count, KB * BLOCK, LANES)

    def edge_bands(count):
        return shaped(count, KB * EDGE, LANES)

    inner_result, inner_grads, inner_forward, inner_backward, inner_edge_forward, inner_edge_backward = call(
        inner_kernel,
        (
            shaped(rows - 2, SPAN, chans),
            shaped(SPAN * (rows - 2), chans),
            bands(rows),
            bands(rows - 2),
            edge_bands(rows),
            edge_bands(rows - 2),
        ),
        [vmem()] * 6 + [pl.BlockSpec(memory_space=pl.ANY)],
        scratch(rows, rows - 2),
        (300000000, 1000000),
        fields, cotangent, taps, w_mix, w_up, w_down, send_a,
    )
    corner = shaped(5 * EDGE, chans)
    corner_a, corner_b = call(
        functools.partial(pack_corners, rows),
        (corner, corner),
        [vmem()] * 2 + [pl.BlockSpec(memory_space=pl.ANY)],
        [],
        (4000000000, 1000000),
        got_d, got_c, inner_result,
    )
    corner_a = swap(corner_a, "lat", 0)
    corner_b = swap_inner_lat(corner_b)
    middle_result, middle_grads, middle_grad_mixed, edge_grads, edge_forward, edge_backward, halo = call(
        middle_kernel,
        (
            shaped(SPAN, rows, chans),
            shaped(SPAN * ext + pad, chans),
            shaped(BLOCK * rows, KB * chans),
            shaped(2, EDGE * ext, chans),
            edge_bands(2),
            edge_bands(2),
            shaped(2, 5 * EDGE, chans),
        ),
        [vmem()] * 13,
        [pltpu.VMEM((2, KB * BLOCK, LANES), BF16), pltpu.VMEM((2, KB * BLOCK, LANES), BF16)] + scratch(rows + 4, 4),
        (2000000000, 5000000),
        got_a, got_b, fields, cotangent, taps, inner_result, inner_grads, inner_forward, inner_backward,
        inner_edge_forward, w_mix, w_up, w_down,
    )
    result, field_grad = call(
        edge_kernel,
        (turned, turned),
        [vmem()] * 18,
        [
            pltpu.VMEM((LANES, 2 * chans), BF16),
            pltpu.VMEM((2 * EDGE * ext, KB * chans), BF16),
            pltpu.VMEM((2 * EDGE * ext, chans), BF16),
            pltpu.VMEM((2 * EDGE * ext, chans), BF16),
            pltpu.VMEM((LANES, 2 * chans), BF16),
            pltpu.VMEM((2 * EDGE * rows, KB * chans), BF16),
            pltpu.VMEM((2, LREACH, rows, chans), BF16),
            pltpu.VMEM((2, EDGE, rows, chans), BF16),
            pltpu.VMEM((BLOCK, rows, chans), BF16),
            pltpu.SemaphoreType.DMA((6,)),
        ],
        (500000000, 3000000),
        middle_result, middle_grads, middle_grad_mixed, edge_grads, inner_edge_forward, inner_edge_backward, edge_forward, edge_backward,
        halo, send_c, send_d, got_d, got_c, corner_a, corner_b, w_mix, w_up, w_down,
        out_specs=(hbm(), hbm()),
    )
    return result.transpose(1, 0, 2), field_grad.transpose(1, 0, 2)


def solution(mesh):
    return jax.shard_map(
        on_device,
        mesh=mesh,
        in_specs=(
            P("lat", "lon", None),
            P(),
            P(None, "lat", None, None),
            P("lat"),
            P(),
            P(),
            P("lat", "lon", None),
        ),
        out_specs=(P("lat", "lon", None), P("lat", "lon", None)),
        check_vma=False,
    )
```

```python
import functools

import jax
import jax.numpy as jnp
from jax import lax
from jax.experimental import pallas as pl
from jax.experimental.pallas import tpu as pltpu
from jax.sharding import PartitionSpec as P

KB = 4
LREACH = 8
TAPS = 2 * LREACH + 1
BLOCK = 64
PITCH = BLOCK + 2 * LREACH
EDGE = 2 * LREACH
EDGE_PITCH = 2 * EDGE
LANES = 256
TAP_LANES = 128
F32 = jnp.float32
BF16 = jnp.bfloat16
VMEM_BYTES = 48 * 1024 * 1024


def ceil_to(size, unit):
    return -(-size // unit) * unit


def vmem():
    return pl.BlockSpec(memory_space=pltpu.VMEM)


def hbm():
    return pl.BlockSpec(memory_space=pltpu.HBM)


def is_odd(axis):
    return lax.rem(lax.axis_index(axis), 2)


def call(kernel, outs, in_specs, scratch, cost, *args, out_specs=None):
    return pl.pallas_call(
        kernel,
        out_shape=outs,
        in_specs=in_specs,
        out_specs=out_specs or jax.tree.map(lambda _: vmem(), outs),
        scratch_shapes=scratch,
        compiler_params=pltpu.CompilerParams(vmem_limit_bytes=VMEM_BYTES),
        cost_estimate=pl.CostEstimate(flops=cost[0], bytes_accessed=cost[1], transcendentals=0),
    )(*args)


def swap(cells, axis, shift):
    count = lax.axis_size(axis)
    pairs = []
    for first in range(shift, count, 2):
        second = (first + 1) % count
        pairs += [(first, second), (second, first)]
    return lax.ppermute(cells, axis, pairs)


def swap_inner_lat(cells):
    count, around = lax.axis_size("lat"), lax.axis_size("lon")
    pairs = []
    for j in range(around):
        pairs += [(i * around + j, i * around + (j + around // 2) % around) for i in (0, count - 1)]
        for i in range(1, count - 1, 2):
            pairs += [(i * around + j, (i + 1) * around + j), ((i + 1) * around + j, i * around + j)]
    return lax.ppermute(cells, ("lat", "lon"), pairs)


def lat_picker(got_a, got_b):
    top_is_a = is_odd("lat") == 1
    index = lax.axis_index("lat")
    inner = (index > 0) & (index < lax.axis_size("lat") - 1)

    def pick(first, last, top):
        a, b = got_a[first:last, :], got_b[first:last, :]
        return jnp.where(top_is_a == top, a, jnp.where(inner, b, jnp.zeros_like(b)))

    return pick


def fetch(fields, cotangent, filters, reach, send_c, send_d, taps, fields_here, cotangent_here, filters_here, reach_here, raw, sems):
    width, rows, chans = fields.shape
    moves = [(filters, filters_here), (reach, reach_here)]
    for part in range(2):
        moves.append((fields.at[pl.ds(part * (width - EDGE), EDGE)], fields_here.at[part]))
        moves.append((cotangent.at[pl.ds(part * (width - LREACH), LREACH)], cotangent_here.at[part]))
    copies = [pltpu.make_async_copy(src, dst, sems.at[n]) for n, (src, dst) in enumerate(moves)]
    for copy in copies:
        copy.start()
    raw[...] = jnp.zeros(raw.shape, F32)
    offset = jnp.abs(lax.broadcasted_iota(jnp.int32, (8 * KB, 128), 1) - LREACH)
    copies[0].wait()
    copies[1].wait()
    for k in range(KB):
        for a in range(3):
            line = filters_here[k, a].astype(F32)
            for r in range(rows):
                raw[r, 8 * k + a : 8 * k + a + 1, 0:TAPS] = line[r : r + 1]
    for r in range(rows):
        taps[r] = jnp.where(offset <= reach_here[r], raw[r], 0.0).astype(BF16)
    for copy in copies[2:]:
        copy.wait()
    sides = []
    for part in range(2):
        cells = jnp.swapaxes(fields_here[part], 0, 1).reshape(EDGE * rows, chans)
        grads = jnp.swapaxes(cotangent_here[part].astype(F32), 0, 1).reshape(LREACH * rows, chans).astype(BF16)
        sides.append((cells, grads))
    fill_lon(send_c, send_d, *sides)


def fill_lat(send, low, fields, cotangent, taps):
    rows, width, chans = fields.shape
    step = ceil_to(width, 16)
    send[0:width, :] = fields[low * (rows - 2)]
    send[step : step + width, :] = fields[low * (rows - 2) + 1]
    send[2 * step : 2 * step + width, :] = cotangent[low * (rows - 1)]
    own = taps[low * (rows - 1)]
    send[3 * step : 3 * step + 16, 0:128] = own[0:16]
    send[3 * step : 3 * step + 16, 128:256] = own[16:32]


def fill_lon(send_c, send_d, near, far):
    odd = is_odd("lon") == 1
    at = 0
    for first, last in zip(near, far, strict=True):
        size = first.shape[0]
        send_c[at : at + size, :] = jnp.where(odd, first, last)
        send_d[at : at + size, :] = jnp.where(odd, last, first)
        at += size


def pack_lat(fields, cotangent, taps, send_a, send_b, fields_rows, cotangent_rows):
    fields_rows[...] = jnp.swapaxes(fields[...], 0, 1)
    cotangent_rows[...] = jnp.swapaxes(cotangent[...], 0, 1)
    odd = is_odd("lat")
    fill_lat(send_a, 1 - odd, fields_rows, cotangent_rows, taps)
    fill_lat(send_b, odd, fields_rows, cotangent_rows, taps)


def pack_corners(rows, got_d, got_c, inner, send_a, send_b):
    odd = is_odd("lat")
    left_is_c = is_odd("lon") == 1
    for send, low in ((send_a, 1 - odd), (send_b, odd)):
        at = pl.multiple_of(low * (rows - 2) * EDGE, EDGE)
        c, d = got_c[pl.ds(at, 2 * EDGE), :], got_d[pl.ds(at, 2 * EDGE), :]
        send[0 : 2 * EDGE, :] = jnp.where(left_is_c, c, d)
        send[2 * EDGE : 4 * EDGE, :] = jnp.where(left_is_c, d, c)
        first, last = EDGE * rows, (EDGE + LREACH) * rows
        c, d = [
            jnp.where(low == 1, x[last - EDGE : last, :].astype(F32)[LREACH:], x[first : first + EDGE, :].astype(F32)[0:LREACH])
            for x in (got_c, got_d)
        ]
        both = [jnp.where(left_is_c, c, d), jnp.where(left_is_c, d, c)]
        send[4 * EDGE : 5 * EDGE, :] = jnp.concatenate(both, axis=0).astype(BF16)


def lay_taps(every, pitch, lanes):
    groups = every.shape[0] // 8

    def places(shape, dim):
        col = lax.broadcasted_iota(jnp.int32, shape, dim)
        turned = col >= lanes
        inner = jnp.where(turned, col - lanes, col)
        part = jnp.where(inner >= pitch, 1, 0) + jnp.where(inner >= 2 * pitch, 1, 0)
        return turned, inner - pitch * part, part

    turned, place, _ = places((128, 2 * lanes), 1)
    tap = lax.broadcasted_iota(jnp.int32, (128, 2 * lanes), 0)
    wanted = jnp.where(turned, 2 * LREACH - place, place)
    table = jnp.where((tap == wanted) & (tap < TAPS), 1.0, 0.0).astype(BF16)
    spread = jnp.dot(every, table, preferred_element_type=F32).reshape(groups, 8, 2 * lanes)
    turned, _, part = places((groups, 8, 2 * lanes), 2)
    lat_tap = lax.broadcasted_iota(jnp.int32, (groups, 8, 2 * lanes), 1)
    chosen = jnp.where(turned, 2 - part, part) == lat_tap
    return jnp.sum(jnp.where(chosen, spread, 0.0), axis=1)


def slant(line, size, shift):
    lanes = line.shape[1]
    return pltpu.roll(jnp.broadcast_to(line, (size, lanes)), shift, 1, stride=1, stride_axis=0).astype(BF16)


def build_bands(every, size, pitch, first, forward, forward_rows, backward, backward_rows):
    edge = size == EDGE
    lanes = TAP_LANES if edge else LANES
    lines = lay_taps(every, pitch, lanes)
    lane = lax.broadcasted_iota(jnp.int32, (1, lanes), 1)

    def lean(line, row):
        if edge:
            line = jnp.concatenate([line, jnp.zeros((1, LANES - lanes), F32)], axis=1)
        return slant(line, size, pitch * row if edge else 0)

    for place, i in enumerate(forward_rows):
        for k in range(KB):
            at = KB * i + k
            forward[place, size * k : size * (k + 1), :] = lean(lines[at : at + 1, 0:lanes], i + first)
    for place, i in enumerate(backward_rows):
        for k in range(KB):
            near = [lines[KB * (i + t - 1) + k : KB * (i + t - 1) + k + 1, lanes:] for t in range(3)]
            line = jnp.where(lane < pitch, near[0], jnp.where(lane < 2 * pitch, near[1], near[2]))
            backward[place, size * k : size * (k + 1), :] = lean(line, i + first - 1)


def gelu_parts(pre):
    size = jnp.abs(pre)
    bell = jnp.exp(-0.5 * pre * pre)
    t = 1.0 / (1.0 + 0.23164188836 * size)
    poly = t * (0.127414796 + t * (-0.142248368 + t * (0.7107068705 + t * (-0.7265760135 + t * 0.5307027145))))
    tail = poly * bell
    cdf = jnp.where(pre >= 0.0, 1.0 - tail, tail)
    return pre * cdf, cdf + pre * bell * 0.3989422804014327


def contract_last(left, right):
    return lax.dot_general(left, right, (((1,), (1,)), ((), ())), preferred_element_type=F32)


def mlp(hidden, upstream, w_up, w_down, first, last):
    arriving = contract_last(upstream[...], w_down[...])
    pre = jnp.dot(hidden[...], w_up[...], preferred_element_type=F32)
    active, slope = gelu_parts(pre)
    grad = (upstream[...].astype(F32) + contract_last((arriving * slope).astype(BF16), w_up[...])).astype(BF16)
    out = hidden[first:last, :].astype(F32) + jnp.dot(
        active[first:last].astype(BF16), w_down[...], preferred_element_type=F32
    )
    return out, grad


SPAN = BLOCK + EDGE


def middle_rows(lines, start, cotangents, bands, edge_bands, firsts, w_mix, w_up, w_down, out_rows, scratch):
    wide, narrow, basis, hidden, upstream = scratch
    chans = w_up.shape[0]
    width = lines[0].shape[0]
    fill = PITCH + EDGE - width
    if start:
        narrow[...] = jnp.zeros(narrow.shape, BF16)
    for f, line in enumerate(lines):
        wide[PITCH * f : PITCH * (f + 1), :] = line[0:PITCH]
        tail = jnp.concatenate([line[BLOCK:].astype(F32), jnp.zeros((fill, chans), F32)], axis=0)
        narrow[EDGE_PITCH * (start + f) : EDGE_PITCH * (start + f + 1), :] = tail.astype(BF16)
    wide[PITCH * len(lines) :, :] = jnp.zeros((LANES - 3 * PITCH, chans), BF16)
    others = jnp.dot(jnp.concatenate(edge_bands, axis=0), narrow[...], preferred_element_type=F32).astype(BF16)
    for n, f in enumerate(firsts):
        at = SPAN * n
        moved = jnp.dot(bands[n], wide[PITCH * f : PITCH * f + LANES, :], preferred_element_type=F32).astype(BF16)
        other = others[KB * EDGE * n : KB * EDGE * (n + 1)]
        for k in range(KB):
            basis[at : at + BLOCK, chans * k : chans * (k + 1)] = moved[BLOCK * k : BLOCK * (k + 1)]
            basis[at + BLOCK : at + SPAN, chans * k : chans * (k + 1)] = other[EDGE * k : EDGE * (k + 1)]
    stacked = jnp.concatenate([w_mix[:, chans * k : chans * (k + 1)] for k in range(KB)], axis=0)
    spatial = jnp.dot(basis[...], stacked, preferred_element_type=F32)
    for n, f in enumerate(firsts):
        at = PITCH * (f + 1)
        first = wide[at : at + PITCH, :].astype(F32)[LREACH : LREACH + BLOCK]
        at = EDGE_PITCH * (start + f + 1)
        second = narrow[at : at + EDGE_PITCH, :].astype(F32)[LREACH : LREACH + EDGE]
        here = SPAN * n
        mine = jnp.concatenate([first, second], axis=0) + spatial[here : here + SPAN]
        hidden[here : here + SPAN, :] = mine.astype(BF16)
        upstream[here : here + SPAN, :] = cotangents[n].astype(F32)[LREACH : LREACH + SPAN].astype(BF16)
    return mlp(hidden, upstream, w_up, w_down, SPAN * out_rows[0], SPAN * out_rows[1])


def inner_kernel(
    fields, cotangent, taps, w_mix, w_up, w_down, sent,
    result, grads, forward, backward, edge_forward, edge_backward, *scratch,
):
    rows = fields.shape[0]
    every = jnp.concatenate([taps[r] for r in range(rows)], axis=0)
    own, inner = range(rows), range(1, rows - 1)
    build_bands(every, BLOCK, PITCH, 1, forward, own, backward, inner)
    build_bands(every, EDGE, EDGE_PITCH, 1, edge_forward, own, edge_backward, inner)
    out, grad = middle_rows(
        [fields[r] for r in own],
        2,
        [cotangent[r] for r in inner],
        [forward[r] for r in inner],
        [edge_forward[r] for r in inner],
        [r - 1 for r in inner],
        w_mix, w_up, w_down, (0, rows - 2), scratch,
    )
    result[...] = out.reshape(result.shape).astype(BF16)
    grads[...] = grad


def middle_kernel(
    got_a, got_b, fields, cotangent, taps, inner_result, inner_grads, inner_forward, inner_backward,
    inner_edge_forward, w_mix, w_up, w_down,
    result, grads, grad_mixed, edge_grads, edge_forward, edge_backward, halo,
    forward, backward, *scratch,
):
    rows, width, chans = fields.shape
    step = ceil_to(width, 16)
    pick = lat_picker(got_a, got_b)
    ext = rows + 2

    def taps_of(top):
        both = pick(3 * step, 3 * step + 16, top)
        return [both[:, 0:128], both[:, 128:256]]

    for part, (fields_at, cotangent_at) in enumerate(((0, 0), (width - EDGE, width - LREACH))):
        cells = [
            pick(step * n, step * n + width, top).astype(F32)[fields_at : fields_at + EDGE]
            for top in (True, False)
            for n in range(2)
        ]
        cells += [
            pick(2 * step, 2 * step + width, top).astype(F32)[cotangent_at : cotangent_at + LREACH] for top in (True, False)
        ]
        halo[part] = jnp.concatenate(cells, axis=0).astype(BF16)

    every = jnp.concatenate(taps_of(True) + [taps[r] for r in range(rows)] + taps_of(False), axis=0)
    ends = (0, ext - 1), (1, rows)
    build_bands(every, BLOCK, PITCH, 0, forward, ends[0], backward, ends[1])
    build_bands(every, EDGE, EDGE_PITCH, 0, edge_forward, ends[0], edge_backward, ends[1])

    lines = [pick(step * n, step * n + width, True) for n in range(2)]
    lines += [fields[r] for r in range(rows)]
    lines += [pick(step * n, step * n + width, False) for n in range(2)]
    out, grad = middle_rows(
        lines,
        0,
        [pick(2 * step, 2 * step + width, True), cotangent[0], cotangent[rows - 1], pick(2 * step, 2 * step + width, False)],
        [forward[0], inner_forward[0], inner_forward[rows - 1], forward[1]],
        [edge_forward[0], inner_edge_forward[0], inner_edge_forward[rows - 1], edge_forward[1]],
        [0, 1, ext - 2, ext - 1],
        w_mix, w_up, w_down, (1, 3), scratch,
    )
    lines = [out[0:SPAN].astype(BF16)] + [inner_result[r] for r in range(rows - 2)] + [out[SPAN:].astype(BF16)]
    result[...] = jnp.swapaxes(jnp.stack(lines), 0, 1)
    grads[0 : 2 * SPAN, :] = grad[0 : 2 * SPAN]
    grads[2 * SPAN : (ext - 2) * SPAN, :] = inner_grads[...]
    grads[(ext - 2) * SPAN : ext * SPAN, :] = grad[2 * SPAN :]
    grads[SPAN * ext :, :] = jnp.zeros((LANES - 3 * PITCH, chans), BF16)
    far = width - EDGE - 2 * LREACH
    for i in range(ext):
        mine = grads[SPAN * i : SPAN * (i + 1), :]
        edge_grads[0, EDGE * i : EDGE * (i + 1), :] = mine[0:EDGE]
        edge_grads[1, EDGE * i : EDGE * (i + 1), :] = mine.astype(F32)[far : far + EDGE].astype(BF16)

    bands = [backward[0]] + [inner_backward[r] for r in range(rows - 2)] + [backward[1]]
    for i in range(rows):
        moved = jnp.dot(bands[i], grads[PITCH * i : PITCH * i + LANES, :], preferred_element_type=F32).astype(BF16)
        for k in range(KB):
            grad_mixed[BLOCK * i : BLOCK * (i + 1), chans * k : chans * (k + 1)] = moved[BLOCK * k : BLOCK * (k + 1)]


def edge_kernel(
    middle_result, middle_grads, middle_grad_mixed, edge_grads, inner_edge_forward, inner_edge_backward, end_edge_forward, end_edge_backward,
    halo, send_c, send_d, got_c, got_d, corner_b, corner_a, w_mix, w_up, w_down,
    result, field_grad, source, basis, hidden, upstream, grads, grad_mixed, result_edges, grad_edges, turned_grad, sems,
):
    width, rows, chans = result.shape
    ext = rows + 2
    copies = []

    def store(here, out, first, size):
        copies.append(pltpu.make_async_copy(here.at[pl.ds(0, size)], out.at[pl.ds(first, size)], sems.at[len(copies)]))
        copies[-1].start()

    store(middle_result, result, LREACH, width - 2 * LREACH)
    left_is_c = is_odd("lon") == 1
    edge_forward = [end_edge_forward[0]] + [inner_edge_forward[r] for r in range(rows)] + [end_edge_forward[1]]
    edge_backward = [end_edge_backward[0]] + [inner_edge_backward[r] for r in range(rows - 2)] + [end_edge_backward[1]]
    pick = lat_picker(corner_a, corner_b)

    def own_cells(at):
        sent_c, sent_d, came_c, came_d = [x[at : at + EDGE, :] for x in (send_c, send_d, got_c, got_d)]
        return (
            jnp.where(left_is_c, came_c, came_d),
            jnp.where(left_is_c, sent_c, sent_d),
            jnp.where(left_is_c, sent_d, sent_c),
            jnp.where(left_is_c, came_d, came_c),
        )

    for i in range(rows + 4):
        if 2 <= i < rows + 2:
            cells = own_cells(EDGE * (i - 2))
        else:
            top = i < 2
            n = i if top else i - rows - 2
            at = EDGE * (i if top else i - rows)
            left, right = [pick(EDGE * m, EDGE * (m + 1), top) for m in (n, n + 2)]
            cells = left, halo[0, at : at + EDGE, :], halo[1, at : at + EDGE, :], right
        at = EDGE_PITCH * i
        source[at : at + EDGE, 0:chans] = cells[0]
        source[at + EDGE : at + 2 * EDGE, 0:chans] = cells[1]
        source[at : at + EDGE, chans:] = cells[2]
        source[at + EDGE : at + 2 * EDGE, chans:] = cells[3]

    for i in range(ext):
        if 0 < i < ext - 1:
            inside = LREACH * ((i - 1) % 2)
            cells = own_cells(EDGE * rows + EDGE * ((i - 1) // 2))
            cells = [x.astype(F32)[inside : inside + LREACH] for x in cells]
        else:
            inside = 0 if i == 0 else LREACH
            near, far = [halo[part, 4 * EDGE : 5 * EDGE, :].astype(F32)[inside : inside + LREACH] for part in range(2)]
            both = pick(4 * EDGE, 5 * EDGE, i == 0).astype(F32)
            cells = both[0:LREACH], near, far, both[LREACH:]
        here = 2 * EDGE * i
        upstream[here : here + EDGE, :] = jnp.concatenate(cells[0:2], axis=0).astype(BF16)
        upstream[here + EDGE : here + 2 * EDGE, :] = jnp.concatenate(cells[2:4], axis=0).astype(BF16)

    def spread(bands, cells, out):
        moved = jnp.dot(jnp.concatenate(bands, axis=0), cells, preferred_element_type=F32).astype(BF16)
        for i in range(len(bands)):
            for part in range(2):
                at = EDGE * (2 * i + part)
                for k in range(KB):
                    here = EDGE * (KB * i + k)
                    out[at : at + EDGE, chans * k : chans * (k + 1)] = moved[
                        here : here + EDGE, chans * part : chans * (part + 1)
                    ]

    spread(edge_forward, source[...], basis)
    stacked = jnp.concatenate([w_mix[:, chans * k : chans * (k + 1)] for k in range(KB)], axis=0)
    spatial = jnp.dot(basis[...], stacked, preferred_element_type=F32)
    for i in range(ext):
        at = EDGE_PITCH * (i + 1)
        cells = source[at : at + EDGE_PITCH, :].astype(F32)[LREACH : LREACH + EDGE]
        for part in range(2):
            here = EDGE * (2 * i + part)
            hidden[here : here + EDGE, :] = (
                cells[:, chans * part : chans * (part + 1)] + spatial[here : here + EDGE]
            ).astype(BF16)
    out, grad = mlp(hidden, upstream, w_up, w_down, 2 * EDGE, 2 * EDGE * (rows + 1))
    for i in range(ext):
        at = EDGE_PITCH * i
        here = 2 * EDGE * i
        grads[at : at + EDGE, 0:chans] = grad[here : here + EDGE]
        grads[at + EDGE : at + 2 * EDGE, 0:chans] = edge_grads[0, EDGE * i : EDGE * (i + 1), :]
        grads[at : at + EDGE, chans:] = edge_grads[1, EDGE * i : EDGE * (i + 1), :]
        grads[at + EDGE : at + 2 * EDGE, chans:] = grad[here + EDGE : here + 2 * EDGE]
    grads[EDGE_PITCH * ext :, :] = jnp.zeros((LANES - EDGE_PITCH * ext, 2 * chans), BF16)
    back = contract_last(middle_grad_mixed[...], w_mix[...])
    lines = []
    for i in range(rows):
        at = PITCH * (i + 1)
        own = middle_grads[at : at + PITCH, :].astype(F32)[LREACH : LREACH + BLOCK]
        lines.append((own + back[BLOCK * i : BLOCK * (i + 1)]).astype(BF16))
    turned_grad[...] = jnp.swapaxes(jnp.stack(lines), 0, 1)
    store(turned_grad, field_grad, EDGE, width - 2 * EDGE)
    spread(edge_backward, grads[...], grad_mixed)
    back = contract_last(grad_mixed[...], w_mix[...])
    for part in range(2):
        inside = 0 if part else LREACH
        lines = [out[at + inside : at + inside + LREACH] for at in (EDGE * (2 * i + part) for i in range(rows))]
        result_edges[part] = jnp.swapaxes(jnp.stack(lines), 0, 1).astype(BF16)
        store(result_edges.at[part], result, part * (width - LREACH), LREACH)

    for part in range(2):
        lines = []
        for i in range(rows):
            at = EDGE_PITCH * (i + 1)
            own = grads[at : at + EDGE_PITCH, chans * part : chans * (part + 1)].astype(F32)[LREACH : LREACH + EDGE]
            here = EDGE * (2 * i + part)
            lines.append(own + back[here : here + EDGE])
        grad_edges[part] = jnp.swapaxes(jnp.stack(lines), 0, 1).astype(BF16)
        store(grad_edges.at[part], field_grad, part * (width - EDGE), EDGE)
    for copy in copies:
        copy.wait()


def on_device(fields, w_mix, filters, reach, w_up, w_down, cotangent):
    rows, width, chans = fields.shape
    step = ceil_to(width, 16)
    ext = rows + 2
    pad = LANES - 3 * PITCH

    def shaped(*shape):
        return jax.ShapeDtypeStruct(shape, BF16)

    turned = shaped(width, rows, chans)
    whole = shaped(rows, width, chans)
    sent = shaped(3 * step + 16, chans)
    edge = shaped((EDGE + LREACH) * rows, chans)
    fields = fields.transpose(1, 0, 2)
    cotangent = cotangent.transpose(1, 0, 2)
    send_c, send_d, taps = call(
        fetch,
        (edge, edge, shaped(rows, 8 * KB, 128)),
        [hbm()] * 4,
        [
            pltpu.VMEM((2, EDGE, rows, chans), BF16),
            pltpu.VMEM((2, LREACH, rows, chans), BF16),
            pltpu.VMEM((KB, 3, rows, TAPS), BF16),
            pltpu.SMEM((rows,), jnp.int32),
            pltpu.VMEM((rows, 8 * KB, 128), F32),
            pltpu.SemaphoreType.DMA((6,)),
        ],
        (1000, 1000000),
        *(
            pltpu.with_memory_space_constraint(x, pltpu.HBM)
            for x in (fields, cotangent, filters.transpose(0, 2, 1, 3), reach)
        ),
    )
    got_c = swap(send_c, "lon", 0)
    got_d = swap(send_d, "lon", 1)
    send_a, send_b, fields, cotangent = call(
        pack_lat, (sent, sent, whole, whole), [vmem()] * 3, [], (2000000000, 5000000), fields, cotangent, taps
    )
    got_a = swap(send_a, "lat", 0)
    got_b = swap_inner_lat(send_b)

    def scratch(lines, out_lines):
        return [
            pltpu.VMEM((PITCH * lines + pad, chans), BF16),
            pltpu.VMEM((LANES, chans), BF16),
            pltpu.VMEM((SPAN * out_lines, KB * chans), BF16),
            pltpu.VMEM((SPAN * out_lines, chans), BF16),
            pltpu.VMEM((SPAN * out_lines, chans), BF16),
        ]

    def bands(count):
        return shaped(count, KB * BLOCK, LANES)

    def edge_bands(count):
        return shaped(count, KB * EDGE, LANES)

    inner_result, inner_grads, inner_forward, inner_backward, inner_edge_forward, inner_edge_backward = call(
        inner_kernel,
        (
            shaped(rows - 2, SPAN, chans),
            shaped(SPAN * (rows - 2), chans),
            bands(rows),
            bands(rows - 2),
            edge_bands(rows),
            edge_bands(rows - 2),
        ),
        [vmem()] * 6 + [pl.BlockSpec(memory_space=pl.ANY)],
        scratch(rows, rows - 2),
        (300000000, 1000000),
        fields, cotangent, taps, w_mix, w_up, w_down, send_a,
    )
    corner = shaped(5 * EDGE, chans)
    corner_a, corner_b = call(
        functools.partial(pack_corners, rows),
        (corner, corner),
        [vmem()] * 2 + [pl.BlockSpec(memory_space=pl.ANY)],
        [],
        (4000000000, 1000000),
        got_d, got_c, inner_result,
    )
    corner_a = swap(corner_a, "lat", 0)
    corner_b = swap_inner_lat(corner_b)
    middle_result, middle_grads, middle_grad_mixed, edge_grads, edge_forward, edge_backward, halo = call(
        middle_kernel,
        (
            shaped(SPAN, rows, chans),
            shaped(SPAN * ext + pad, chans),
            shaped(BLOCK * rows, KB * chans),
            shaped(2, EDGE * ext, chans),
            edge_bands(2),
            edge_bands(2),
            shaped(2, 5 * EDGE, chans),
        ),
        [vmem()] * 13,
        [pltpu.VMEM((2, KB * BLOCK, LANES), BF16), pltpu.VMEM((2, KB * BLOCK, LANES), BF16)] + scratch(rows + 4, 4),
        (2000000000, 5000000),
        got_a, got_b, fields, cotangent, taps, inner_result, inner_grads, inner_forward, inner_backward,
        inner_edge_forward, w_mix, w_up, w_down,
    )
    result, field_grad = call(
        edge_kernel,
        (turned, turned),
        [vmem()] * 18,
        [
            pltpu.VMEM((LANES, 2 * chans), BF16),
            pltpu.VMEM((2 * EDGE * ext, KB * chans), BF16),
            pltpu.VMEM((2 * EDGE * ext, chans), BF16),
            pltpu.VMEM((2 * EDGE * ext, chans), BF16),
            pltpu.VMEM((LANES, 2 * chans), BF16),
            pltpu.VMEM((2 * EDGE * rows, KB * chans), BF16),
            pltpu.VMEM((2, LREACH, rows, chans), BF16),
            pltpu.VMEM((2, EDGE, rows, chans), BF16),
            pltpu.VMEM((BLOCK, rows, chans), BF16),
            pltpu.SemaphoreType.DMA((6,)),
        ],
        (500000000, 3000000),
        middle_result, middle_grads, middle_grad_mixed, edge_grads, inner_edge_forward, inner_edge_backward, edge_forward, edge_backward,
        halo, send_c, send_d, got_c, got_d, corner_b, corner_a, w_mix, w_up, w_down,
        out_specs=(hbm(), hbm()),
    )
    return result.transpose(1, 0, 2), field_grad.transpose(1, 0, 2)


def solution(mesh):
    return jax.shard_map(
        on_device,
        mesh=mesh,
        in_specs=(
            P("lat", "lon", None),
            P(),
            P(None, "lat", None, None),
            P("lat"),
            P(),
            P(),
            P("lat", "lon", None),
        ),
        out_specs=(P("lat", "lon", None), P("lat", "lon", None)),
        check_vma=False,
    )
```

```python
import functools

import jax
import jax.numpy as jnp
from jax import lax
from jax.experimental import pallas as pl
from jax.experimental.pallas import tpu as pltpu
from jax.sharding import PartitionSpec as P

KB = 4
LREACH = 8
TAPS = 2 * LREACH + 1
BLOCK = 64
PITCH = BLOCK + 2 * LREACH
EDGE = 2 * LREACH
EDGE_PITCH = 2 * EDGE
LANES = 256
TAP_LANES = 128
F32 = jnp.float32
BF16 = jnp.bfloat16
VMEM_BYTES = 48 * 1024 * 1024


def ceil_to(size, unit):
    return -(-size // unit) * unit


def vmem():
    return pl.BlockSpec(memory_space=pltpu.VMEM)


def hbm():
    return pl.BlockSpec(memory_space=pltpu.HBM)


def is_odd(axis):
    return lax.rem(lax.axis_index(axis), 2)


def call(kernel, outs, in_specs, scratch, cost, *args, out_specs=None):
    return pl.pallas_call(
        kernel,
        out_shape=outs,
        in_specs=in_specs,
        out_specs=out_specs or jax.tree.map(lambda _: vmem(), outs),
        scratch_shapes=scratch,
        compiler_params=pltpu.CompilerParams(vmem_limit_bytes=VMEM_BYTES),
        cost_estimate=pl.CostEstimate(flops=cost[0], bytes_accessed=cost[1], transcendentals=0),
    )(*args)


def swap(cells, axis, shift):
    count = lax.axis_size(axis)
    pairs = []
    for first in range(shift, count, 2):
        second = (first + 1) % count
        pairs += [(first, second), (second, first)]
    return lax.ppermute(cells, axis, pairs)


def swap_inner_lat(cells, idle):
    count, around = lax.axis_size("lat"), lax.axis_size("lon")
    pairs = []
    for j in range(around):
        partner = j ^ 1 if idle else (j + around // 2) % around
        pairs += [(i * around + j, i * around + partner) for i in (0, count - 1)]
        for i in range(1, count - 1, 2):
            pairs += [(i * around + j, (i + 1) * around + j), ((i + 1) * around + j, i * around + j)]
    return lax.ppermute(cells, ("lat", "lon"), pairs)


def lat_picker(got_a, got_b):
    top_is_a = is_odd("lat") == 1
    index = lax.axis_index("lat")
    inner = (index > 0) & (index < lax.axis_size("lat") - 1)

    def pick(first, last, top):
        a, b = got_a[first:last, :], got_b[first:last, :]
        return jnp.where(top_is_a == top, a, jnp.where(inner, b, jnp.zeros_like(b)))

    return pick


def fetch(fields, cotangent, filters, reach, send_c, send_d, taps, fields_here, cotangent_here, filters_here, reach_here, raw, sems):
    width, rows, chans = fields.shape
    moves = [(filters, filters_here), (reach, reach_here)]
    for part in range(2):
        moves.append((fields.at[pl.ds(part * (width - EDGE), EDGE)], fields_here.at[part]))
        moves.append((cotangent.at[pl.ds(part * (width - LREACH), LREACH)], cotangent_here.at[part]))
    copies = [pltpu.make_async_copy(src, dst, sems.at[n]) for n, (src, dst) in enumerate(moves)]
    for copy in copies:
        copy.start()
    raw[...] = jnp.zeros(raw.shape, F32)
    offset = jnp.abs(lax.broadcasted_iota(jnp.int32, (8 * KB, 128), 1) - LREACH)
    copies[0].wait()
    copies[1].wait()
    for k in range(KB):
        for a in range(3):
            line = filters_here[k, a].astype(F32)
            for r in range(rows):
                raw[r, 8 * k + a : 8 * k + a + 1, 0:TAPS] = line[r : r + 1]
    for r in range(rows):
        taps[r] = jnp.where(offset <= reach_here[r], raw[r], 0.0).astype(BF16)
    for copy in copies[2:]:
        copy.wait()
    sides = []
    for part in range(2):
        cells = jnp.swapaxes(fields_here[part], 0, 1).reshape(EDGE * rows, chans)
        grads = jnp.swapaxes(cotangent_here[part].astype(F32), 0, 1).reshape(LREACH * rows, chans).astype(BF16)
        sides.append((cells, grads))
    fill_lon(send_c, send_d, *sides)


def fill_lat(send, low, fields, cotangent, taps):
    rows, width, chans = fields.shape
    step = ceil_to(width, 16)
    send[0:width, :] = fields[low * (rows - 2)]
    send[step : step + width, :] = fields[low * (rows - 2) + 1]
    send[2 * step : 2 * step + width, :] = cotangent[low * (rows - 1)]
    own = taps[low * (rows - 1)]
    send[3 * step : 3 * step + 16, 0:128] = own[0:16]
    send[3 * step : 3 * step + 16, 128:256] = own[16:32]


def fill_lon(send_c, send_d, near, far):
    odd = is_odd("lon") == 1
    at = 0
    for first, last in zip(near, far, strict=True):
        size = first.shape[0]
        send_c[at : at + size, :] = jnp.where(odd, first, last)
        send_d[at : at + size, :] = jnp.where(odd, last, first)
        at += size


def pack_lat(fields, cotangent, taps, send_a, send_b, fields_rows, cotangent_rows):
    fields_rows[...] = jnp.swapaxes(fields[...], 0, 1)
    cotangent_rows[...] = jnp.swapaxes(cotangent[...], 0, 1)
    odd = is_odd("lat")
    fill_lat(send_a, 1 - odd, fields_rows, cotangent_rows, taps)
    fill_lat(send_b, odd, fields_rows, cotangent_rows, taps)


def pack_corners(rows, got_d, got_c, inner, send_a, send_b):
    odd = is_odd("lat")
    left_is_c = is_odd("lon") == 1
    for send, low in ((send_a, 1 - odd), (send_b, odd)):
        at = pl.multiple_of(low * (rows - 2) * EDGE, EDGE)
        c, d = got_c[pl.ds(at, 2 * EDGE), :], got_d[pl.ds(at, 2 * EDGE), :]
        send[0 : 2 * EDGE, :] = jnp.where(left_is_c, c, d)
        send[2 * EDGE : 4 * EDGE, :] = jnp.where(left_is_c, d, c)
        first, last = EDGE * rows, (EDGE + LREACH) * rows
        c, d = [
            jnp.where(low == 1, x[last - EDGE : last, :].astype(F32)[LREACH:], x[first : first + EDGE, :].astype(F32)[0:LREACH])
            for x in (got_c, got_d)
        ]
        both = [jnp.where(left_is_c, c, d), jnp.where(left_is_c, d, c)]
        send[4 * EDGE : 5 * EDGE, :] = jnp.concatenate(both, axis=0).astype(BF16)


def lay_taps(every, pitch, lanes):
    groups = every.shape[0] // 8

    def places(shape, dim):
        col = lax.broadcasted_iota(jnp.int32, shape, dim)
        turned = col >= lanes
        inner = jnp.where(turned, col - lanes, col)
        part = jnp.where(inner >= pitch, 1, 0) + jnp.where(inner >= 2 * pitch, 1, 0)
        return turned, inner - pitch * part, part

    turned, place, _ = places((128, 2 * lanes), 1)
    tap = lax.broadcasted_iota(jnp.int32, (128, 2 * lanes), 0)
    wanted = jnp.where(turned, 2 * LREACH - place, place)
    table = jnp.where((tap == wanted) & (tap < TAPS), 1.0, 0.0).astype(BF16)
    spread = jnp.dot(every, table, preferred_element_type=F32).reshape(groups, 8, 2 * lanes)
    turned, _, part = places((groups, 8, 2 * lanes), 2)
    lat_tap = lax.broadcasted_iota(jnp.int32, (groups, 8, 2 * lanes), 1)
    chosen = jnp.where(turned, 2 - part, part) == lat_tap
    return jnp.sum(jnp.where(chosen, spread, 0.0), axis=1)


def slant(line, size, shift):
    lanes = line.shape[1]
    return pltpu.roll(jnp.broadcast_to(line, (size, lanes)), shift, 1, stride=1, stride_axis=0).astype(BF16)


def build_bands(every, size, pitch, first, forward, forward_rows, backward, backward_rows):
    edge = size == EDGE
    lanes = TAP_LANES if edge else LANES
    lines = lay_taps(every, pitch, lanes)
    lane = lax.broadcasted_iota(jnp.int32, (1, lanes), 1)

    def lean(line, row):
        if edge:
            line = jnp.concatenate([line, jnp.zeros((1, LANES - lanes), F32)], axis=1)
        return slant(line, size, pitch * row if edge else 0)

    for place, i in enumerate(forward_rows):
        for k in range(KB):
            at = KB * i + k
            forward[place, size * k : size * (k + 1), :] = lean(lines[at : at + 1, 0:lanes], i + first)
    for place, i in enumerate(backward_rows):
        for k in range(KB):
            near = [lines[KB * (i + t - 1) + k : KB * (i + t - 1) + k + 1, lanes:] for t in range(3)]
            line = jnp.where(lane < pitch, near[0], jnp.where(lane < 2 * pitch, near[1], near[2]))
            backward[place, size * k : size * (k + 1), :] = lean(line, i + first - 1)


def gelu_parts(pre):
    size = jnp.abs(pre)
    bell = jnp.exp(-0.5 * pre * pre)
    t = 1.0 / (1.0 + 0.23164188836 * size)
    poly = t * (0.127414796 + t * (-0.142248368 + t * (0.7107068705 + t * (-0.7265760135 + t * 0.5307027145))))
    tail = poly * bell
    cdf = jnp.where(pre >= 0.0, 1.0 - tail, tail)
    return pre * cdf, cdf + pre * bell * 0.3989422804014327


def contract_last(left, right):
    return lax.dot_general(left, right, (((1,), (1,)), ((), ())), preferred_element_type=F32)


def mlp(hidden, upstream, w_up, w_down, first, last):
    arriving = contract_last(upstream[...], w_down[...])
    pre = jnp.dot(hidden[...], w_up[...], preferred_element_type=F32)
    active, slope = gelu_parts(pre)
    grad = (upstream[...].astype(F32) + contract_last((arriving * slope).astype(BF16), w_up[...])).astype(BF16)
    out = hidden[first:last, :].astype(F32) + jnp.dot(
        active[first:last].astype(BF16), w_down[...], preferred_element_type=F32
    )
    return out, grad


SPAN = BLOCK + EDGE


def middle_rows(lines, start, cotangents, bands, edge_bands, firsts, w_mix, w_up, w_down, out_rows, scratch):
    wide, narrow, basis, hidden, upstream = scratch
    chans = w_up.shape[0]
    width = lines[0].shape[0]
    fill = PITCH + EDGE - width
    if start:
        narrow[...] = jnp.zeros(narrow.shape, BF16)
    for f, line in enumerate(lines):
        wide[PITCH * f : PITCH * (f + 1), :] = line[0:PITCH]
        tail = jnp.concatenate([line[BLOCK:].astype(F32), jnp.zeros((fill, chans), F32)], axis=0)
        narrow[EDGE_PITCH * (start + f) : EDGE_PITCH * (start + f + 1), :] = tail.astype(BF16)
    wide[PITCH * len(lines) :, :] = jnp.zeros((LANES - 3 * PITCH, chans), BF16)
    others = jnp.dot(jnp.concatenate(edge_bands, axis=0), narrow[...], preferred_element_type=F32).astype(BF16)
    for n, f in enumerate(firsts):
        at = SPAN * n
        moved = jnp.dot(bands[n], wide[PITCH * f : PITCH * f + LANES, :], preferred_element_type=F32).astype(BF16)
        other = others[KB * EDGE * n : KB * EDGE * (n + 1)]
        for k in range(KB):
            basis[at : at + BLOCK, chans * k : chans * (k + 1)] = moved[BLOCK * k : BLOCK * (k + 1)]
            basis[at + BLOCK : at + SPAN, chans * k : chans * (k + 1)] = other[EDGE * k : EDGE * (k + 1)]
    stacked = jnp.concatenate([w_mix[:, chans * k : chans * (k + 1)] for k in range(KB)], axis=0)
    spatial = jnp.dot(basis[...], stacked, preferred_element_type=F32)
    for n, f in enumerate(firsts):
        at = PITCH * (f + 1)
        first = wide[at : at + PITCH, :].astype(F32)[LREACH : LREACH + BLOCK]
        at = EDGE_PITCH * (start + f + 1)
        second = narrow[at : at + EDGE_PITCH, :].astype(F32)[LREACH : LREACH + EDGE]
        here = SPAN * n
        mine = jnp.concatenate([first, second], axis=0) + spatial[here : here + SPAN]
        hidden[here : here + SPAN, :] = mine.astype(BF16)
        upstream[here : here + SPAN, :] = cotangents[n].astype(F32)[LREACH : LREACH + SPAN].astype(BF16)
    return mlp(hidden, upstream, w_up, w_down, SPAN * out_rows[0], SPAN * out_rows[1])


def inner_kernel(
    fields, cotangent, taps, w_mix, w_up, w_down, sent,
    result, grads, forward, backward, edge_forward, edge_backward, *scratch,
):
    rows = fields.shape[0]
    every = jnp.concatenate([taps[r] for r in range(rows)], axis=0)
    own, inner = range(rows), range(1, rows - 1)
    build_bands(every, BLOCK, PITCH, 1, forward, own, backward, inner)
    build_bands(every, EDGE, EDGE_PITCH, 1, edge_forward, own, edge_backward, inner)
    out, grad = middle_rows(
        [fields[r] for r in own],
        2,
        [cotangent[r] for r in inner],
        [forward[r] for r in inner],
        [edge_forward[r] for r in inner],
        [r - 1 for r in inner],
        w_mix, w_up, w_down, (0, rows - 2), scratch,
    )
    result[...] = out.reshape(result.shape).astype(BF16)
    grads[...] = grad


def middle_kernel(
    got_a, got_b, fields, cotangent, taps, inner_result, inner_grads, inner_forward, inner_backward,
    inner_edge_forward, w_mix, w_up, w_down,
    result, grads, grad_mixed, edge_grads, edge_forward, edge_backward, halo,
    forward, backward, *scratch,
):
    rows, width, chans = fields.shape
    step = ceil_to(width, 16)
    pick = lat_picker(got_a, got_b)
    ext = rows + 2

    def taps_of(top):
        both = pick(3 * step, 3 * step + 16, top)
        return [both[:, 0:128], both[:, 128:256]]

    for part, (fields_at, cotangent_at) in enumerate(((0, 0), (width - EDGE, width - LREACH))):
        cells = [
            pick(step * n, step * n + width, top).astype(F32)[fields_at : fields_at + EDGE]
            for top in (True, False)
            for n in range(2)
        ]
        cells += [
            pick(2 * step, 2 * step + width, top).astype(F32)[cotangent_at : cotangent_at + LREACH] for top in (True, False)
        ]
        halo[part] = jnp.concatenate(cells, axis=0).astype(BF16)

    every = jnp.concatenate(taps_of(True) + [taps[r] for r in range(rows)] + taps_of(False), axis=0)
    ends = (0, ext - 1), (1, rows)
    build_bands(every, BLOCK, PITCH, 0, forward, ends[0], backward, ends[1])
    build_bands(every, EDGE, EDGE_PITCH, 0, edge_forward, ends[0], edge_backward, ends[1])

    lines = [pick(step * n, step * n + width, True) for n in range(2)]
    lines += [fields[r] for r in range(rows)]
    lines += [pick(step * n, step * n + width, False) for n in range(2)]
    out, grad = middle_rows(
        lines,
        0,
        [pick(2 * step, 2 * step + width, True), cotangent[0], cotangent[rows - 1], pick(2 * step, 2 * step + width, False)],
        [forward[0], inner_forward[0], inner_forward[rows - 1], forward[1]],
        [edge_forward[0], inner_edge_forward[0], inner_edge_forward[rows - 1], edge_forward[1]],
        [0, 1, ext - 2, ext - 1],
        w_mix, w_up, w_down, (1, 3), scratch,
    )
    lines = [out[0:SPAN].astype(BF16)] + [inner_result[r] for r in range(rows - 2)] + [out[SPAN:].astype(BF16)]
    result[...] = jnp.swapaxes(jnp.stack(lines), 0, 1)
    grads[0 : 2 * SPAN, :] = grad[0 : 2 * SPAN]
    grads[2 * SPAN : (ext - 2) * SPAN, :] = inner_grads[...]
    grads[(ext - 2) * SPAN : ext * SPAN, :] = grad[2 * SPAN :]
    grads[SPAN * ext :, :] = jnp.zeros((LANES - 3 * PITCH, chans), BF16)
    far = width - EDGE - 2 * LREACH
    for i in range(ext):
        mine = grads[SPAN * i : SPAN * (i + 1), :]
        edge_grads[0, EDGE * i : EDGE * (i + 1), :] = mine[0:EDGE]
        edge_grads[1, EDGE * i : EDGE * (i + 1), :] = mine.astype(F32)[far : far + EDGE].astype(BF16)

    bands = [backward[0]] + [inner_backward[r] for r in range(rows - 2)] + [backward[1]]
    for i in range(rows):
        moved = jnp.dot(bands[i], grads[PITCH * i : PITCH * i + LANES, :], preferred_element_type=F32).astype(BF16)
        for k in range(KB):
            grad_mixed[BLOCK * i : BLOCK * (i + 1), chans * k : chans * (k + 1)] = moved[BLOCK * k : BLOCK * (k + 1)]


def edge_kernel(
    middle_result, middle_grads, middle_grad_mixed, edge_grads, inner_edge_forward, inner_edge_backward, end_edge_forward, end_edge_backward,
    halo, send_c, send_d, got_c, got_d, corner_b, corner_a, w_mix, w_up, w_down,
    result, field_grad, source, basis, hidden, upstream, grads, grad_mixed, result_edges, grad_edges, turned_grad, sems,
):
    width, rows, chans = result.shape
    ext = rows + 2
    copies = []

    def store(here, out, first, size):
        copies.append(pltpu.make_async_copy(here.at[pl.ds(0, size)], out.at[pl.ds(first, size)], sems.at[len(copies)]))
        copies[-1].start()

    store(middle_result, result, LREACH, width - 2 * LREACH)
    left_is_c = is_odd("lon") == 1
    edge_forward = [end_edge_forward[0]] + [inner_edge_forward[r] for r in range(rows)] + [end_edge_forward[1]]
    edge_backward = [end_edge_backward[0]] + [inner_edge_backward[r] for r in range(rows - 2)] + [end_edge_backward[1]]
    pick = lat_picker(corner_a, corner_b)

    def own_cells(at):
        sent_c, sent_d, came_c, came_d = [x[at : at + EDGE, :] for x in (send_c, send_d, got_c, got_d)]
        return (
            jnp.where(left_is_c, came_c, came_d),
            jnp.where(left_is_c, sent_c, sent_d),
            jnp.where(left_is_c, sent_d, sent_c),
            jnp.where(left_is_c, came_d, came_c),
        )

    for i in range(rows + 4):
        if 2 <= i < rows + 2:
            cells = own_cells(EDGE * (i - 2))
        else:
            top = i < 2
            n = i if top else i - rows - 2
            at = EDGE * (i if top else i - rows)
            left, right = [pick(EDGE * m, EDGE * (m + 1), top) for m in (n, n + 2)]
            cells = left, halo[0, at : at + EDGE, :], halo[1, at : at + EDGE, :], right
        at = EDGE_PITCH * i
        source[at : at + EDGE, 0:chans] = cells[0]
        source[at + EDGE : at + 2 * EDGE, 0:chans] = cells[1]
        source[at : at + EDGE, chans:] = cells[2]
        source[at + EDGE : at + 2 * EDGE, chans:] = cells[3]

    for i in range(ext):
        if 0 < i < ext - 1:
            inside = LREACH * ((i - 1) % 2)
            cells = own_cells(EDGE * rows + EDGE * ((i - 1) // 2))
            cells = [x.astype(F32)[inside : inside + LREACH] for x in cells]
        else:
            inside = 0 if i == 0 else LREACH
            near, far = [halo[part, 4 * EDGE : 5 * EDGE, :].astype(F32)[inside : inside + LREACH] for part in range(2)]
            both = pick(4 * EDGE, 5 * EDGE, i == 0).astype(F32)
            cells = both[0:LREACH], near, far, both[LREACH:]
        here = 2 * EDGE * i
        upstream[here : here + EDGE, :] = jnp.concatenate(cells[0:2], axis=0).astype(BF16)
        upstream[here + EDGE : here + 2 * EDGE, :] = jnp.concatenate(cells[2:4], axis=0).astype(BF16)

    def spread(bands, cells, out):
        moved = jnp.dot(jnp.concatenate(bands, axis=0), cells, preferred_element_type=F32).astype(BF16)
        for i in range(len(bands)):
            for part in range(2):
                at = EDGE * (2 * i + part)
                for k in range(KB):
                    here = EDGE * (KB * i + k)
                    out[at : at + EDGE, chans * k : chans * (k + 1)] = moved[
                        here : here + EDGE, chans * part : chans * (part + 1)
                    ]

    spread(edge_forward, source[...], basis)
    stacked = jnp.concatenate([w_mix[:, chans * k : chans * (k + 1)] for k in range(KB)], axis=0)
    spatial = jnp.dot(basis[...], stacked, preferred_element_type=F32)
    for i in range(ext):
        at = EDGE_PITCH * (i + 1)
        cells = source[at : at + EDGE_PITCH, :].astype(F32)[LREACH : LREACH + EDGE]
        for part in range(2):
            here = EDGE * (2 * i + part)
            hidden[here : here + EDGE, :] = (
                cells[:, chans * part : chans * (part + 1)] + spatial[here : here + EDGE]
            ).astype(BF16)
    out, grad = mlp(hidden, upstream, w_up, w_down, 2 * EDGE, 2 * EDGE * (rows + 1))
    for i in range(ext):
        at = EDGE_PITCH * i
        here = 2 * EDGE * i
        grads[at : at + EDGE, 0:chans] = grad[here : here + EDGE]
        grads[at + EDGE : at + 2 * EDGE, 0:chans] = edge_grads[0, EDGE * i : EDGE * (i + 1), :]
        grads[at : at + EDGE, chans:] = edge_grads[1, EDGE * i : EDGE * (i + 1), :]
        grads[at + EDGE : at + 2 * EDGE, chans:] = grad[here + EDGE : here + 2 * EDGE]
    grads[EDGE_PITCH * ext :, :] = jnp.zeros((LANES - EDGE_PITCH * ext, 2 * chans), BF16)
    back = contract_last(middle_grad_mixed[...], w_mix[...])
    lines = []
    for i in range(rows):
        at = PITCH * (i + 1)
        own = middle_grads[at : at + PITCH, :].astype(F32)[LREACH : LREACH + BLOCK]
        lines.append((own + back[BLOCK * i : BLOCK * (i + 1)]).astype(BF16))
    turned_grad[...] = jnp.swapaxes(jnp.stack(lines), 0, 1)
    store(turned_grad, field_grad, EDGE, width - 2 * EDGE)
    spread(edge_backward, grads[...], grad_mixed)
    back = contract_last(grad_mixed[...], w_mix[...])
    for part in range(2):
        inside = 0 if part else LREACH
        lines = [out[at + inside : at + inside + LREACH] for at in (EDGE * (2 * i + part) for i in range(rows))]
        result_edges[part] = jnp.swapaxes(jnp.stack(lines).astype(BF16), 0, 1)
        store(result_edges.at[part], result, part * (width - LREACH), LREACH)

    for part in range(2):
        lines = []
        for i in range(rows):
            at = EDGE_PITCH * (i + 1)
            own = grads[at : at + EDGE_PITCH, chans * part : chans * (part + 1)].astype(F32)[LREACH : LREACH + EDGE]
            here = EDGE * (2 * i + part)
            lines.append(own + back[here : here + EDGE])
        grad_edges[part] = jnp.swapaxes(jnp.stack(lines).astype(BF16), 0, 1)
        store(grad_edges.at[part], field_grad, part * (width - EDGE), EDGE)
    for copy in copies:
        copy.wait()


def on_device(fields, w_mix, filters, reach, w_up, w_down, cotangent):
    rows, width, chans = fields.shape
    step = ceil_to(width, 16)
    ext = rows + 2
    pad = LANES - 3 * PITCH

    def shaped(*shape):
        return jax.ShapeDtypeStruct(shape, BF16)

    turned = shaped(width, rows, chans)
    whole = shaped(rows, width, chans)
    sent = shaped(3 * step + 16, chans)
    edge = shaped((EDGE + LREACH) * rows, chans)
    fields = fields.transpose(1, 0, 2)
    cotangent = cotangent.transpose(1, 0, 2)
    send_c, send_d, taps = call(
        fetch,
        (edge, edge, shaped(rows, 8 * KB, 128)),
        [hbm()] * 4,
        [
            pltpu.VMEM((2, EDGE, rows, chans), BF16),
            pltpu.VMEM((2, LREACH, rows, chans), BF16),
            pltpu.VMEM((KB, 3, rows, TAPS), BF16),
            pltpu.SMEM((rows,), jnp.int32),
            pltpu.VMEM((rows, 8 * KB, 128), F32),
            pltpu.SemaphoreType.DMA((6,)),
        ],
        (1000, 1000000),
        *(
            pltpu.with_memory_space_constraint(x, pltpu.HBM)
            for x in (fields, cotangent, filters.transpose(0, 2, 1, 3), reach)
        ),
    )
    got_c = swap(send_c, "lon", 0)
    got_d = swap(send_d, "lon", 1)
    send_a, send_b, fields, cotangent = call(
        pack_lat, (sent, sent, whole, whole), [vmem()] * 3, [], (2000000000, 5000000), fields, cotangent, taps
    )
    got_a = swap(send_a, "lat", 0)
    got_b = swap_inner_lat(send_b, 0)

    def scratch(lines, out_lines):
        return [
            pltpu.VMEM((PITCH * lines + pad, chans), BF16),
            pltpu.VMEM((LANES, chans), BF16),
            pltpu.VMEM((SPAN * out_lines, KB * chans), BF16),
            pltpu.VMEM((SPAN * out_lines, chans), BF16),
            pltpu.VMEM((SPAN * out_lines, chans), BF16),
        ]

    def bands(count):
        return shaped(count, KB * BLOCK, LANES)

    def edge_bands(count):
        return shaped(count, KB * EDGE, LANES)

    inner_result, inner_grads, inner_forward, inner_backward, inner_edge_forward, inner_edge_backward = call(
        inner_kernel,
        (
            shaped(rows - 2, SPAN, chans),
            shaped(SPAN * (rows - 2), chans),
            bands(rows),
            bands(rows - 2),
            edge_bands(rows),
            edge_bands(rows - 2),
        ),
        [vmem()] * 6 + [pl.BlockSpec(memory_space=pl.ANY)],
        scratch(rows, rows - 2),
        (300000000, 1000000),
        fields, cotangent, taps, w_mix, w_up, w_down, send_a,
    )
    corner = shaped(5 * EDGE, chans)
    corner_a, corner_b = call(
        functools.partial(pack_corners, rows),
        (corner, corner),
        [vmem()] * 2 + [pl.BlockSpec(memory_space=pl.ANY)],
        [],
        (4000000000, 1000000),
        got_d, got_c, inner_result,
    )
    corner_a = swap(corner_a, "lat", 0)
    corner_b = swap_inner_lat(corner_b, 1)
    middle_result, middle_grads, middle_grad_mixed, edge_grads, edge_forward, edge_backward, halo = call(
        middle_kernel,
        (
            shaped(SPAN, rows, chans),
            shaped(SPAN * ext + pad, chans),
            shaped(BLOCK * rows, KB * chans),
            shaped(2, EDGE * ext, chans),
            edge_bands(2),
            edge_bands(2),
            shaped(2, 5 * EDGE, chans),
        ),
        [vmem()] * 13,
        [pltpu.VMEM((2, KB * BLOCK, LANES), BF16), pltpu.VMEM((2, KB * BLOCK, LANES), BF16)] + scratch(rows + 4, 4),
        (2000000000, 5000000),
        got_a, got_b, fields, cotangent, taps, inner_result, inner_grads, inner_forward, inner_backward,
        inner_edge_forward, w_mix, w_up, w_down,
    )
    result, field_grad = call(
        edge_kernel,
        (turned, turned),
        [vmem()] * 18,
        [
            pltpu.VMEM((LANES, 2 * chans), BF16),
            pltpu.VMEM((2 * EDGE * ext, KB * chans), BF16),
            pltpu.VMEM((2 * EDGE * ext, chans), BF16),
            pltpu.VMEM((2 * EDGE * ext, chans), BF16),
            pltpu.VMEM((LANES, 2 * chans), BF16),
            pltpu.VMEM((2 * EDGE * rows, KB * chans), BF16),
            pltpu.VMEM((2, LREACH, rows, chans), BF16),
            pltpu.VMEM((2, EDGE, rows, chans), BF16),
            pltpu.VMEM((BLOCK, rows, chans), BF16),
            pltpu.SemaphoreType.DMA((6,)),
        ],
        (500000000, 3000000),
        middle_result, middle_grads, middle_grad_mixed, edge_grads, inner_edge_forward, inner_edge_backward, edge_forward, edge_backward,
        halo, send_c, send_d, got_c, got_d, corner_b, corner_a, w_mix, w_up, w_down,
        out_specs=(hbm(), hbm()),
    )
    return result.transpose(1, 0, 2), field_grad.transpose(1, 0, 2)


def solution(mesh):
    return jax.shard_map(
        on_device,
        mesh=mesh,
        in_specs=(
            P("lat", "lon", None),
            P(),
            P(None, "lat", None, None),
            P("lat"),
            P(),
            P(),
            P("lat", "lon", None),
        ),
        out_specs=(P("lat", "lon", None), P("lat", "lon", None)),
        check_vma=False,
    )
```
